128 devices in a mesh: gx: 16 (over z, y), gy: 8 (over x, core).
Axes of the slice: x: 4, y: 4, z: 4, core: 2. Of those that a mesh axis runs over, the one named last changes fastest.
Arguments:
- tokens_one: bfloat16 [32768, 768], P(('gx', 'gy')), may hold values from -6 to 6
- gates_one: float32 [32768], P(('gx', 'gy')), may hold values from 0.2 to 1
- routes_one: int32 [32768, 1], P(('gx', 'gy')), may hold values from 0 to 127; in each aligned block of 256 rows (0 to 255, 256 to 511, ...) at most 4 rows name the same one
- old_place: int32 [128], replicated, may hold values from 0 to 127, each once
- move_slots: int32 [25, 2], replicated, may hold values from 0 to 127, as said below
- tokens_two: bfloat16 [32768, 768], P(('gx', 'gy')), may hold values from -6 to 6
- gates_two: float32 [32768], P(('gx', 'gy')), may hold values from 0.2 to 1
- routes_two: int32 [32768, 1], P(('gx', 'gy')), may hold values from 0 to 127; in each aligned block of 256 rows (0 to 255, 256 to 511, ...) at most 4 rows name the same one
- expert_in: bfloat16 [128, 3072, 768], P(('gx', 'gy')), may hold values from -0.21875 to 0.21875
- expert_out: bfloat16 [128, 3072, 768], P(('gx', 'gy')), may hold values from -0.109375 to 0.109375
Outputs:
- mixed_one: bfloat16 [32768, 768], P(('gx', 'gy'))
- mixed_two: bfloat16 [32768, 768], P(('gx', 'gy'))
- expert_in_new: bfloat16 [128, 3072, 768], P(('gx', 'gy'))
- expert_out_new: bfloat16 [128, 3072, 768], P(('gx', 'gy'))
The draws below stay inside these ranges and needn't reach their ends.
Inputs may be any that keep to these rules, and one draw needn't show every extreme that they name: `routes_one`: among the tokens of one device no expert is named by more than 4 tokens. `routes_two`: among the tokens of one device no slot is named by more than 4 tokens. `old_place`: each expert has one slot. `move_slots`: source slots lie on 25 distinct devices; the destination slots are the same set of slots, and no move stays on its device, so each device sends at most one expert and receives at most one.
All inputs are finite; a program needn't handle non-finite values.
Results may differ from the reference program's by a relative error of at most 0.0058.
Values may be sent and summed in bfloat16 or wider, within the bound.
A program may use at most 128 MiB of HBM per device.

```python
import math
import jax
import jax.numpy as jnp
import numpy as np
from jax import lax

D = 768
FF = 3072
EXP_DEV = 1
TOK_DEV = 256
EXPERTS = 128
MOST = 4
MOVES = 25
TOKENS = 32768
N_GX = 16
N_GY = 8


def draw_move_slots(key, part):
    key = jax.random.fold_in(key, 7)
    first, second, third = jax.random.split(key, 3)
    host_count = EXPERTS // EXP_DEV
    middle = jax.random.permutation(first, host_count - 2)[:MOVES - 2] + 1
    hosts = jnp.concatenate([jnp.array([0, host_count - 1], jnp.int32), middle.astype(jnp.int32)])
    within = jax.random.randint(second, (MOVES,), 0, EXP_DEV).astype(jnp.int32)
    within = within.at[0].set(0).at[1].set(EXP_DEV - 1)
    sources = (hosts * EXP_DEV + within).astype(jnp.int32)
    order = jax.random.permutation(third, MOVES)
    sources = sources[order].astype(jnp.int32)
    return jnp.stack([sources, jnp.roll(sources, -1)], axis=1).astype(jnp.int32)


def block_levels(own_key, extent, cuts, smallest, top_value):
    level, own = 1.0, jax.random.fold_in(own_key, 6)
    for dim, shards_of in cuts:
        heights = jnp.exp(jax.random.uniform(jax.random.fold_in(own, dim), (shards_of,), jnp.float32, smallest / len(cuts), top_value / len(cuts)))
        level = level * jnp.repeat(heights, extent[dim] // shards_of).reshape([-1 if axis == dim else 1 for axis in range(len(extent))])
    return level


def deal_out(rng, own, number, rows, count, top, reach, lean):
    sequence = jax.random.permutation(rng, count)
    packed, ordinary = portions_of(count, rows * top, reach, lean, True), portions_of(count, rows * top, reach, lean, False)
    places = jnp.arange(count)

    def named(tallies, offset_by):
        used = int((tallies > 0).sum())
        fixed = max(1, used // 4)
        moved = fixed + (places - fixed + offset_by * (used - fixed)) % max(1, count - fixed)
        return jnp.zeros((count,), jnp.int32).at[sequence[jnp.where(places < fixed, places, moved)]].set(jnp.asarray(tallies, jnp.int32))

    tallies = jnp.where(number % 4 == 0, named(packed, number // 4), named(ordinary, number - number // 4 - 1))
    mixed = jax.random.permutation(jax.random.fold_in(own, 3), count)
    giver, receiver = mixed[0:count // 2 * 2:2], mixed[1:count // 2 * 2:2]
    margin = jnp.minimum(tallies[giver] - 1, reach - tallies[receiver]) // 2
    margin = jnp.where((giver == sequence[0]) | (receiver == sequence[0]) | (tallies[receiver] == 0), 0, jnp.maximum(margin, 0))
    moved = jax.random.randint(jax.random.fold_in(own, 4), (count // 2,), 0, 1 << 20) % (margin + 1)
    tallies = tallies.at[giver].add(-moved).at[receiver].add(moved)
    items = jnp.searchsorted(jnp.cumsum(tallies), jnp.arange(rows * top), side="right").astype(jnp.int32)
    grid = items.reshape(top, rows).T
    grid = grid[jax.random.permutation(jax.random.fold_in(own, 1), rows)]
    offset_by = jax.random.randint(jax.random.fold_in(own, 2), (rows, 1), 0, top)
    return jnp.take_along_axis(grid, (jnp.arange(top)[None, :] + offset_by) % top, axis=1)


def portions_of(amount, total, bound, lean, full):
    loads = [(1 << 20) // math.isqrt(standing ** lean) + 1 for standing in range(1, amount + 1)]
    largest = bound if full else min(bound, max(-(-total // amount), total * loads[0] // sum(loads)))
    least = 1 if total - largest >= amount - 1 else 0
    given, surplus = [largest] + [least] * (amount - 1), total - largest - least * (amount - 1)
    while surplus > 0:
        movable = [i for i in range(1, amount) if given[i] < largest] or [i for i in range(1, amount) if given[i] < bound]
        pool, left = sum([loads[i] for i in movable]), surplus
        for i in movable:
            more = min(bound - given[i], max(1, left * loads[i] // pool), surplus)
            given[i] = given[i] + more
            surplus = surplus - more
    return np.array(given)


def bell_draw(key, extent, deviation, reach, pieces=(), held_as=jnp.bfloat16):
    values = deviation * jax.random.normal(key, extent, jnp.float32)
    if pieces:
        values = values * block_levels(key, extent, pieces, -0.22, 0.18)
    return jnp.clip(values, -reach, reach).astype(held_as)


def setup_inputs(seed: int = 0) -> dict:
    splits = jax.random.split(jax.random.key(seed), 11)
    tokens_one = bell_draw(splits[0], (TOKENS, D), 1.0, 6.0, ((0, 128),))
    gates_one = jnp.clip(0.2 + 0.8 * jax.random.uniform(splits[1], (TOKENS,), jnp.float32) ** block_levels(splits[1], (TOKENS,), ((0, 128),), -0.2, 0.2), 0.2, 1.0)
    routes_one_keys = jax.random.split(jax.random.fold_in(splits[2], 1), TOKENS // TOK_DEV)
    routes_one_turns = jax.random.permutation(jax.random.fold_in(splits[2], 3), TOKENS // TOK_DEV)
    routes_one = jax.vmap(lambda own, number: deal_out(jax.random.fold_in(splits[2], 2), own, number, TOK_DEV, EXPERTS, 1, MOST, 2))(routes_one_keys, routes_one_turns).reshape((TOKENS, 1))
    old_place = jax.random.permutation(splits[3], EXPERTS).astype(jnp.int32)
    move_slots = draw_move_slots(jax.random.fold_in(splits[10], 71), 0)
    tokens_two = bell_draw(splits[5], (TOKENS, D), 1.0, 6.0, ((0, 128),))
    gates_two = jnp.clip(0.2 + 0.8 * jax.random.uniform(splits[6], (TOKENS,), jnp.float32) ** block_levels(splits[6], (TOKENS,), ((0, 128),), -0.2, 0.2), 0.2, 1.0)
    routes_two_keys = jax.random.split(jax.random.fold_in(splits[7], 1), TOKENS // TOK_DEV)
    routes_two_turns = jax.random.permutation(jax.random.fold_in(splits[7], 3), TOKENS // TOK_DEV)
    routes_two = jax.vmap(lambda own, number: deal_out(jax.random.fold_in(splits[7], 2), own, number, TOK_DEV, EXPERTS, 1, MOST, 2))(routes_two_keys, routes_two_turns).reshape((TOKENS, 1))
    expert_in = bell_draw(splits[8], (EXPERTS, FF, D), D ** -0.5, 0.21875, ((0, 128),))
    expert_out = bell_draw(splits[9], (EXPERTS, FF, D), FF ** -0.5, 0.109375, ((0, 128),))
    return dict(tokens_one=tokens_one, gates_one=gates_one, routes_one=routes_one, old_place=old_place, move_slots=move_slots, tokens_two=tokens_two, gates_two=gates_two, routes_two=routes_two, expert_in=expert_in, expert_out=expert_out)


def expert_layer(tokens, gates, slot_ids, expert_in, expert_out):
    capacity = N_GX * N_GY * MOST

    def per_slot(combined, which):
        chosen = jnp.nonzero(slot_ids == which, size=capacity, fill_value=TOKENS)[0]
        chosen = chosen.astype(jnp.int32)
        bounded = jnp.minimum(chosen, TOKENS - 1)
        picked = tokens[bounded]
        hidden = jnp.dot(picked, expert_in[which].T, preferred_element_type=jnp.float32)
        hidden = jnp.maximum(hidden, 0.0).astype(jnp.bfloat16)
        result = jnp.dot(hidden, expert_out[which], preferred_element_type=jnp.float32).astype(jnp.bfloat16)
        combined = combined.at[chosen].set(result, mode="drop")
        return combined, None

    start = jnp.zeros((TOKENS, D), jnp.bfloat16)
    combined, unused = lax.scan(per_slot, start, jnp.arange(EXPERTS, dtype=jnp.int32))
    return (gates[:, None] * combined.astype(jnp.float32)).astype(jnp.bfloat16)


def reference(tokens_one, gates_one, routes_one, old_place, move_slots, tokens_two, gates_two, routes_two, expert_in, expert_out):
    slot_one = old_place[routes_one[:, 0]].astype(jnp.int32)
    sources = move_slots[:, 0].astype(jnp.int32)
    targets = move_slots[:, 1].astype(jnp.int32)
    expert_in_new = expert_in.at[targets].set(expert_in[sources])
    expert_out_new = expert_out.at[targets].set(expert_out[sources])
    mixed_one = expert_layer(tokens_one, gates_one, slot_one, expert_in, expert_out)
    slot_two = routes_two[:, 0].astype(jnp.int32)
    mixed_two = expert_layer(tokens_two, gates_two, slot_two, expert_in_new, expert_out_new)
    return (mixed_one, mixed_two, expert_in_new, expert_out_new)
```

```python
import functools

import jax
import jax.numpy as jnp
from jax import lax
from jax.experimental import pallas as pl
from jax.experimental.pallas import tpu as pltpu
from jax.sharding import PartitionSpec as P

MESH = pl.DeviceIdType.MESH
SIDE = 4
CORES = 2
LINE = SIDE * CORES
TURNS = ((0, 1, 2), (1, 2, 0), (2, 0, 1))
LINE_MOST = 5
PLANE_MOST = 6


def bucket_layout(slot_ids, total_slots):
    columns = jnp.arange(total_slots, dtype=jnp.int32)
    member = (slot_ids[:, None] == columns[None, :]).astype(jnp.int32)
    return jnp.sum(jnp.cumsum(member, axis=0) * member, axis=1) - 1


def coordinates(device):
    return ((device // CORES) % SIDE, (device // LINE) % SIDE, device // (LINE * SIDE)), device % CORES


def mesh_id(place, core):
    x, y, z = place
    return (z * SIDE + y, x * CORES + core)


def plan_tables(move_slots, myself):
    moves = move_slots.shape[0]
    source, target = move_slots[:, 0], move_slots[:, 1]
    s_at, s_core = coordinates(source)
    t_at, t_core = coordinates(target)
    m_at, m_core = coordinates(myself)
    order = jnp.arange(moves, dtype=jnp.int32)

    def stack(at, axis):
        return jnp.stack([at[turn[axis]] for turn in TURNS])

    sa, sb, sc = (stack(s_at, axis) for axis in range(3))
    ta, tb, tc = (stack(t_at, axis) for axis in range(3))
    ma, mb, mc = (stack(m_at, axis) for axis in range(3))
    s_line, t_line, planes = sb * SIDE + sc, tb * SIDE + tc, sc * SIDE + tc
    m_line = mb * SIDE + mc

    def rank(group):
        return jnp.sum(
            (group[:, :, None] == group[:, None, :]) & (order[None, :] < order[:, None]),
            axis=2,
            dtype=jnp.int32,
        )

    rank_s, rank_p, rank_t = rank(s_line), rank(planes), rank(t_line)
    fits = (
        (jnp.max(rank_s) < LINE_MOST) & (jnp.max(rank_t) < LINE_MOST) & (jnp.max(rank_p) < PLANE_MOST)
    )

    def pick(mask, slot, count, value):
        hit = mask[:, None, :] & (slot[:, None, :] == jnp.arange(count, dtype=jnp.int32)[None, :, None])
        return jnp.sum(jnp.where(hit, value[:, None, :], 0), axis=2, dtype=jnp.int32)

    two = pick(s_line == m_line[:, None], rank_s, LINE_MOST, sa * CORES + s_core[None])
    three = pick(
        (sc == mc[:, None]) & (rank_p < PLANE_MOST),
        tc * PLANE_MOST + rank_p,
        SIDE * PLANE_MOST,
        jnp.minimum(sb * LINE_MOST + rank_s, SIDE * LINE_MOST - 1),
    )
    four = pick(
        (tc == mc[:, None]) & (rank_t < LINE_MOST),
        tb * LINE_MOST + rank_t,
        SIDE * LINE_MOST,
        jnp.minimum(sc * PLANE_MOST + rank_p, SIDE * PLANE_MOST - 1),
    )
    five = pick(
        t_line == m_line[:, None], ta * CORES + t_core[None], LINE, jnp.minimum(rank_t, LINE_MOST - 1)
    )
    return two, three, four, five, fits


def relocate_kernel(
    two, three, four, five, w_in, w_out, new_in, new_out, first, sent, spread, crossing, crossed, landed, local, send, recv
):
    gx, gy = lax.axis_index("gx"), lax.axis_index("gy")
    at, core = (gy // CORES, gx % SIDE, gx // SIDE), gy % CORES
    piece = first[0][0].shape[1]
    block = spread[0][0].shape[2]
    third = piece * LINE
    sources, targets = (w_in, w_out), (new_in, new_out)
    others = [(step, flip) for step in range(SIDE) for flip in range(CORES) if (step, flip) != (0, 0)]

    def beside(axis, step, flip=0):
        place = list(at)
        place[axis] = (place[axis] + step) % SIDE
        return place, (core + flip) % CORES

    barrier = pltpu.get_barrier_semaphore()
    peers = [beside(0, 0, 1)] + [
        beside(axis, step, flip) for axis in range(3) for step in range(1, SIDE) for flip in range(CORES)
    ]
    for place, which in peers:
        pl.semaphore_signal(barrier, inc=1, device_id=mesh_id(place, which), device_id_type=MESH)
    pl.semaphore_wait(barrier, len(peers))

    def ship(src, dst, stage, half, turn, place, which):
        pltpu.make_async_remote_copy(
            src_ref=src,
            dst_ref=dst,
            send_sem=send.at[stage, half, turn],
            recv_sem=recv.at[stage, half, turn],
            device_id=mesh_id(place, which),
            device_id_type=MESH,
        ).start()

    def settle(semaphore, ref):
        pltpu.make_async_copy(ref, ref, semaphore).wait()

    def rows(turn, index):
        return pl.ds(pl.multiple_of(turn * third + index * piece, piece), piece)

    def spot(turn):
        return at[TURNS[turn][0]] * CORES + core

    def own_first(half, turn):
        me = spot(turn)
        return pltpu.make_async_copy(
            sources[half].at[rows(turn, me)], first[half][turn].at[me], local.at[0, half, turn]
        )

    def own_last(half, turn):
        me = spot(turn)
        return pltpu.make_async_copy(
            first[half][turn].at[me], targets[half].at[rows(turn, me)], local.at[1, half, turn]
        )

    def stage_one(half):
        for turn in range(3):
            me = spot(turn)
            for step, flip in others:
                place, which = beside(TURNS[turn][0], step, flip)
                index = place[TURNS[turn][0]] * CORES + which
                ship(
                    sources[half].at[rows(turn, index)], first[half][turn].at[me], 0, half, turn, place, which
                )
            own_first(half, turn).start()

    def stage_two(half):
        for turn in range(3):
            b = TURNS[turn][1]
            own_first(half, turn).wait()
            settle(recv.at[0, half, turn], first[half][turn].at[pl.ds(0, LINE - 1)])
            for step in (1, 2, 3, 0):
                place, which = beside(b, step)
                cut = pl.ds(pl.multiple_of(place[b] * block, block), block)

                def take(k, carry):
                    data = first[half][turn][two[turn, k], cut, :]
                    if step == 0:
                        spread[half][turn][at[b], k] = data
                    else:
                        sent[half, turn, step - 1, k] = data
                    return carry

                lax.fori_loop(0, LINE_MOST, take, 0)
                if step:
                    ship(sent.at[half, turn, step - 1], spread[half][turn].at[at[b]], 1, half, turn, place, which)

    def stage_three(half):
        for turn in range(3):
            c = TURNS[turn][2]
            settle(recv.at[1, half, turn], spread[half][turn].at[pl.ds(0, SIDE - 1)])
            for step in (1, 2, 3, 0):
                place, which = beside(c, step)

                def take(k, carry):
                    index = three[turn, place[c] * PLANE_MOST + k]
                    data = spread[half][turn][index // LINE_MOST, index % LINE_MOST]
                    if step == 0:
                        crossed[half][turn][at[c], k] = data
                    else:
                        crossing[half, turn, step - 1, k] = data
                    return carry

                lax.fori_loop(0, PLANE_MOST, take, 0)
                if step:
                    ship(crossing.at[half, turn, step - 1], crossed[half][turn].at[at[c]], 2, half, turn, place, which)

    def stage_four(half):
        for turn in range(3):
            b = TURNS[turn][1]
            settle(recv.at[2, half, turn], crossed[half][turn].at[pl.ds(0, SIDE - 1)])
            settle(send.at[1, half, turn], sent.at[half, turn])
            for step in (1, 2, 3, 0):
                place, which = beside(b, step)

                def take(k, carry):
                    index = four[turn, place[b] * LINE_MOST + k]
                    data = crossed[half][turn][index // PLANE_MOST, index % PLANE_MOST]
                    if step == 0:
                        landed[half][turn][at[b], k] = data
                    else:
                        sent[half, turn, step - 1, k] = data
                    return carry

                lax.fori_loop(0, LINE_MOST, take, 0)
                if step:
                    ship(sent.at[half, turn, step - 1], landed[half][turn].at[at[b]], 3, half, turn, place, which)

    def stage_five(half):
        for turn in range(3):
            me = spot(turn)
            settle(recv.at[3, half, turn], landed[half][turn].at[pl.ds(0, SIDE - 1)])
            for step, flip in others + [(0, 0)]:
                place, which = beside(TURNS[turn][0], step, flip)
                index = place[TURNS[turn][0]] * CORES + which
                chosen = five[turn, index]

                def take(quarter, carry):
                    first[half][turn][index, pl.ds(pl.multiple_of(quarter * block, block), block), :] = landed[half][turn][
                        quarter, chosen
                    ]
                    return carry

                lax.fori_loop(0, SIDE, take, 0)
                if (step, flip) != (0, 0):
                    ship(
                        first[half][turn].at[index], targets[half].at[rows(turn, me)], 4, half, turn, place, which
                    )
            own_last(half, turn).start()

    for stage in (stage_one, stage_two, stage_three, stage_four, stage_five):
        for half in range(2):
            stage(half)

    for half in range(2):
        for turn in range(3):
            settle(send.at[0, half, turn], first[half][turn].at[pl.ds(0, LINE - 1)])
            settle(send.at[2, half, turn], crossing.at[half, turn])
            settle(send.at[3, half, turn], sent.at[half, turn])
            settle(send.at[4, half, turn], first[half][turn].at[pl.ds(0, LINE - 1)])
            settle(recv.at[4, half, turn], targets[half].at[pl.ds(0, (LINE - 1) * piece)])
            own_last(half, turn).wait()


def relocate_lines(expert_in, expert_out, two, three, four, five):
    hidden_units, width = expert_in.shape
    piece = hidden_units // (3 * LINE)
    block = piece // SIDE
    dtype = expert_in.dtype
    smem = pl.BlockSpec(memory_space=pltpu.SMEM)
    hbm = pl.BlockSpec(memory_space=pl.ANY)

    def each(*shape):
        return [[pltpu.VMEM(shape, dtype)] * 3] * 2

    return pl.pallas_call(
        relocate_kernel,
        out_shape=[jax.ShapeDtypeStruct((hidden_units, width), dtype)] * 2,
        in_specs=[smem] * 4 + [hbm] * 2,
        out_specs=[hbm] * 2,
        scratch_shapes=[
            each(LINE, piece, width),
            pltpu.VMEM((2, 3, SIDE - 1, LINE_MOST, block, width), dtype),
            each(SIDE, LINE_MOST, block, width),
            pltpu.VMEM((2, 3, SIDE - 1, PLANE_MOST, block, width), dtype),
            each(SIDE, PLANE_MOST, block, width),
            each(SIDE, LINE_MOST, block, width),
            pltpu.SemaphoreType.DMA((2, 2, 3)),
            pltpu.SemaphoreType.DMA((5, 2, 3)),
            pltpu.SemaphoreType.DMA((5, 2, 3)),
        ],
        compiler_params=pltpu.CompilerParams(
            collective_id=1, has_side_effects=True, vmem_limit_bytes=56 * 1024 * 1024
        ),
        cost_estimate=pl.CostEstimate(flops=0, bytes_accessed=400_000_000, transcendentals=0),
    )(two, three, four, five, expert_in, expert_out)


def relocate_everywhere(expert_in, expert_out, move_slots, myself):
    hidden_units, width = expert_in.shape
    device_count = lax.axis_size("gx") * lax.axis_size("gy")
    sources, targets = move_slots[:, 0], move_slots[:, 1]
    devices = jnp.arange(device_count, dtype=jnp.int32)
    anchor = jnp.sum(jnp.where(targets[None, :] == devices[:, None], sources[None, :], 0), axis=1)
    shape = (device_count, hidden_units // device_count, width)
    results = []
    for weights in (expert_in, expert_out):
        held = lax.all_to_all(weights.reshape(shape), ("gx", "gy"), split_axis=0, concat_axis=0, tiled=True)
        forward = jnp.take(held, anchor, axis=0)
        back = lax.all_to_all(forward, ("gx", "gy"), split_axis=0, concat_axis=0, tiled=True)
        results.append(back.reshape(hidden_units, width))
    return results


def shards(
    tokens_one,
    gates_one,
    routes_one,
    old_place,
    move_slots,
    tokens_two,
    gates_two,
    routes_two,
    expert_in,
    expert_out,
):
    experts_all = old_place.shape[0]
    tokens_here, width = tokens_one.shape
    device_count = lax.axis_size("gx") * lax.axis_size("gy")
    capacity = 2 * tokens_here // device_count
    myself = lax.axis_index(("gx", "gy")).astype(jnp.int32)
    columns = jnp.arange(experts_all, dtype=jnp.int32)
    weights_in, weights_out = expert_in[0], expert_out[0]

    slot_one = jnp.sum(jnp.where(routes_one == columns[None, :], old_place[None, :], 0), axis=1)
    came = jnp.sum(
        jnp.where(routes_two == move_slots[None, :, 1], move_slots[None, :, 0] - routes_two, 0), axis=1
    )
    slot_two = routes_two[:, 0] + came
    layout_one = slot_one * (2 * capacity) + bucket_layout(slot_one, experts_all)
    layout_two = slot_two * (2 * capacity) + capacity + bucket_layout(slot_two, experts_all)
    layout = jnp.concatenate([layout_one, layout_two])
    outbox = (
        jnp.zeros((device_count * 2 * capacity, width), jnp.bfloat16)
        .at[layout]
        .set(jnp.concatenate([tokens_one, tokens_two]))
    )
    framed = outbox.reshape(device_count, 2 * capacity, width)
    received = lax.all_to_all(framed, ("gx", "gy"), split_axis=0, concat_axis=0, tiled=True)
    received = received.reshape(device_count * 2 * capacity, width)
    hidden = jnp.einsum("md,fd->mf", received, weights_in, preferred_element_type=jnp.float32)
    hidden = jnp.maximum(hidden, 0.0).astype(jnp.bfloat16)
    produced = jnp.einsum("mf,fd->md", hidden, weights_out, preferred_element_type=jnp.float32)
    produced = produced.astype(jnp.bfloat16).reshape(framed.shape)
    returned = lax.all_to_all(produced, ("gx", "gy"), split_axis=0, concat_axis=0, tiled=True)
    gathered = returned.reshape(-1, width)[layout].astype(jnp.float32)
    mixed_one = (gates_one[:, None] * gathered[:tokens_here]).astype(jnp.bfloat16)
    mixed_two = (gates_two[:, None] * gathered[tokens_here:]).astype(jnp.bfloat16)

    two, three, four, five, fits = plan_tables(move_slots, myself)
    arrived_in, arrived_out = lax.cond(
        fits,
        lambda: tuple(relocate_lines(weights_in, weights_out, two, three, four, five)),
        lambda: tuple(relocate_everywhere(weights_in, weights_out, move_slots, myself)),
    )
    arriving = jnp.any(move_slots[:, 1] == myself)
    fresh_in = jnp.where(arriving, arrived_in, weights_in)[None]
    fresh_out = jnp.where(arriving, arrived_out, weights_out)[None]
    return (mixed_one, mixed_two, fresh_in, fresh_out)


def solution(mesh):
    return jax.shard_map(
        shards,
        mesh=mesh,
        in_specs=(
            P(("gx", "gy"), None),
            P(("gx", "gy")),
            P(("gx", "gy"), None),
            P(),
            P(),
            P(("gx", "gy"), None),
            P(("gx", "gy")),
            P(("gx", "gy"), None),
            P(("gx", "gy"), None, None),
            P(("gx", "gy"), None, None),
        ),
        out_specs=(
            P(("gx", "gy"), None),
            P(("gx", "gy"), None),
            P(("gx", "gy"), None, None),
            P(("gx", "gy"), None, None),
        ),
        check_vma=False,
    )
```

```python
import jax
import jax.numpy as jnp
from jax import lax
from jax.experimental import pallas as pl
from jax.experimental.pallas import tpu as pltpu
from jax.sharding import PartitionSpec as P

MESH = pl.DeviceIdType.MESH
SIDE = 4
CORES = 2
LINE = SIDE * CORES
TURNS = ((0, 1, 2), (1, 2, 0), (2, 0, 1))
LINE_MOST = 5
PLANE_MOST = 6
HALVES = 2
BATCHES = 2


def coordinates(device):
    return ((device // CORES) % SIDE, (device // LINE) % SIDE, device // (LINE * SIDE)), device % CORES


def mesh_id(place, core):
    x, y, z = place
    return (z * SIDE + y, x * CORES + core)


def iota(shape, axis):
    return lax.broadcasted_iota(jnp.int32, shape, axis)


def as_row(column):
    count = column.shape[0]
    return jnp.sum(jnp.where(iota((count, count), 0) == iota((count, count), 1), column, 0), axis=0, keepdims=True)


def as_column(row):
    count = row.shape[1]
    return jnp.sum(jnp.where(iota((count, count), 0) == iota((count, count), 1), row, 0), axis=1, keepdims=True)


def rank_in(group):
    count = group.shape[0]
    same = (group == as_row(group)) & (iota((count, count), 1) < iota((count, count), 0))
    return jnp.sum(jnp.where(same, 1, 0), axis=1, keepdims=True)


def split_rows(blocks):
    count, tall, half = blocks.shape
    wide = blocks.astype(jnp.float32)
    left = wide[:, : tall // 2].reshape(count * tall // 2, half)
    right = wide[:, tall // 2 :].reshape(count * tall // 2, half)
    return jnp.concatenate([left, right], axis=1)


def join_rows(rows, tall):
    count, width = rows.shape[0] // (tall // 2), rows.shape[1]
    left = rows[:, : width // 2].reshape(count, tall // 2, width // 2)
    right = rows[:, width // 2 :].reshape(count, tall // 2, width // 2)
    return jnp.concatenate([left, right], axis=1)


def layer_kernel(
    tokens_one, tokens_two, gates_one, gates_two, routes_one, routes_two, old_place, moves, w_in, w_out,
    mixed_one, mixed_two, fits, new_in, new_out,
    first, sent, spread, crossed, landed, outbox, mailbox, returned, held_in, held_out, feed, total, mixing,
    plan, table, local, send, recv, token_send, token_recv, loads,
):
    gx, gy = lax.axis_index("gx"), lax.axis_index("gy")
    at, core = (gy // CORES, gx % SIDE, gx // SIDE), gy % CORES
    devices = outbox.shape[0]
    tall = outbox.shape[1]
    capacity = tall // 2
    myself = gx * LINE + gy
    piece = first[0][0].shape[1]
    block = spread[0][0].shape[2]
    third = piece * LINE
    sources, targets = (w_in, w_out), (new_in, new_out)
    others = [(step, flip) for step in range(SIDE) for flip in range(CORES) if (step, flip) != (0, 0)]

    def beside(axis, step, flip=0):
        place = list(at)
        place[axis] = (place[axis] + step) % SIDE
        return place, (core + flip) % CORES

    def flat_id(device):
        return (device // LINE, device % LINE)

    barrier = pltpu.get_barrier_semaphore()

    def greet(step, carry):
        peer = (myself + step) % devices
        pl.semaphore_signal(barrier, inc=1, device_id=flat_id(peer), device_id_type=MESH)
        return carry

    lax.fori_loop(1, devices, greet, 0)
    pl.semaphore_wait(barrier, devices - 1)

    def ship(src, dst, stage, half, turn, place, which):
        pltpu.make_async_remote_copy(
            src_ref=src,
            dst_ref=dst,
            send_sem=send.at[stage, half, turn],
            recv_sem=recv.at[stage, half, turn],
            device_id=mesh_id(place, which),
            device_id_type=MESH,
        ).start()

    def settle(semaphore, ref):
        pltpu.make_async_copy(ref, ref, semaphore).wait()

    def rows(turn, index):
        return pl.ds(pl.multiple_of(turn * third + index * piece, piece), piece)

    def spot(turn):
        return at[TURNS[turn][0]] * CORES + core

    def own_first(half, turn):
        me = spot(turn)
        return pltpu.make_async_copy(
            sources[half].at[rows(turn, me)], first[half][turn].at[me], local.at[0, half, turn]
        )

    def own_last(half, turn):
        me = spot(turn)
        return pltpu.make_async_copy(
            first[half][turn].at[me], targets[half].at[rows(turn, me)], local.at[1, half, turn]
        )

    def stage_one(half):
        for turn in range(3):
            me = spot(turn)
            for step, flip in others:
                place, which = beside(TURNS[turn][0], step, flip)
                index = place[TURNS[turn][0]] * CORES + which
                ship(
                    sources[half].at[rows(turn, index)], first[half][turn].at[me], 0, half, turn, place, which
                )
            own_first(half, turn).start()

    def stage_two(half):
        for turn in range(3):
            b = TURNS[turn][1]
            own_first(half, turn).wait()
            settle(recv.at[0, half, turn], first[half][turn].at[pl.ds(0, LINE - 1)])
            for step in (1, 2, 3, 0):
                place, which = beside(b, step)
                cut = pl.ds(pl.multiple_of(place[b] * block, block), block)

                def take(k, carry):
                    data = first[half][turn][table[4 * turn, k], cut, :]
                    if step == 0:
                        spread[half][turn][at[b], k] = data
                    else:
                        sent[half, turn, step - 1, k] = data
                    return carry

                lax.fori_loop(0, LINE_MOST, take, 0)
                if step:
                    ship(sent.at[half, turn, step - 1, pl.ds(0, LINE_MOST)], spread[half][turn].at[at[b]], 1, half, turn, place, which)

    def stage_three(half):
        for turn in range(3):
            c = TURNS[turn][2]
            settle(recv.at[1, half, turn], spread[half][turn].at[pl.ds(0, SIDE - 1)])
            settle(send.at[1, half, turn], sent.at[half, turn, :, pl.ds(0, LINE_MOST)])
            for step in (1, 2, 3, 0):
                place, which = beside(c, step)

                def take(k, carry):
                    index = table[4 * turn + 1, place[c] * PLANE_MOST + k]
                    data = spread[half][turn][index // LINE_MOST, index % LINE_MOST]
                    if step == 0:
                        crossed[half][turn][at[c], k] = data
                    else:
                        sent[half, turn, step - 1, k] = data
                    return carry

                lax.fori_loop(0, PLANE_MOST, take, 0)
                if step:
                    ship(sent.at[half, turn, step - 1, pl.ds(0, PLANE_MOST)], crossed[half][turn].at[at[c]], 2, half, turn, place, which)

    def stage_four(half):
        for turn in range(3):
            b = TURNS[turn][1]
            settle(recv.at[2, half, turn], crossed[half][turn].at[pl.ds(0, SIDE - 1)])
            settle(send.at[2, half, turn], sent.at[half, turn, :, pl.ds(0, PLANE_MOST)])
            for step in (1, 2, 3, 0):
                place, which = beside(b, step)

                def take(k, carry):
                    index = table[4 * turn + 2, place[b] * LINE_MOST + k]
                    data = crossed[half][turn][index // PLANE_MOST, index % PLANE_MOST]
                    if step == 0:
                        landed[half][turn][at[b], k] = data
                    else:
                        sent[half, turn, step - 1, k] = data
                    return carry

                lax.fori_loop(0, LINE_MOST, take, 0)
                if step:
                    ship(sent.at[half, turn, step - 1, pl.ds(0, LINE_MOST)], landed[half][turn].at[at[b]], 3, half, turn, place, which)

    def stage_five(half):
        for turn in range(3):
            me = spot(turn)
            settle(recv.at[3, half, turn], landed[half][turn].at[pl.ds(0, SIDE - 1)])
            for step, flip in others + [(0, 0)]:
                place, which = beside(TURNS[turn][0], step, flip)
                index = place[TURNS[turn][0]] * CORES + which
                chosen = table[4 * turn + 3, index]

                def take(quarter, carry):
                    first[half][turn][index, pl.ds(pl.multiple_of(quarter * block, block), block), :] = landed[half][turn][
                        quarter, chosen
                    ]
                    return carry

                lax.fori_loop(0, SIDE, take, 0)
                if (step, flip) != (0, 0):
                    ship(
                        first[half][turn].at[index], targets[half].at[rows(turn, me)], 4, half, turn, place, which
                    )
            own_last(half, turn).start()

    def make_plan():
        source, target = moves[:, 0:1], moves[:, 1:2]
        count = source.shape[0]
        s_at, s_core = coordinates(source)
        t_at, t_core = coordinates(target)
        wide = (count, plan.shape[1])
        entry = iota(wide, 1)
        worst = jnp.zeros((1, 1), jnp.int32)
        plan[...] = jnp.zeros(plan.shape, jnp.int32)
        for turn, (a, b, c) in enumerate(TURNS):
            s_line, t_line = s_at[b] * SIDE + s_at[c], t_at[b] * SIDE + t_at[c]
            rank_s, rank_t, rank_p = rank_in(s_line), rank_in(t_line), rank_in(s_at[c] * SIDE + t_at[c])
            over = jnp.maximum(jnp.maximum(rank_s, rank_t) - LINE_MOST, rank_p - PLANE_MOST) + 1
            worst = jnp.maximum(worst, jnp.max(over, axis=0, keepdims=True))
            rank_s, rank_t = jnp.minimum(rank_s, LINE_MOST - 1), jnp.minimum(rank_t, LINE_MOST - 1)
            rank_p = jnp.minimum(rank_p, PLANE_MOST - 1)
            here = at[b] * SIDE + at[c]
            for row, (mine, slot, value, largest) in enumerate(
                (
                    (s_line == here, rank_s, s_at[a] * CORES + s_core, LINE - 1),
                    (
                        s_at[c] == at[c],
                        t_at[c] * PLANE_MOST + rank_p,
                        s_at[b] * LINE_MOST + rank_s,
                        SIDE * LINE_MOST - 1,
                    ),
                    (
                        t_at[c] == at[c],
                        t_at[b] * LINE_MOST + rank_t,
                        s_at[c] * PLANE_MOST + rank_p,
                        SIDE * PLANE_MOST - 1,
                    ),
                    (t_line == here, t_at[a] * CORES + t_core, rank_t, LINE_MOST - 1),
                )
            ):
                key = jnp.where(mine, slot, -1)
                found = jnp.sum(jnp.where(key == entry, value, 0), axis=0, keepdims=True)
                index = 4 * turn + row
                plan[index : index + 1, :] = jnp.minimum(found, largest)
        fits[...] = jnp.broadcast_to(worst, fits.shape)
        copy = pltpu.make_async_copy(plan, table, loads.at[2])
        copy.start()
        copy.wait()

    def positions():
        routes = routes_one[...]
        slot_one = jnp.sum(
            jnp.where(routes == iota((routes.shape[0], old_place.shape[1]), 1), old_place[...], 0),
            axis=1,
            keepdims=True,
        )
        goal = routes_two[...]
        source, target = as_row(moves[:, 0:1]), as_row(moves[:, 1:2])
        slot_two = goal + jnp.sum(jnp.where(goal == target, source - goal, 0), axis=1, keepdims=True)
        place_one = slot_one * capacity + rank_in(slot_one)
        place_two = slot_two * capacity + capacity // BATCHES + rank_in(slot_two)
        return place_one, place_two

    def one_hot(mask):
        return jnp.where(mask, 1.0, 0.0).astype(jnp.bfloat16)

    def fill_outbox(place_one, place_two):
        row_one, row_two = as_row(place_one), as_row(place_two)
        group = 16
        count = group * capacity

        def fill(index, carry):
            rows_here = iota((count, row_one.shape[1]), 0) + index * count
            picked = jnp.dot(one_hot(rows_here == row_one), tokens_one[...], preferred_element_type=jnp.float32)
            picked += jnp.dot(one_hot(rows_here == row_two), tokens_two[...], preferred_element_type=jnp.float32)
            outbox[pl.ds(index * group, group)] = join_rows(picked, tall).astype(jnp.bfloat16)
            return carry

        lax.fori_loop(0, devices // group, fill, 0)

    def post(src, dst, way, peer):
        pltpu.make_async_remote_copy(
            src_ref=src,
            dst_ref=dst,
            send_sem=token_send.at[way],
            recv_sem=token_recv.at[way],
            device_id=flat_id(peer),
            device_id_type=MESH,
        ).start()

    def send_tokens():
        def go(step, carry):
            peer = (myself + step) % devices
            post(outbox.at[peer], mailbox.at[myself], 0, peer)
            return carry

        lax.fori_loop(1, devices, go, 0)
        mailbox[myself] = outbox[myself]

    group = 32
    tile = 512

    def experts(index):
        begin = index * group
        feed[...] = split_rows(mailbox[pl.ds(begin, group)]).astype(jnp.bfloat16)
        total[...] = jnp.zeros(total.shape, jnp.float32)

        def part(step, carry):
            cut = pl.ds(pl.multiple_of(step * tile, tile), tile)
            hidden = lax.dot_general(
                feed[...], held_in[cut, :], (((1,), (1,)), ((), ())), preferred_element_type=jnp.float32
            )
            hidden = jnp.maximum(hidden, 0.0).astype(jnp.bfloat16)
            total[...] += jnp.dot(hidden, held_out[cut, :], preferred_element_type=jnp.float32)
            return carry

        lax.fori_loop(0, held_in.shape[0] // tile, part, 0)
        mailbox[pl.ds(begin, group)] = join_rows(total[...], tall).astype(jnp.bfloat16)

        def back(peer, carry):
            @pl.when(peer != myself)
            def _():
                post(mailbox.at[peer], returned.at[myself], 1, peer)

            return carry

        lax.fori_loop(begin, begin + group, back, 0)

    def collect(place_one, place_two):
        count = group * capacity
        mixing[...] = jnp.zeros(mixing.shape, jnp.float32)
        tokens_here = place_one.shape[0]

        def add(index, carry):
            results = split_rows(returned[pl.ds(index * group, group)]).astype(jnp.bfloat16)
            columns = iota((tokens_here, count), 1) + index * count
            for batch, place in enumerate((place_one, place_two)):
                mixing[batch] += jnp.dot(one_hot(columns == place), results, preferred_element_type=jnp.float32)
            return carry

        lax.fori_loop(0, devices // group, add, 0)
        mixed_one[...] = (as_column(gates_one[...]) * mixing[0]).astype(jnp.bfloat16)
        mixed_two[...] = (as_column(gates_two[...]) * mixing[1]).astype(jnp.bfloat16)

    load_in = pltpu.make_async_copy(w_in, held_in, loads.at[0])
    load_out = pltpu.make_async_copy(w_out, held_out, loads.at[1])

    stage_one(0)
    place_one, place_two = positions()
    fill_outbox(place_one, place_two)
    send_tokens()
    stage_one(1)
    load_in.start()
    load_out.start()
    make_plan()
    stage_two(0)
    stage_two(1)
    stage_three(0)
    load_in.wait()
    load_out.wait()
    settle(token_recv.at[0], mailbox.at[pl.ds(0, devices - 1)])
    experts(0)
    experts(1)
    stage_three(1)
    experts(2)
    experts(3)
    returned[myself] = mailbox[myself]
    stage_four(0)
    stage_four(1)
    stage_five(0)
    stage_five(1)
    settle(token_recv.at[1], returned.at[pl.ds(0, devices - 1)])
    collect(place_one, place_two)
    settle(token_send.at[0], outbox.at[pl.ds(0, devices - 1)])
    settle(token_send.at[1], mailbox.at[pl.ds(0, devices - 1)])

    for half in range(HALVES):
        for turn in range(3):
            settle(send.at[0, half, turn], first[half][turn].at[pl.ds(0, LINE - 1)])
            settle(send.at[3, half, turn], sent.at[half, turn, :, pl.ds(0, LINE_MOST)])
            settle(send.at[4, half, turn], first[half][turn].at[pl.ds(0, LINE - 1)])
            settle(recv.at[4, half, turn], targets[half].at[pl.ds(0, (LINE - 1) * piece)])
            own_last(half, turn).wait()


def layer(tokens_one, tokens_two, gates_one, gates_two, routes_one, routes_two, old_place, moves, w_in, w_out):
    hidden_units, width = w_in.shape
    tokens_here = tokens_one.shape[0]
    devices = lax.axis_size("gx") * lax.axis_size("gy")
    tall = 2 * BATCHES * (2 * tokens_here // devices)
    piece = hidden_units // (3 * LINE)
    block = piece // SIDE
    dtype = w_in.dtype
    vmem = pl.BlockSpec(memory_space=pltpu.VMEM)
    hbm = pl.BlockSpec(memory_space=pl.ANY)
    most = max(LINE_MOST, PLANE_MOST)

    def each(*shape):
        return [[pltpu.VMEM(shape, dtype)] * 3] * HALVES

    return pl.pallas_call(
        layer_kernel,
        out_shape=[jax.ShapeDtypeStruct((tokens_here, width), dtype)] * 2
        + [jax.ShapeDtypeStruct((8, 128), jnp.int32)]
        + [jax.ShapeDtypeStruct((hidden_units, width), dtype)] * 2,
        in_specs=[vmem] * 8 + [hbm] * 2,
        out_specs=[vmem] * 3 + [hbm] * 2,
        scratch_shapes=[
            each(LINE, piece, width),
            pltpu.VMEM((HALVES, 3, SIDE - 1, most, block, width), dtype),
            each(SIDE, LINE_MOST, block, width),
            each(SIDE, PLANE_MOST, block, width),
            each(SIDE, LINE_MOST, block, width),
            pltpu.VMEM((devices, tall, width // 2), dtype),
            pltpu.VMEM((devices, tall, width // 2), dtype),
            pltpu.VMEM((devices, tall, width // 2), dtype),
            pltpu.VMEM((hidden_units, width), dtype),
            pltpu.VMEM((hidden_units, width), dtype),
            pltpu.VMEM((32 * tall // 2, width), dtype),
            pltpu.VMEM((32 * tall // 2, width), jnp.float32),
            pltpu.VMEM((BATCHES, tokens_here, width), jnp.float32),
            pltpu.VMEM((16, 128), jnp.int32),
            pltpu.SMEM((16, 128), jnp.int32),
            pltpu.SemaphoreType.DMA((2, HALVES, 3)),
            pltpu.SemaphoreType.DMA((5, HALVES, 3)),
            pltpu.SemaphoreType.DMA((5, HALVES, 3)),
            pltpu.SemaphoreType.DMA((2,)),
            pltpu.SemaphoreType.DMA((2,)),
            pltpu.SemaphoreType.DMA((3,)),
        ],
        compiler_params=pltpu.CompilerParams(
            collective_id=1, has_side_effects=True, vmem_limit_bytes=60 * 1024 * 1024
        ),
        cost_estimate=pl.CostEstimate(
            flops=8 * tokens_here * hidden_units * width, bytes_accessed=400_000_000, transcendentals=0
        ),
    )(
        tokens_one,
        tokens_two,
        gates_one.reshape(1, tokens_here),
        gates_two.reshape(1, tokens_here),
        routes_one,
        routes_two,
        old_place.reshape(1, -1),
        moves,
        w_in,
        w_out,
    )


def keep_kernel(arriving, came_in, came_out, own_in, own_out, fresh_in, fresh_out, sems):
    def carry(sources):
        parts = 4
        copies = []
        for half, (source, target) in enumerate(zip(sources, (fresh_in, fresh_out))):
            count = source.shape[0] // parts
            for part in range(parts):
                cut = pl.ds(part * count, count)
                copies.append(pltpu.make_async_copy(source.at[cut], target.at[0, cut], sems.at[half, part]))
        for copy in copies:
            copy.start()
        for copy in copies:
            copy.wait()

    @pl.when(arriving[0] != 0)
    def _():
        carry((came_in, came_out))

    @pl.when(arriving[0] == 0)
    def _():
        carry((own_in.at[0], own_out.at[0]))


def keep(arriving, came_in, came_out, own_in, own_out):
    hbm = pl.BlockSpec(memory_space=pl.ANY)
    return pl.pallas_call(
        keep_kernel,
        out_shape=[jax.ShapeDtypeStruct(own_in.shape, own_in.dtype)] * 2,
        in_specs=[pl.BlockSpec(memory_space=pltpu.SMEM)] + [hbm] * 4,
        out_specs=[hbm] * 2,
        scratch_shapes=[pltpu.SemaphoreType.DMA((HALVES, 4))],
    )(arriving, came_in, came_out, own_in, own_out)


def relocate_everywhere(expert_in, expert_out, move_slots, myself):
    hidden_units, width = expert_in.shape
    device_count = lax.axis_size("gx") * lax.axis_size("gy")
    sources, targets = move_slots[:, 0], move_slots[:, 1]
    devices = jnp.arange(device_count, dtype=jnp.int32)
    anchor = jnp.sum(jnp.where(targets[None, :] == devices[:, None], sources[None, :], 0), axis=1)
    shape = (device_count, hidden_units // device_count, width)
    results = []
    for weights in (expert_in, expert_out):
        held = lax.all_to_all(weights.reshape(shape), ("gx", "gy"), split_axis=0, concat_axis=0, tiled=True)
        forward = jnp.take(held, anchor, axis=0)
        back = lax.all_to_all(forward, ("gx", "gy"), split_axis=0, concat_axis=0, tiled=True)
        results.append(back.reshape(hidden_units, width))
    return results


def shards(
    tokens_one,
    gates_one,
    routes_one,
    old_place,
    move_slots,
    tokens_two,
    gates_two,
    routes_two,
    expert_in,
    expert_out,
):
    myself = lax.axis_index(("gx", "gy")).astype(jnp.int32)
    weights_in, weights_out = expert_in[0], expert_out[0]
    mixed_one, mixed_two, excess, came_in, came_out = layer(
        tokens_one,
        tokens_two,
        gates_one,
        gates_two,
        routes_one,
        routes_two,
        old_place,
        move_slots,
        weights_in,
        weights_out,
    )
    came_in, came_out = lax.cond(
        excess[0, 0] == 0,
        lambda: (came_in, came_out),
        lambda: tuple(relocate_everywhere(weights_in, weights_out, move_slots, myself)),
    )
    arriving = jnp.any(move_slots[:, 1] == myself).astype(jnp.int32).reshape(1)
    fresh_in, fresh_out = keep(arriving, came_in, came_out, expert_in, expert_out)
    return (mixed_one, mixed_two, fresh_in, fresh_out)


def solution(mesh):
    return jax.shard_map(
        shards,
        mesh=mesh,
        in_specs=(
            P(("gx", "gy"), None),
            P(("gx", "gy")),
            P(("gx", "gy"), None),
            P(),
            P(),
            P(("gx", "gy"), None),
            P(("gx", "gy")),
            P(("gx", "gy"), None),
            P(("gx", "gy"), None, None),
            P(("gx", "gy"), None, None),
        ),
        out_specs=(
            P(("gx", "gy"), None),
            P(("gx", "gy"), None),
            P(("gx", "gy"), None, None),
            P(("gx", "gy"), None, None),
        ),
        check_vma=False,
    )
```

```python
import jax
import jax.numpy as jnp
from jax import lax
from jax.experimental import pallas as pl
from jax.experimental.pallas import tpu as pltpu
from jax.sharding import PartitionSpec as P

MESH = pl.DeviceIdType.MESH
SIDE = 4
CORES = 2
LINE = SIDE * CORES
TURNS = ((0, 1, 2), (1, 2, 0), (2, 0, 1))
LINE_MOST = 5
PLANE_MOST = 6
HALVES = 2
BATCHES = 2


def coordinates(device):
    return ((device // CORES) % SIDE, (device // LINE) % SIDE, device // (LINE * SIDE)), device % CORES


def mesh_id(place, core):
    x, y, z = place
    return (z * SIDE + y, x * CORES + core)


def iota(shape, axis):
    return lax.broadcasted_iota(jnp.int32, shape, axis)


def as_row(column):
    count = column.shape[0]
    return jnp.sum(jnp.where(iota((count, count), 0) == iota((count, count), 1), column, 0), axis=0, keepdims=True)


def as_column(row):
    count = row.shape[1]
    return jnp.sum(jnp.where(iota((count, count), 0) == iota((count, count), 1), row, 0), axis=1, keepdims=True)


def rank_in(group):
    count = group.shape[0]
    same = (group == as_row(group)) & (iota((count, count), 1) < iota((count, count), 0))
    return jnp.sum(jnp.where(same, 1, 0), axis=1, keepdims=True)


def split_rows(blocks):
    count, tall, half = blocks.shape
    wide = blocks.astype(jnp.float32)
    left = wide[:, : tall // 2].reshape(count * tall // 2, half)
    right = wide[:, tall // 2 :].reshape(count * tall // 2, half)
    return jnp.concatenate([left, right], axis=1)


def join_rows(rows, tall):
    count, width = rows.shape[0] // (tall // 2), rows.shape[1]
    left = rows[:, : width // 2].reshape(count, tall // 2, width // 2)
    right = rows[:, width // 2 :].reshape(count, tall // 2, width // 2)
    return jnp.concatenate([left, right], axis=1)


def layer_kernel(
    tokens_one, tokens_two, gates_one, gates_two, routes_one, routes_two, old_place, moves, w_in, w_out,
    mixed_one, mixed_two, flags, new_in, new_out,
    first, sent, spread, crossed, landed, outbox, mailbox, returned, held_in, held_out, feed, total, mixing,
    plan, table, local, send, recv, token_send, token_recv, loads,
):
    gx, gy = lax.axis_index("gx"), lax.axis_index("gy")
    at, core = (gy // CORES, gx % SIDE, gx // SIDE), gy % CORES
    devices = outbox.shape[0]
    tall = outbox.shape[1]
    capacity = tall // 2
    myself = gx * LINE + gy
    piece = first[0][0].shape[1]
    block = spread[0][0].shape[2]
    third = piece * LINE
    sources, targets = (w_in, w_out), (new_in, new_out)
    others = [(step, flip) for step in range(SIDE) for flip in range(CORES) if (step, flip) != (0, 0)]

    def beside(axis, step, flip=0):
        place = list(at)
        place[axis] = (place[axis] + step) % SIDE
        return place, (core + flip) % CORES

    def flat_id(device):
        return (device // LINE, device % LINE)

    barrier = pltpu.get_barrier_semaphore()

    def greet(step, carry):
        peer = (myself + step) % devices
        pl.semaphore_signal(barrier, inc=1, device_id=flat_id(peer), device_id_type=MESH)
        return carry

    lax.fori_loop(1, devices, greet, 0)
    pl.semaphore_wait(barrier, devices - 1)

    def ship(src, dst, stage, half, turn, place, which):
        pltpu.make_async_remote_copy(
            src_ref=src,
            dst_ref=dst,
            send_sem=send.at[stage, half, turn],
            recv_sem=recv.at[stage, half, turn],
            device_id=mesh_id(place, which),
            device_id_type=MESH,
        ).start()

    def settle(semaphore, ref):
        pltpu.make_async_copy(ref, ref, semaphore).wait()

    def rows(turn, index):
        return pl.ds(pl.multiple_of(turn * third + index * piece, piece), piece)

    def spot(turn):
        return at[TURNS[turn][0]] * CORES + core

    def own_first(half, turn):
        me = spot(turn)
        return pltpu.make_async_copy(
            sources[half].at[rows(turn, me)], first[half][turn].at[me], local.at[0, half, turn]
        )

    def own_last(half, turn):
        me = spot(turn)
        return pltpu.make_async_copy(
            first[half][turn].at[me], targets[half].at[rows(turn, me)], local.at[1, half, turn]
        )

    def stage_one(half):
        for turn in range(3):
            me = spot(turn)
            for step, flip in others:
                place, which = beside(TURNS[turn][0], step, flip)
                index = place[TURNS[turn][0]] * CORES + which
                ship(
                    sources[half].at[rows(turn, index)], first[half][turn].at[me], 0, half, turn, place, which
                )
            own_first(half, turn).start()

    def stage_two(half):
        for turn in range(3):
            b = TURNS[turn][1]
            own_first(half, turn).wait()
            settle(recv.at[0, half, turn], first[half][turn].at[pl.ds(0, LINE - 1)])
            for step in (1, 2, 3, 0):
                place, which = beside(b, step)
                cut = pl.ds(pl.multiple_of(place[b] * block, block), block)

                def take(k, carry):
                    data = first[half][turn][table[4 * turn, k], cut, :]
                    if step == 0:
                        spread[half][turn][at[b], k] = data
                    else:
                        sent[half, turn, step - 1, k] = data
                    return carry

                lax.fori_loop(0, LINE_MOST, take, 0)
                if step:
                    ship(sent.at[half, turn, step - 1, pl.ds(0, LINE_MOST)], spread[half][turn].at[at[b]], 1, half, turn, place, which)

    def stage_three(half):
        for turn in range(3):
            c = TURNS[turn][2]
            settle(recv.at[1, half, turn], spread[half][turn].at[pl.ds(0, SIDE - 1)])
            settle(send.at[1, half, turn], sent.at[half, turn, :, pl.ds(0, LINE_MOST)])
            for step in (1, 2, 3, 0):
                place, which = beside(c, step)

                def take(k, carry):
                    index = table[4 * turn + 1, place[c] * PLANE_MOST + k]
                    data = spread[half][turn][index // LINE_MOST, index % LINE_MOST]
                    if step == 0:
                        crossed[half][turn][at[c], k] = data
                    else:
                        sent[half, turn, step - 1, k] = data
                    return carry

                lax.fori_loop(0, PLANE_MOST, take, 0)
                if step:
                    ship(sent.at[half, turn, step - 1, pl.ds(0, PLANE_MOST)], crossed[half][turn].at[at[c]], 2, half, turn, place, which)

    def stage_four(half):
        for turn in range(3):
            b = TURNS[turn][1]
            settle(recv.at[2, half, turn], crossed[half][turn].at[pl.ds(0, SIDE - 1)])
            settle(send.at[2, half, turn], sent.at[half, turn, :, pl.ds(0, PLANE_MOST)])
            for step in (1, 2, 3, 0):
                place, which = beside(b, step)

                def take(k, carry):
                    index = table[4 * turn + 2, place[b] * LINE_MOST + k]
                    data = crossed[half][turn][index // PLANE_MOST, index % PLANE_MOST]
                    if step == 0:
                        landed[half][turn][at[b], k] = data
                    else:
                        sent[half, turn, step - 1, k] = data
                    return carry

                lax.fori_loop(0, LINE_MOST, take, 0)
                if step:
                    ship(sent.at[half, turn, step - 1, pl.ds(0, LINE_MOST)], landed[half][turn].at[at[b]], 3, half, turn, place, which)

    def stage_five(half):
        for turn in range(3):
            me = spot(turn)
            settle(recv.at[3, half, turn], landed[half][turn].at[pl.ds(0, SIDE - 1)])
            for step, flip in others + [(0, 0)]:
                place, which = beside(TURNS[turn][0], step, flip)
                index = place[TURNS[turn][0]] * CORES + which
                chosen = table[4 * turn + 3, index]

                def take(quarter, carry):
                    first[half][turn][index, pl.ds(pl.multiple_of(quarter * block, block), block), :] = landed[half][turn][
                        quarter, chosen
                    ]
                    return carry

                lax.fori_loop(0, SIDE, take, 0)
                if (step, flip) != (0, 0):
                    ship(
                        first[half][turn].at[index], targets[half].at[rows(turn, me)], 4, half, turn, place, which
                    )
            own_last(half, turn).start()

    def make_plan():
        source, target = as_column(moves[0:1, :]), as_column(moves[1:2, :])
        count = source.shape[0]
        s_at, s_core = coordinates(source)
        t_at, t_core = coordinates(target)
        wide = (count, plan.shape[1])
        entry = iota(wide, 1)
        worst = jnp.zeros((1, 1), jnp.int32)
        plan[...] = jnp.zeros(plan.shape, jnp.int32)
        for turn, (a, b, c) in enumerate(TURNS):
            s_line, t_line = s_at[b] * SIDE + s_at[c], t_at[b] * SIDE + t_at[c]
            rank_s, rank_t, rank_p = rank_in(s_line), rank_in(t_line), rank_in(s_at[c] * SIDE + t_at[c])
            over = jnp.maximum(jnp.maximum(rank_s, rank_t) - LINE_MOST, rank_p - PLANE_MOST) + 1
            worst = jnp.maximum(worst, jnp.max(over, axis=0, keepdims=True))
            rank_s, rank_t = jnp.minimum(rank_s, LINE_MOST - 1), jnp.minimum(rank_t, LINE_MOST - 1)
            rank_p = jnp.minimum(rank_p, PLANE_MOST - 1)
            here = at[b] * SIDE + at[c]
            for row, (mine, slot, value, largest) in enumerate(
                (
                    (s_line == here, rank_s, s_at[a] * CORES + s_core, LINE - 1),
                    (
                        s_at[c] == at[c],
                        t_at[c] * PLANE_MOST + rank_p,
                        s_at[b] * LINE_MOST + rank_s,
                        SIDE * LINE_MOST - 1,
                    ),
                    (
                        t_at[c] == at[c],
                        t_at[b] * LINE_MOST + rank_t,
                        s_at[c] * PLANE_MOST + rank_p,
                        SIDE * PLANE_MOST - 1,
                    ),
                    (t_line == here, t_at[a] * CORES + t_core, rank_t, LINE_MOST - 1),
                )
            ):
                key = jnp.where(mine, slot, -1)
                found = jnp.sum(jnp.where(key == entry, value, 0), axis=0, keepdims=True)
                index = 4 * turn + row
                plan[index : index + 1, :] = jnp.minimum(found, largest)
        arriving = jnp.max(jnp.where(target == myself, 1, 0), axis=0, keepdims=True)
        flags[0:1, :] = jnp.broadcast_to(jnp.maximum(worst, 0), (1, flags.shape[1]))
        flags[1:2, :] = jnp.broadcast_to(arriving, (1, flags.shape[1]))
        copy = pltpu.make_async_copy(plan, table, loads.at[2])
        copy.start()
        copy.wait()

    def positions():
        routes = as_column(routes_one[...])
        slot_one = jnp.sum(
            jnp.where(routes == iota((routes.shape[0], old_place.shape[1]), 1), old_place[...], 0),
            axis=1,
            keepdims=True,
        )
        goal = as_column(routes_two[...])
        source, target = moves[0:1, :], moves[1:2, :]
        slot_two = goal + jnp.sum(jnp.where(goal == target, source - goal, 0), axis=1, keepdims=True)
        place_one = slot_one * capacity + rank_in(slot_one)
        place_two = slot_two * capacity + capacity // BATCHES + rank_in(slot_two)
        return place_one, place_two

    def one_hot(mask):
        return jnp.where(mask, 1.0, 0.0).astype(jnp.bfloat16)

    def fill_outbox(place_one, place_two):
        row_one, row_two = as_row(place_one), as_row(place_two)
        group = 16
        count = group * capacity

        def fill(index, carry):
            rows_here = iota((count, row_one.shape[1]), 0) + index * count
            picked = jnp.dot(one_hot(rows_here == row_one), tokens_one[...], preferred_element_type=jnp.float32)
            picked += jnp.dot(one_hot(rows_here == row_two), tokens_two[...], preferred_element_type=jnp.float32)
            outbox[pl.ds(index * group, group)] = join_rows(picked, tall).astype(jnp.bfloat16)
            return carry

        lax.fori_loop(0, devices // group, fill, 0)

    def post(src, dst, way, peer):
        pltpu.make_async_remote_copy(
            src_ref=src,
            dst_ref=dst,
            send_sem=token_send.at[way],
            recv_sem=token_recv.at[way],
            device_id=flat_id(peer),
            device_id_type=MESH,
        ).start()

    def send_tokens():
        def go(step, carry):
            peer = (myself + step) % devices
            post(outbox.at[peer], mailbox.at[myself], 0, peer)
            return carry

        lax.fori_loop(1, devices, go, 0)
        mailbox[myself] = outbox[myself]

    group = 32
    tile = 512

    def experts(index):
        begin = index * group
        feed[...] = split_rows(mailbox[pl.ds(begin, group)]).astype(jnp.bfloat16)
        total[...] = jnp.zeros(total.shape, jnp.float32)

        def part(step, carry):
            cut = pl.ds(pl.multiple_of(step * tile, tile), tile)
            hidden = lax.dot_general(
                feed[...], held_in[cut, :], (((1,), (1,)), ((), ())), preferred_element_type=jnp.float32
            )
            hidden = jnp.maximum(hidden, 0.0).astype(jnp.bfloat16)
            total[...] += jnp.dot(hidden, held_out[cut, :], preferred_element_type=jnp.float32)
            return carry

        lax.fori_loop(0, held_in.shape[0] // tile, part, 0)
        mailbox[pl.ds(begin, group)] = join_rows(total[...], tall).astype(jnp.bfloat16)

        def back(peer, carry):
            @pl.when(peer != myself)
            def _():
                post(mailbox.at[peer], returned.at[myself], 1, peer)

            return carry

        lax.fori_loop(begin, begin + group, back, 0)

    def collect(place_one, place_two):
        count = group * capacity
        mixing[...] = jnp.zeros(mixing.shape, jnp.float32)
        tokens_here = place_one.shape[0]

        def add(index, carry):
            results = split_rows(returned[pl.ds(index * group, group)]).astype(jnp.bfloat16)
            columns = iota((tokens_here, count), 1) + index * count
            for batch, place in enumerate((place_one, place_two)):
                mixing[batch] += jnp.dot(one_hot(columns == place), results, preferred_element_type=jnp.float32)
            return carry

        lax.fori_loop(0, devices // group, add, 0)
        mixed_one[...] = (as_column(gates_one[...]) * mixing[0]).astype(jnp.bfloat16)
        mixed_two[...] = (as_column(gates_two[...]) * mixing[1]).astype(jnp.bfloat16)

    load_in = pltpu.make_async_copy(w_in, held_in, loads.at[0])
    load_out = pltpu.make_async_copy(w_out, held_out, loads.at[1])

    stage_one(0)
    place_one, place_two = positions()
    fill_outbox(place_one, place_two)
    send_tokens()
    stage_one(1)
    load_in.start()
    load_out.start()
    make_plan()
    stage_two(0)
    stage_two(1)
    stage_three(0)
    load_in.wait()
    load_out.wait()
    settle(token_recv.at[0], mailbox.at[pl.ds(0, devices - 1)])
    experts(0)
    experts(1)
    stage_three(1)
    experts(2)
    experts(3)
    returned[myself] = mailbox[myself]
    stage_four(0)
    stage_four(1)
    stage_five(0)
    stage_five(1)
    settle(token_recv.at[1], returned.at[pl.ds(0, devices - 1)])
    collect(place_one, place_two)
    settle(token_send.at[0], outbox.at[pl.ds(0, devices - 1)])
    settle(token_send.at[1], mailbox.at[pl.ds(0, devices - 1)])

    for half in range(HALVES):
        for turn in range(3):
            settle(send.at[0, half, turn], first[half][turn].at[pl.ds(0, LINE - 1)])
            settle(send.at[3, half, turn], sent.at[half, turn, :, pl.ds(0, LINE_MOST)])
            settle(send.at[4, half, turn], first[half][turn].at[pl.ds(0, LINE - 1)])
            settle(recv.at[4, half, turn], targets[half].at[pl.ds(0, (LINE - 1) * piece)])
            own_last(half, turn).wait()


def layer(tokens_one, tokens_two, gates_one, gates_two, routes_one, routes_two, old_place, moves, w_in, w_out):
    hidden_units, width = w_in.shape
    tokens_here = tokens_one.shape[0]
    devices = lax.axis_size("gx") * lax.axis_size("gy")
    tall = 2 * BATCHES * (2 * tokens_here // devices)
    piece = hidden_units // (3 * LINE)
    block = piece // SIDE
    dtype = w_in.dtype
    vmem = pl.BlockSpec(memory_space=pltpu.VMEM)
    hbm = pl.BlockSpec(memory_space=pl.ANY)
    most = max(LINE_MOST, PLANE_MOST)

    def each(*shape):
        return [[pltpu.VMEM(shape, dtype)] * 3] * HALVES

    return pl.pallas_call(
        layer_kernel,
        out_shape=[jax.ShapeDtypeStruct((tokens_here, width), dtype)] * 2
        + [jax.ShapeDtypeStruct((2, 128), jnp.int32)]
        + [jax.ShapeDtypeStruct((hidden_units, width), dtype)] * 2,
        in_specs=[vmem] * 8 + [hbm] * 2,
        out_specs=[vmem] * 3 + [hbm] * 2,
        scratch_shapes=[
            each(LINE, piece, width),
            pltpu.VMEM((HALVES, 3, SIDE - 1, most, block, width), dtype),
            each(SIDE, LINE_MOST, block, width),
            each(SIDE, PLANE_MOST, block, width),
            each(SIDE, LINE_MOST, block, width),
            pltpu.VMEM((devices, tall, width // 2), dtype),
            pltpu.VMEM((devices, tall, width // 2), dtype),
            pltpu.VMEM((devices, tall, width // 2), dtype),
            pltpu.VMEM((hidden_units, width), dtype),
            pltpu.VMEM((hidden_units, width), dtype),
            pltpu.VMEM((32 * tall // 2, width), dtype),
            pltpu.VMEM((32 * tall // 2, width), jnp.float32),
            pltpu.VMEM((BATCHES, tokens_here, width), jnp.float32),
            pltpu.VMEM((16, 128), jnp.int32),
            pltpu.SMEM((16, 128), jnp.int32),
            pltpu.SemaphoreType.DMA((2, HALVES, 3)),
            pltpu.SemaphoreType.DMA((5, HALVES, 3)),
            pltpu.SemaphoreType.DMA((5, HALVES, 3)),
            pltpu.SemaphoreType.DMA((2,)),
            pltpu.SemaphoreType.DMA((2,)),
            pltpu.SemaphoreType.DMA((3,)),
        ],
        compiler_params=pltpu.CompilerParams(
            collective_id=1, has_side_effects=True, vmem_limit_bytes=60 * 1024 * 1024
        ),
        cost_estimate=pl.CostEstimate(
            flops=8 * tokens_here * hidden_units * width, bytes_accessed=400_000_000, transcendentals=0
        ),
    )(
        tokens_one,
        tokens_two,
        gates_one.reshape(1, tokens_here),
        gates_two.reshape(1, tokens_here),
        routes_one.reshape(1, tokens_here),
        routes_two.reshape(1, tokens_here),
        old_place.reshape(1, -1),
        moves.T,
        w_in,
        w_out,
    )


def keep_kernel(flags, came_in, came_out, mixed_one, mixed_two, own_in, own_out, *rest):
    *outs, through, mixed, load_sems, store_sems = rest
    parts = load_sems.shape[1]
    count = through.shape[2]
    stores = []

    def load(source, half, part):
        cut = pl.ds(part * count, count)
        return pltpu.make_async_copy(source.at[cut], through.at[half, part], load_sems.at[half, part])

    def load_all(sources):
        for part in range(parts):
            for half, source in enumerate(sources):
                load(source, half, part).start()

    @pl.when(flags[1, 0] != 0)
    def _():
        load_all((came_in, came_out))

    @pl.when(flags[1, 0] == 0)
    def _():
        load_all((own_in.at[0], own_out.at[0]))

    mixes = [
        pltpu.make_async_copy(source, mixed.at[batch], load_sems.at[HALVES, batch])
        for batch, source in enumerate((mixed_one, mixed_two))
    ]
    for copy in mixes:
        copy.start()
    for part in range(parts):
        for half in range(HALVES):
            load(came_in, half, part).wait()
            cut = pl.ds(part * count, count)
            stores.append(
                pltpu.make_async_copy(through.at[half, part], outs[2 + half].at[0, cut], store_sems.at[half, part])
            )
            stores[-1].start()
    for batch, copy in enumerate(mixes):
        copy.wait()
        stores.append(pltpu.make_async_copy(mixed.at[batch], outs[batch], store_sems.at[HALVES, batch]))
        stores[-1].start()
    for copy in stores:
        copy.wait()


def keep(flags, came_in, came_out, mixed_one, mixed_two, own_in, own_out):
    hbm = pl.BlockSpec(memory_space=pl.ANY)
    parts = 6
    hidden_units, width = came_in.shape
    like = [jax.ShapeDtypeStruct(x.shape, x.dtype) for x in (mixed_one, mixed_two, own_in, own_out)]
    return pl.pallas_call(
        keep_kernel,
        out_shape=like,
        in_specs=[pl.BlockSpec(memory_space=pltpu.SMEM)] + [hbm] * 6,
        out_specs=[hbm] * 4,
        scratch_shapes=[
            pltpu.VMEM((HALVES, parts, hidden_units // parts, width), came_in.dtype),
            pltpu.VMEM((BATCHES, *mixed_one.shape), mixed_one.dtype),
            pltpu.SemaphoreType.DMA((HALVES + 1, parts)),
            pltpu.SemaphoreType.DMA((HALVES + 1, parts)),
        ],
        compiler_params=pltpu.CompilerParams(vmem_limit_bytes=56 * 1024 * 1024),
    )(flags, came_in, came_out, mixed_one, mixed_two, own_in, own_out)


def relocate_everywhere(expert_in, expert_out, move_slots, myself):
    hidden_units, width = expert_in.shape
    device_count = lax.axis_size("gx") * lax.axis_size("gy")
    sources, targets = move_slots[:, 0], move_slots[:, 1]
    devices = jnp.arange(device_count, dtype=jnp.int32)
    anchor = jnp.sum(jnp.where(targets[None, :] == devices[:, None], sources[None, :], 0), axis=1)
    shape = (device_count, hidden_units // device_count, width)
    results = []
    for weights in (expert_in, expert_out):
        held = lax.all_to_all(weights.reshape(shape), ("gx", "gy"), split_axis=0, concat_axis=0, tiled=True)
        forward = jnp.take(held, anchor, axis=0)
        back = lax.all_to_all(forward, ("gx", "gy"), split_axis=0, concat_axis=0, tiled=True)
        results.append(back.reshape(hidden_units, width))
    return results


def shards(
    tokens_one,
    gates_one,
    routes_one,
    old_place,
    move_slots,
    tokens_two,
    gates_two,
    routes_two,
    expert_in,
    expert_out,
):
    myself = lax.axis_index(("gx", "gy")).astype(jnp.int32)
    weights_in, weights_out = expert_in[0], expert_out[0]
    mixed_one, mixed_two, flags, came_in, came_out = layer(
        tokens_one,
        tokens_two,
        gates_one,
        gates_two,
        routes_one,
        routes_two,
        old_place,
        move_slots,
        weights_in,
        weights_out,
    )
    came_in, came_out = lax.cond(
        flags[0, 0] == 0,
        lambda: (came_in, came_out),
        lambda: tuple(relocate_everywhere(weights_in, weights_out, move_slots, myself)),
    )
    return tuple(keep(flags, came_in, came_out, mixed_one, mixed_two, expert_in, expert_out))


def solution(mesh):
    return jax.shard_map(
        shards,
        mesh=mesh,
        in_specs=(
            P(("gx", "gy"), None),
            P(("gx", "gy")),
            P(("gx", "gy"), None),
            P(),
            P(),
            P(("gx", "gy"), None),
            P(("gx", "gy")),
            P(("gx", "gy"), None),
            P(("gx", "gy"), None, None),
            P(("gx", "gy"), None, None),
        ),
        out_specs=(
            P(("gx", "gy"), None),
            P(("gx", "gy"), None),
            P(("gx", "gy"), None, None),
            P(("gx", "gy"), None, None),
        ),
        check_vma=False,
    )
```

```python
import functools

import jax
import jax.numpy as jnp
from jax import lax
from jax.experimental import pallas as pl
from jax.experimental.pallas import tpu as pltpu
from jax.sharding import PartitionSpec as P

MESH = pl.DeviceIdType.MESH
SIDE = 4
CORES = 2
LINE = SIDE * CORES
TURNS = ((0, 1, 2), (1, 2, 0), (2, 0, 1))
LIMITS = ((4, 4, 8), (5, 5, 8), (6, 6, 8))
HALVES = 2
BATCHES = 2


def coordinates(device):
    return ((device // CORES) % SIDE, (device // LINE) % SIDE, device // (LINE * SIDE)), device % CORES


def mesh_id(place, core):
    x, y, z = place
    return (z * SIDE + y, x * CORES + core)


def iota(shape, axis):
    return lax.broadcasted_iota(jnp.int32, shape, axis)


def as_row(column):
    count = column.shape[0]
    return jnp.sum(jnp.where(iota((count, count), 0) == iota((count, count), 1), column, 0), axis=0, keepdims=True)


def as_column(row):
    count = row.shape[1]
    return jnp.sum(jnp.where(iota((count, count), 0) == iota((count, count), 1), row, 0), axis=1, keepdims=True)


def rank_in(group):
    count = group.shape[0]
    same = (group == as_row(group)) & (iota((count, count), 1) < iota((count, count), 0))
    return jnp.sum(jnp.where(same, 1, 0), axis=1, keepdims=True)


def split_rows(blocks):
    count, tall, half = blocks.shape
    wide = blocks.astype(jnp.float32)
    left = wide[:, : tall // 2].reshape(count * tall // 2, half)
    right = wide[:, tall // 2 :].reshape(count * tall // 2, half)
    return jnp.concatenate([left, right], axis=1)


def join_rows(rows, tall):
    count, width = rows.shape[0] // (tall // 2), rows.shape[1]
    left = rows[:, : width // 2].reshape(count, tall // 2, width // 2)
    right = rows[:, width // 2 :].reshape(count, tall // 2, width // 2)
    return jnp.concatenate([left, right], axis=1)


def layer_kernel(
    limits,
    tokens_one, tokens_two, gates_one, gates_two, routes_one, routes_two, old_place, moves, w_in, w_out,
    mixed_one, mixed_two, flags, new_in, new_out,
    first, sent, spread, crossed, landed, outbox, mailbox, returned, held_in, held_out, feed, total, mixing,
    plan, table, local, send, recv, token_send, token_recv, loads, hello,
):
    gx, gy = lax.axis_index("gx"), lax.axis_index("gy")
    at, core = (gy // CORES, gx % SIDE, gx // SIDE), gy % CORES
    line_most, plane_most, own_most = limits
    devices = outbox.shape[0]
    tall = outbox.shape[1]
    capacity = tall // 2
    myself = gx * LINE + gy
    piece = first[0][0].shape[1]
    block = spread[0][0].shape[2]
    third = piece * LINE
    sources, targets = (w_in, w_out), (new_in, new_out)
    others = [(step, flip) for step in range(SIDE) for flip in range(CORES) if (step, flip) != (0, 0)]

    def beside(axis, step, flip=0):
        place = list(at)
        place[axis] = (place[axis] + step) % SIDE
        return place, (core + flip) % CORES

    def flat_id(device):
        return (device // LINE, device % LINE)

    barrier = pltpu.get_barrier_semaphore()
    peers = [beside(0, 0, 1)] + [
        beside(axis, step, flip) for axis in range(3) for step in range(1, SIDE) for flip in range(CORES)
    ]
    for place, which in peers:
        pl.semaphore_signal(barrier, inc=1, device_id=mesh_id(place, which), device_id_type=MESH)
    pl.semaphore_wait(barrier, len(peers))

    def meet_all():
        for axis in (1, 2):
            for step in range(1, SIDE):
                place, which = beside(axis, step)
                pl.semaphore_signal(hello.at[axis - 1], inc=1, device_id=mesh_id(place, which), device_id_type=MESH)
            pl.semaphore_wait(hello.at[axis - 1], SIDE - 1)

    def ship(src, dst, stage, half, turn, place, which):
        pltpu.make_async_remote_copy(
            src_ref=src,
            dst_ref=dst,
            send_sem=send.at[stage, half, turn],
            recv_sem=recv.at[stage, half, turn],
            device_id=mesh_id(place, which),
            device_id_type=MESH,
        ).start()

    def settle(semaphore, ref):
        pltpu.make_async_copy(ref, ref, semaphore).wait()

    def rows(turn, index):
        return pl.ds(pl.multiple_of(turn * third + index * piece, piece), piece)

    def spot(turn):
        return at[TURNS[turn][0]] * CORES + core

    def own_first(half, turn):
        me = spot(turn)
        return pltpu.make_async_copy(
            sources[half].at[rows(turn, me)], first[half][turn].at[me], local.at[0, half, turn]
        )

    def own_last(half, turn):
        me = spot(turn)
        return pltpu.make_async_copy(
            first[half][turn].at[me], targets[half].at[rows(turn, me)], local.at[1, half, turn]
        )

    def stage_one(half):
        for turn in range(3):
            me = spot(turn)
            for step, flip in others:
                place, which = beside(TURNS[turn][0], step, flip)
                index = place[TURNS[turn][0]] * CORES + which
                ship(
                    sources[half].at[rows(turn, index)], first[half][turn].at[me], 0, half, turn, place, which
                )
            own_first(half, turn).start()

    def stage_two(half):
        for turn in range(3):
            b = TURNS[turn][1]
            own_first(half, turn).wait()
            settle(recv.at[0, half, turn], first[half][turn].at[pl.ds(0, LINE - 1)])
            for step in (1, 2, 3, 0):
                place, which = beside(b, step)
                cut = pl.ds(pl.multiple_of(place[b] * block, block), block)

                def take(k, carry):
                    data = first[half][turn][table[4 * turn, k], cut, :]
                    if step == 0:
                        spread[half][turn][at[b], k] = data
                    else:
                        sent[half, turn, step - 1, k] = data
                    return carry

                lax.fori_loop(0, line_most, take, 0)
                if step:
                    ship(sent.at[half, turn, step - 1, pl.ds(0, line_most)], spread[half][turn].at[at[b]], 1, half, turn, place, which)

    def stage_three(half):
        for turn in range(3):
            c = TURNS[turn][2]
            settle(recv.at[1, half, turn], spread[half][turn].at[pl.ds(0, SIDE - 1)])
            settle(send.at[1, half, turn], sent.at[half, turn, :, pl.ds(0, line_most)])
            for step in (1, 2, 3, 0):
                place, which = beside(c, step)

                def take(k, carry):
                    index = table[4 * turn + 1, place[c] * own_most + k]
                    data = spread[half][turn][index // line_most, index % line_most]
                    if step == 0:
                        crossed[half][turn][at[c], k] = data
                    else:
                        sent[half, turn, step - 1, k] = data
                    return carry

                lax.fori_loop(0, plane_most if step else own_most, take, 0)
                if step:
                    ship(sent.at[half, turn, step - 1, pl.ds(0, plane_most)], crossed[half][turn].at[at[c], pl.ds(0, plane_most)], 2, half, turn, place, which)

    def stage_four(half):
        for turn in range(3):
            b = TURNS[turn][1]
            settle(recv.at[2, half, turn], crossed[half][turn].at[pl.ds(0, SIDE - 1), pl.ds(0, plane_most)])
            settle(send.at[2, half, turn], sent.at[half, turn, :, pl.ds(0, plane_most)])
            for step in (1, 2, 3, 0):
                place, which = beside(b, step)

                def take(k, carry):
                    index = table[4 * turn + 2, place[b] * line_most + k]
                    data = crossed[half][turn][index // own_most, index % own_most]
                    if step == 0:
                        landed[half][turn][at[b], k] = data
                    else:
                        sent[half, turn, step - 1, k] = data
                    return carry

                lax.fori_loop(0, line_most, take, 0)
                if step:
                    ship(sent.at[half, turn, step - 1, pl.ds(0, line_most)], landed[half][turn].at[at[b]], 3, half, turn, place, which)

    def stage_five(half):
        for turn in range(3):
            me = spot(turn)
            settle(recv.at[3, half, turn], landed[half][turn].at[pl.ds(0, SIDE - 1)])
            for step, flip in others + [(0, 0)]:
                place, which = beside(TURNS[turn][0], step, flip)
                index = place[TURNS[turn][0]] * CORES + which
                chosen = table[4 * turn + 3, index]

                def take(quarter, carry):
                    first[half][turn][index, pl.ds(pl.multiple_of(quarter * block, block), block), :] = landed[half][turn][
                        quarter, chosen
                    ]
                    return carry

                lax.fori_loop(0, SIDE, take, 0)
                if (step, flip) != (0, 0):
                    ship(
                        first[half][turn].at[index], targets[half].at[rows(turn, me)], 4, half, turn, place, which
                    )
            own_last(half, turn).start()

    def make_plan():
        source, target = as_column(moves[0:1, :]), as_column(moves[1:2, :])
        count = source.shape[0]
        s_at, s_core = coordinates(source)
        t_at, t_core = coordinates(target)
        wide = (count, plan.shape[1])
        entry = iota(wide, 1)
        plan[...] = jnp.zeros(plan.shape, jnp.int32)
        for turn, (a, b, c) in enumerate(TURNS):
            s_line, t_line = s_at[b] * SIDE + s_at[c], t_at[b] * SIDE + t_at[c]
            rank_s, rank_t, rank_p = rank_in(s_line), rank_in(t_line), rank_in(s_at[c] * SIDE + t_at[c])
            rank_s, rank_t = jnp.minimum(rank_s, line_most - 1), jnp.minimum(rank_t, line_most - 1)
            rank_p = jnp.minimum(rank_p, own_most - 1)
            here = at[b] * SIDE + at[c]
            for row, (mine, slot, value, largest) in enumerate(
                (
                    (s_line == here, rank_s, s_at[a] * CORES + s_core, LINE - 1),
                    (
                        s_at[c] == at[c],
                        t_at[c] * own_most + rank_p,
                        s_at[b] * line_most + rank_s,
                        SIDE * line_most - 1,
                    ),
                    (
                        t_at[c] == at[c],
                        t_at[b] * line_most + rank_t,
                        s_at[c] * own_most + rank_p,
                        SIDE * own_most - 1,
                    ),
                    (t_line == here, t_at[a] * CORES + t_core, rank_t, line_most - 1),
                )
            ):
                key = jnp.where(mine, slot, -1)
                found = jnp.sum(jnp.where(key == entry, value, 0), axis=0, keepdims=True)
                index = 4 * turn + row
                plan[index : index + 1, :] = jnp.minimum(found, largest)
        arriving = jnp.max(jnp.where(target == myself, 1, 0), axis=0, keepdims=True)
        flags[...] = jnp.broadcast_to(arriving, flags.shape)
        copy = pltpu.make_async_copy(plan, table, loads.at[2])
        copy.start()
        copy.wait()

    def positions():
        routes = as_column(routes_one[...])
        slot_one = jnp.sum(
            jnp.where(routes == iota((routes.shape[0], old_place.shape[1]), 1), old_place[...], 0),
            axis=1,
            keepdims=True,
        )
        goal = as_column(routes_two[...])
        source, target = moves[0:1, :], moves[1:2, :]
        slot_two = goal + jnp.sum(jnp.where(goal == target, source - goal, 0), axis=1, keepdims=True)
        place_one = slot_one * capacity + rank_in(slot_one)
        place_two = slot_two * capacity + capacity // BATCHES + rank_in(slot_two)
        return place_one, place_two

    def one_hot(mask):
        return jnp.where(mask, 1.0, 0.0).astype(jnp.bfloat16)

    def fill_outbox(place_one, place_two):
        row_one, row_two = as_row(place_one), as_row(place_two)
        group = 16
        count = group * capacity

        def fill(index, carry):
            rows_here = iota((count, row_one.shape[1]), 0) + index * count
            picked = jnp.dot(one_hot(rows_here == row_one), tokens_one[...], preferred_element_type=jnp.float32)
            picked += jnp.dot(one_hot(rows_here == row_two), tokens_two[...], preferred_element_type=jnp.float32)
            outbox[pl.ds(index * group, group)] = join_rows(picked, tall).astype(jnp.bfloat16)
            return carry

        lax.fori_loop(0, devices // group, fill, 0)

    def post(src, dst, way, peer):
        pltpu.make_async_remote_copy(
            src_ref=src,
            dst_ref=dst,
            send_sem=token_send.at[way],
            recv_sem=token_recv.at[way],
            device_id=flat_id(peer),
            device_id_type=MESH,
        ).start()

    def send_tokens():
        def go(step, carry):
            peer = (myself + step) % devices
            post(outbox.at[peer], mailbox.at[myself], 0, peer)
            return carry

        lax.fori_loop(1, devices, go, 0)
        mailbox[myself] = outbox[myself]

    group = 32
    tile = 512

    def experts(index):
        begin = index * group
        feed[...] = split_rows(mailbox[pl.ds(begin, group)]).astype(jnp.bfloat16)
        total[...] = jnp.zeros(total.shape, jnp.float32)

        def part(step, carry):
            cut = pl.ds(pl.multiple_of(step * tile, tile), tile)
            hidden = lax.dot_general(
                feed[...], held_in[cut, :], (((1,), (1,)), ((), ())), preferred_element_type=jnp.float32
            )
            hidden = jnp.maximum(hidden, 0.0).astype(jnp.bfloat16)
            total[...] += jnp.dot(hidden, held_out[cut, :], preferred_element_type=jnp.float32)
            return carry

        lax.fori_loop(0, held_in.shape[0] // tile, part, 0)
        mailbox[pl.ds(begin, group)] = join_rows(total[...], tall).astype(jnp.bfloat16)

        def back(peer, carry):
            @pl.when(peer != myself)
            def _():
                post(mailbox.at[peer], returned.at[myself], 1, peer)

            return carry

        lax.fori_loop(begin, begin + group, back, 0)

    def collect(place_one, place_two):
        count = group * capacity
        mixing[...] = jnp.zeros(mixing.shape, jnp.float32)
        tokens_here = place_one.shape[0]

        def add(index, carry):
            results = split_rows(returned[pl.ds(index * group, group)]).astype(jnp.bfloat16)
            columns = iota((tokens_here, count), 1) + index * count
            for batch, place in enumerate((place_one, place_two)):
                mixing[batch] += jnp.dot(one_hot(columns == place), results, preferred_element_type=jnp.float32)
            return carry

        lax.fori_loop(0, devices // group, add, 0)
        mixed_one[...] = (as_column(gates_one[...]) * mixing[0]).astype(jnp.bfloat16)
        mixed_two[...] = (as_column(gates_two[...]) * mixing[1]).astype(jnp.bfloat16)

    load_in = pltpu.make_async_copy(w_in, held_in, loads.at[0])
    load_out = pltpu.make_async_copy(w_out, held_out, loads.at[1])

    stage_one(0)
    meet_all()
    place_one, place_two = positions()
    fill_outbox(place_one, place_two)
    send_tokens()
    stage_one(1)
    load_in.start()
    load_out.start()
    make_plan()
    stage_two(0)
    stage_two(1)
    stage_three(0)
    load_in.wait()
    load_out.wait()
    settle(token_recv.at[0], mailbox.at[pl.ds(0, devices - 1)])
    experts(0)
    experts(1)
    stage_three(1)
    experts(2)
    experts(3)
    returned[myself] = mailbox[myself]
    stage_four(0)
    stage_four(1)
    stage_five(0)
    stage_five(1)
    settle(token_recv.at[1], returned.at[pl.ds(0, devices - 1)])
    collect(place_one, place_two)
    settle(token_send.at[0], outbox.at[pl.ds(0, devices - 1)])
    settle(token_send.at[1], mailbox.at[pl.ds(0, devices - 1)])

    for half in range(HALVES):
        for turn in range(3):
            settle(send.at[0, half, turn], first[half][turn].at[pl.ds(0, LINE - 1)])
            settle(send.at[3, half, turn], sent.at[half, turn, :, pl.ds(0, line_most)])
            settle(send.at[4, half, turn], first[half][turn].at[pl.ds(0, LINE - 1)])
            settle(recv.at[4, half, turn], targets[half].at[pl.ds(0, (LINE - 1) * piece)])
            own_last(half, turn).wait()


def layer(which, tokens_one, tokens_two, gates_one, gates_two, routes_one, routes_two, old_place, moves, w_in, w_out):
    line_most, plane_most, own_most = LIMITS[which]
    hidden_units, width = w_in.shape
    tokens_here = tokens_one.shape[0]
    devices = lax.axis_size("gx") * lax.axis_size("gy")
    tall = 2 * BATCHES * (2 * tokens_here // devices)
    piece = hidden_units // (3 * LINE)
    block = piece // SIDE
    dtype = w_in.dtype
    vmem = pl.BlockSpec(memory_space=pltpu.VMEM)
    hbm = pl.BlockSpec(memory_space=pl.ANY)
    most = max(line_most, plane_most)

    def each(*shape):
        return [[pltpu.VMEM(shape, dtype)] * 3] * HALVES

    return pl.pallas_call(
        functools.partial(layer_kernel, LIMITS[which]),
        out_shape=[jax.ShapeDtypeStruct((tokens_here, width), dtype)] * 2
        + [jax.ShapeDtypeStruct((1, 128), jnp.int32)]
        + [jax.ShapeDtypeStruct((hidden_units, width), dtype)] * 2,
        in_specs=[vmem] * 8 + [hbm] * 2,
        out_specs=[vmem] * 3 + [hbm] * 2,
        scratch_shapes=[
            each(LINE, piece, width),
            pltpu.VMEM((HALVES, 3, SIDE - 1, most, block, width), dtype),
            each(SIDE, line_most, block, width),
            each(SIDE, own_most, block, width),
            each(SIDE, line_most, block, width),
            pltpu.VMEM((devices, tall, width // 2), dtype),
            pltpu.VMEM((devices, tall, width // 2), dtype),
            pltpu.VMEM((devices, tall, width // 2), dtype),
            pltpu.VMEM((hidden_units, width), dtype),
            pltpu.VMEM((hidden_units, width), dtype),
            pltpu.VMEM((32 * tall // 2, width), dtype),
            pltpu.VMEM((32 * tall // 2, width), jnp.float32),
            pltpu.VMEM((BATCHES, tokens_here, width), jnp.float32),
            pltpu.VMEM((16, 128), jnp.int32),
            pltpu.SMEM((16, 128), jnp.int32),
            pltpu.SemaphoreType.DMA((2, HALVES, 3)),
            pltpu.SemaphoreType.DMA((5, HALVES, 3)),
            pltpu.SemaphoreType.DMA((5, HALVES, 3)),
            pltpu.SemaphoreType.DMA((2,)),
            pltpu.SemaphoreType.DMA((2,)),
            pltpu.SemaphoreType.DMA((3,)),
            pltpu.SemaphoreType.REGULAR((2,)),
        ],
        compiler_params=pltpu.CompilerParams(
            collective_id=1 + which, has_side_effects=True, vmem_limit_bytes=60 * 1024 * 1024
        ),
        cost_estimate=pl.CostEstimate(
            flops=8 * tokens_here * hidden_units * width, bytes_accessed=400_000_000, transcendentals=0
        ),
    )(
        tokens_one,
        tokens_two,
        gates_one.reshape(1, tokens_here),
        gates_two.reshape(1, tokens_here),
        routes_one.reshape(1, tokens_here),
        routes_two.reshape(1, tokens_here),
        old_place.reshape(1, -1),
        moves.T,
        w_in,
        w_out,
    )


def keep_kernel(flags, came_in, came_out, mixed_one, mixed_two, own_in, own_out, *rest):
    *outs, through, mixed, load_sems, store_sems = rest
    parts = load_sems.shape[1]
    count = through.shape[2]
    stores = []

    def load(source, half, part):
        cut = pl.ds(part * count, count)
        return pltpu.make_async_copy(source.at[cut], through.at[half, part], load_sems.at[half, part])

    def load_all(sources):
        for part in range(parts):
            for half, source in enumerate(sources):
                load(source, half, part).start()

    @pl.when(flags[0, 0] != 0)
    def _():
        load_all((came_in, came_out))

    @pl.when(flags[0, 0] == 0)
    def _():
        load_all((own_in.at[0], own_out.at[0]))

    mixes = [
        pltpu.make_async_copy(source, mixed.at[batch], load_sems.at[HALVES, batch])
        for batch, source in enumerate((mixed_one, mixed_two))
    ]
    for copy in mixes:
        copy.start()
    for part in range(parts):
        for half in range(HALVES):
            load(came_in, half, part).wait()
            cut = pl.ds(part * count, count)
            stores.append(
                pltpu.make_async_copy(through.at[half, part], outs[2 + half].at[0, cut], store_sems.at[half, part])
            )
            stores[-1].start()
    for batch, copy in enumerate(mixes):
        copy.wait()
        stores.append(pltpu.make_async_copy(mixed.at[batch], outs[batch], store_sems.at[HALVES, batch]))
        stores[-1].start()
    for copy in stores:
        copy.wait()


def keep(flags, came_in, came_out, mixed_one, mixed_two, own_in, own_out):
    hbm = pl.BlockSpec(memory_space=pl.ANY)
    parts = 6
    hidden_units, width = came_in.shape
    like = [jax.ShapeDtypeStruct(x.shape, x.dtype) for x in (mixed_one, mixed_two, own_in, own_out)]
    return pl.pallas_call(
        keep_kernel,
        out_shape=like,
        in_specs=[pl.BlockSpec(memory_space=pltpu.SMEM)] + [hbm] * 6,
        out_specs=[hbm] * 4,
        scratch_shapes=[
            pltpu.VMEM((HALVES, parts, hidden_units // parts, width), came_in.dtype),
            pltpu.VMEM((BATCHES, *mixed_one.shape), mixed_one.dtype),
            pltpu.SemaphoreType.DMA((HALVES + 1, parts)),
            pltpu.SemaphoreType.DMA((HALVES + 1, parts)),
        ],
        compiler_params=pltpu.CompilerParams(vmem_limit_bytes=56 * 1024 * 1024),
    )(flags, came_in, came_out, mixed_one, mixed_two, own_in, own_out)


def limits_needed(move_slots):
    (sx, sy, sz), _ = coordinates(move_slots[:, 0])
    (tx, ty, tz), _ = coordinates(move_slots[:, 1])

    def same(value):
        return value[:, None] == value[None, :]

    def counts(*masks):
        fields = sum(jnp.where(mask, 1 << (5 * i), 0) for i, mask in enumerate(masks))
        total = jnp.sum(fields, axis=1, dtype=jnp.int32)
        return [(total >> (5 * i)) & 31 for i in range(len(masks))]

    ex, ey, ez, fx, fy, fz = (same(value) for value in (sx, sy, sz, tx, ty, tz))
    lines = counts(ey & ez, ez & ex, ex & ey, fy & fz, fz & fx, fx & fy)
    planes = counts(ez & fz, ex & fx, ey & fy)
    level = 0
    for line_most, plane_most, own_most in LIMITS:
        over = functools.reduce(jnp.logical_or, [count > line_most for count in lines])
        for count, start, end in zip(planes, (sz, sx, sy), (tz, tx, ty)):
            over |= count > jnp.where(start == end, own_most, plane_most)
        level += over.astype(jnp.int32)
    return jnp.max(level)


def relocate_everywhere(expert_in, expert_out, move_slots, myself):
    hidden_units, width = expert_in.shape
    device_count = lax.axis_size("gx") * lax.axis_size("gy")
    sources, targets = move_slots[:, 0], move_slots[:, 1]
    devices = jnp.arange(device_count, dtype=jnp.int32)
    anchor = jnp.sum(jnp.where(targets[None, :] == devices[:, None], sources[None, :], 0), axis=1)
    shape = (device_count, hidden_units // device_count, width)
    results = []
    for weights in (expert_in, expert_out):
        held = lax.all_to_all(weights.reshape(shape), ("gx", "gy"), split_axis=0, concat_axis=0, tiled=True)
        forward = jnp.take(held, anchor, axis=0)
        back = lax.all_to_all(forward, ("gx", "gy"), split_axis=0, concat_axis=0, tiled=True)
        results.append(back.reshape(hidden_units, width))
    return results


def shards(
    tokens_one,
    gates_one,
    routes_one,
    old_place,
    move_slots,
    tokens_two,
    gates_two,
    routes_two,
    expert_in,
    expert_out,
):
    myself = lax.axis_index(("gx", "gy")).astype(jnp.int32)
    weights_in, weights_out = expert_in[0], expert_out[0]
    operands = (
        tokens_one,
        tokens_two,
        gates_one,
        gates_two,
        routes_one,
        routes_two,
        old_place,
        move_slots,
        weights_in,
        weights_out,
    )

    def beyond():
        mixed_one, mixed_two, flags, *_ = layer(0, *operands)
        return (mixed_one, mixed_two, flags, *relocate_everywhere(weights_in, weights_out, move_slots, myself))

    mixed_one, mixed_two, flags, came_in, came_out = lax.switch(
        limits_needed(move_slots),
        [lambda which=which: tuple(layer(which, *operands)) for which in range(len(LIMITS))] + [beyond],
    )
    return tuple(keep(flags, came_in, came_out, mixed_one, mixed_two, expert_in, expert_out))


def solution(mesh):
    return jax.shard_map(
        shards,
        mesh=mesh,
        in_specs=(
            P(("gx", "gy"), None),
            P(("gx", "gy")),
            P(("gx", "gy"), None),
            P(),
            P(),
            P(("gx", "gy"), None),
            P(("gx", "gy")),
            P(("gx", "gy"), None),
            P(("gx", "gy"), None, None),
            P(("gx", "gy"), None, None),
        ),
        out_specs=(
            P(("gx", "gy"), None),
            P(("gx", "gy"), None),
            P(("gx", "gy"), None, None),
            P(("gx", "gy"), None, None),
        ),
        check_vma=False,
    )
```

```python
import functools

import jax
import jax.numpy as jnp
from jax import lax
from jax.experimental import pallas as pl
from jax.experimental.pallas import tpu as pltpu
from jax.sharding import PartitionSpec as P

MESH = pl.DeviceIdType.MESH
SIDE = 4
CORES = 2
LINE = SIDE * CORES
TURNS = ((0, 1, 2), (1, 2, 0), (2, 0, 1))
LIMITS = ((4, 4, 8), (5, 5, 8), (6, 6, 8))
HALVES = 2
BATCHES = 2


def coordinates(device):
    return ((device // CORES) % SIDE, (device // LINE) % SIDE, device // (LINE * SIDE)), device % CORES


def mesh_id(place, core):
    x, y, z = place
    return (z * SIDE + y, x * CORES + core)


def iota(shape, axis):
    return lax.broadcasted_iota(jnp.int32, shape, axis)


def as_row(column):
    count = column.shape[0]
    return jnp.sum(jnp.where(iota((count, count), 0) == iota((count, count), 1), column, 0), axis=0, keepdims=True)


def as_column(row):
    count = row.shape[1]
    return jnp.sum(jnp.where(iota((count, count), 0) == iota((count, count), 1), row, 0), axis=1, keepdims=True)


def rank_in(group):
    count = group.shape[0]
    same = (group == as_row(group)) & (iota((count, count), 1) < iota((count, count), 0))
    return jnp.sum(jnp.where(same, 1, 0), axis=1, keepdims=True)


def split_rows(blocks):
    count, tall, half = blocks.shape
    wide = blocks.astype(jnp.float32)
    left = wide[:, : tall // 2].reshape(count * tall // 2, half)
    right = wide[:, tall // 2 :].reshape(count * tall // 2, half)
    return jnp.concatenate([left, right], axis=1)


def join_rows(rows, tall):
    count, width = rows.shape[0] // (tall // 2), rows.shape[1]
    left = rows[:, : width // 2].reshape(count, tall // 2, width // 2)
    right = rows[:, width // 2 :].reshape(count, tall // 2, width // 2)
    return jnp.concatenate([left, right], axis=1)


def layer_kernel(
    limits,
    tokens_one, tokens_two, gates_one, gates_two, routes_one, routes_two, old_place, moves, w_in, w_out,
    mixed_one, mixed_two, flags, new_in, new_out,
    first, sent, spread, crossed, landed, outbox, mailbox, returned, held_in, held_out, feed, total, mixing,
    plan, table, local, send, recv, token_send, token_recv, loads, hello,
):
    gx, gy = lax.axis_index("gx"), lax.axis_index("gy")
    at, core = (gy // CORES, gx % SIDE, gx // SIDE), gy % CORES
    line_most, plane_most, own_most = limits
    devices = outbox.shape[0]
    tall = outbox.shape[1]
    capacity = tall // 2
    myself = gx * LINE + gy
    piece = first[0][0].shape[1]
    block = spread[0][0].shape[2]
    third = piece * LINE
    sources, targets = (w_in, w_out), (new_in, new_out)
    others = [(step, flip) for step in range(SIDE) for flip in range(CORES) if (step, flip) != (0, 0)]

    def beside(axis, step, flip=0):
        place = list(at)
        place[axis] = (place[axis] + step) % SIDE
        return place, (core + flip) % CORES

    def flat_id(device):
        return (device // LINE, device % LINE)

    barrier = pltpu.get_barrier_semaphore()
    peers = [beside(0, 0, 1)] + [
        beside(axis, step, flip) for axis in range(3) for step in range(1, SIDE) for flip in range(CORES)
    ]
    for place, which in peers:
        pl.semaphore_signal(barrier, inc=1, device_id=mesh_id(place, which), device_id_type=MESH)
    pl.semaphore_wait(barrier, len(peers))

    def meet_all():
        for axis in (1, 2):
            for step in range(1, SIDE):
                place, which = beside(axis, step)
                pl.semaphore_signal(hello.at[axis - 1], inc=1, device_id=mesh_id(place, which), device_id_type=MESH)
            pl.semaphore_wait(hello.at[axis - 1], SIDE - 1)

    def ship(src, dst, stage, half, turn, place, which):
        pltpu.make_async_remote_copy(
            src_ref=src,
            dst_ref=dst,
            send_sem=send.at[stage, half, turn],
            recv_sem=recv.at[stage, half, turn],
            device_id=mesh_id(place, which),
            device_id_type=MESH,
        ).start()

    def settle(semaphore, ref):
        pltpu.make_async_copy(ref, ref, semaphore).wait()

    def rows(turn, index):
        return pl.ds(pl.multiple_of(turn * third + index * piece, piece), piece)

    def spot(turn):
        return at[TURNS[turn][0]] * CORES + core

    def own_first(half, turn):
        me = spot(turn)
        return pltpu.make_async_copy(
            sources[half].at[rows(turn, me)], first[half][turn].at[me], local.at[0, half, turn]
        )

    def own_last(half, turn):
        me = spot(turn)
        return pltpu.make_async_copy(
            first[half][turn].at[me], targets[half].at[rows(turn, me)], local.at[1, half, turn]
        )

    def stage_one(half):
        for turn in range(3):
            me = spot(turn)
            for step, flip in others:
                place, which = beside(TURNS[turn][0], step, flip)
                index = place[TURNS[turn][0]] * CORES + which
                ship(
                    sources[half].at[rows(turn, index)], first[half][turn].at[me], 0, half, turn, place, which
                )
            own_first(half, turn).start()

    def stage_two(half):
        for turn in range(3):
            b = TURNS[turn][1]
            own_first(half, turn).wait()
            settle(recv.at[0, half, turn], first[half][turn].at[pl.ds(0, LINE - 1)])
            for step in (1, 2, 3, 0):
                place, which = beside(b, step)
                cut = pl.ds(pl.multiple_of(place[b] * block, block), block)

                def take(k, carry):
                    data = first[half][turn][table[4 * turn, k], cut, :]
                    if step == 0:
                        spread[half][turn][at[b], k] = data
                    else:
                        sent[half, turn, step - 1, k] = data
                    return carry

                lax.fori_loop(0, line_most, take, 0)
                if step:
                    ship(sent.at[half, turn, step - 1, pl.ds(0, line_most)], spread[half][turn].at[at[b]], 1, half, turn, place, which)

    def stage_three(half):
        for turn in range(3):
            c = TURNS[turn][2]
            settle(recv.at[1, half, turn], spread[half][turn].at[pl.ds(0, SIDE - 1)])
            settle(send.at[1, half, turn], sent.at[half, turn, :, pl.ds(0, line_most)])
            for step in (1, 2, 3, 0):
                place, which = beside(c, step)

                def take(k, carry):
                    index = table[4 * turn + 1, place[c] * own_most + k]
                    data = spread[half][turn][index // line_most, index % line_most]
                    if step == 0:
                        crossed[half][turn][at[c], k] = data
                    else:
                        sent[half, turn, step - 1, k] = data
                    return carry

                lax.fori_loop(0, plane_most if step else own_most, take, 0)
                if step:
                    ship(sent.at[half, turn, step - 1, pl.ds(0, plane_most)], crossed[half][turn].at[at[c], pl.ds(0, plane_most)], 2, half, turn, place, which)

    def stage_four(half):
        for turn in range(3):
            b = TURNS[turn][1]
            settle(recv.at[2, half, turn], crossed[half][turn].at[pl.ds(0, SIDE - 1), pl.ds(0, plane_most)])
            settle(send.at[2, half, turn], sent.at[half, turn, :, pl.ds(0, plane_most)])
            for step in (1, 2, 3, 0):
                place, which = beside(b, step)

                def take(k, carry):
                    index = table[4 * turn + 2, place[b] * line_most + k]
                    data = crossed[half][turn][index // own_most, index % own_most]
                    if step == 0:
                        landed[half][turn][at[b], k] = data
                    else:
                        sent[half, turn, step - 1, k] = data
                    return carry

                lax.fori_loop(0, line_most, take, 0)
                if step:
                    ship(sent.at[half, turn, step - 1, pl.ds(0, line_most)], landed[half][turn].at[at[b]], 3, half, turn, place, which)

    def stage_five(half):
        for turn in range(3):
            me = spot(turn)
            settle(recv.at[3, half, turn], landed[half][turn].at[pl.ds(0, SIDE - 1)])
            for step, flip in others + [(0, 0)]:
                place, which = beside(TURNS[turn][0], step, flip)
                index = place[TURNS[turn][0]] * CORES + which
                chosen = table[4 * turn + 3, index]

                def take(quarter, carry):
                    first[half][turn][index, pl.ds(pl.multiple_of(quarter * block, block), block), :] = landed[half][turn][
                        quarter, chosen
                    ]
                    return carry

                lax.fori_loop(0, SIDE, take, 0)
                if (step, flip) != (0, 0):
                    ship(
                        first[half][turn].at[index], targets[half].at[rows(turn, me)], 4, half, turn, place, which
                    )
            own_last(half, turn).start()

    def make_plan():
        source, target = as_column(moves[0:1, :]), as_column(moves[1:2, :])
        count = source.shape[0]
        s_at, s_core = coordinates(source)
        t_at, t_core = coordinates(target)
        wide = (count, plan.shape[1])
        entry = iota(wide, 1)
        plan[...] = jnp.zeros(plan.shape, jnp.int32)
        for turn, (a, b, c) in enumerate(TURNS):
            s_line, t_line = s_at[b] * SIDE + s_at[c], t_at[b] * SIDE + t_at[c]
            rank_s, rank_t, rank_p = rank_in(s_line), rank_in(t_line), rank_in(s_at[c] * SIDE + t_at[c])
            rank_s, rank_t = jnp.minimum(rank_s, line_most - 1), jnp.minimum(rank_t, line_most - 1)
            rank_p = jnp.minimum(rank_p, own_most - 1)
            here = at[b] * SIDE + at[c]
            for row, (mine, slot, value, largest) in enumerate(
                (
                    (s_line == here, rank_s, s_at[a] * CORES + s_core, LINE - 1),
                    (
                        s_at[c] == at[c],
                        t_at[c] * own_most + rank_p,
                        s_at[b] * line_most + rank_s,
                        SIDE * line_most - 1,
                    ),
                    (
                        t_at[c] == at[c],
                        t_at[b] * line_most + rank_t,
                        s_at[c] * own_most + rank_p,
                        SIDE * own_most - 1,
                    ),
                    (t_line == here, t_at[a] * CORES + t_core, rank_t, line_most - 1),
                )
            ):
                key = jnp.where(mine, slot, -1)
                found = jnp.sum(jnp.where(key == entry, value, 0), axis=0, keepdims=True)
                index = 4 * turn + row
                plan[index : index + 1, :] = jnp.minimum(found, largest)
        arriving = jnp.max(jnp.where(target == myself, 1, 0), axis=0, keepdims=True)
        flags[...] = jnp.broadcast_to(arriving, flags.shape)
        copy = pltpu.make_async_copy(plan, table, loads.at[2])
        copy.start()
        copy.wait()

    def positions():
        routes = as_column(routes_one[...])
        slot_one = jnp.sum(
            jnp.where(routes == iota((routes.shape[0], old_place.shape[1]), 1), old_place[...], 0),
            axis=1,
            keepdims=True,
        )
        goal = as_column(routes_two[...])
        source, target = moves[0:1, :], moves[1:2, :]
        slot_two = goal + jnp.sum(jnp.where(goal == target, source - goal, 0), axis=1, keepdims=True)
        place_one = slot_one * capacity + rank_in(slot_one)
        place_two = slot_two * capacity + capacity // BATCHES + rank_in(slot_two)
        return place_one, place_two

    def one_hot(mask):
        return jnp.where(mask, 1.0, 0.0).astype(jnp.bfloat16)

    def fill_outbox(place_one, place_two):
        row_one, row_two = as_row(place_one), as_row(place_two)
        group = 16
        count = group * capacity

        def fill(index, carry):
            rows_here = iota((count, row_one.shape[1]), 0) + index * count
            picked = jnp.dot(one_hot(rows_here == row_one), tokens_one[...], preferred_element_type=jnp.float32)
            picked += jnp.dot(one_hot(rows_here == row_two), tokens_two[...], preferred_element_type=jnp.float32)
            outbox[pl.ds(index * group, group)] = join_rows(picked, tall).astype(jnp.bfloat16)
            return carry

        lax.fori_loop(0, devices // group, fill, 0)

    def post(src, dst, way, peer):
        pltpu.make_async_remote_copy(
            src_ref=src,
            dst_ref=dst,
            send_sem=token_send.at[way],
            recv_sem=token_recv.at[way],
            device_id=flat_id(peer),
            device_id_type=MESH,
        ).start()

    def send_tokens():
        def go(step, carry):
            peer = (myself + step * 79) % devices
            post(outbox.at[peer], mailbox.at[my_slot], 0, peer)
            return carry

        lax.fori_loop(1, devices, go, 0)
        mailbox[my_slot] = outbox[myself]

    group = SIDE * LINE
    tile = 512
    my_sum = (at[0] + at[1] + at[2]) % SIDE
    my_slot = my_sum * group + myself % group

    def experts(index):
        quarter = (index + my_sum) % SIDE
        begin = quarter * group
        feed[...] = split_rows(mailbox[pl.ds(begin, group)]).astype(jnp.bfloat16)
        total[...] = jnp.zeros(total.shape, jnp.float32)

        def part(step, carry):
            cut = pl.ds(pl.multiple_of(step * tile, tile), tile)
            hidden = lax.dot_general(
                feed[...], held_in[cut, :], (((1,), (1,)), ((), ())), preferred_element_type=jnp.float32
            )
            hidden = jnp.maximum(hidden, 0.0).astype(jnp.bfloat16)
            total[...] += jnp.dot(hidden, held_out[cut, :], preferred_element_type=jnp.float32)
            return carry

        lax.fori_loop(0, held_in.shape[0] // tile, part, 0)
        mailbox[pl.ds(begin, group)] = join_rows(total[...], tall).astype(jnp.bfloat16)

        def back(step, carry):
            low = (myself + step * 13) % group
            z = (quarter + 2 * SIDE - (low // LINE) % SIDE - (low // CORES) % SIDE) % SIDE
            peer = z * group + low

            @pl.when(peer != myself)
            def _():
                post(mailbox.at[begin + low], returned.at[myself], 1, peer)

            return carry

        lax.fori_loop(0, group, back, 0)

    def collect(place_one, place_two):
        count = group * capacity
        mixing[...] = jnp.zeros(mixing.shape, jnp.float32)
        tokens_here = place_one.shape[0]

        def add(index, carry):
            results = split_rows(returned[pl.ds(index * group, group)]).astype(jnp.bfloat16)
            columns = iota((tokens_here, count), 1) + index * count
            for batch, place in enumerate((place_one, place_two)):
                mixing[batch] += jnp.dot(one_hot(columns == place), results, preferred_element_type=jnp.float32)
            return carry

        lax.fori_loop(0, devices // group, add, 0)
        mixed_one[...] = (as_column(gates_one[...]) * mixing[0]).astype(jnp.bfloat16)
        mixed_two[...] = (as_column(gates_two[...]) * mixing[1]).astype(jnp.bfloat16)

    load_in = pltpu.make_async_copy(w_in, held_in, loads.at[0])
    load_out = pltpu.make_async_copy(w_out, held_out, loads.at[1])

    stage_one(0)
    meet_all()
    place_one, place_two = positions()
    fill_outbox(place_one, place_two)
    send_tokens()
    stage_one(1)
    load_in.start()
    load_out.start()
    make_plan()
    stage_two(0)
    stage_two(1)
    stage_three(0)
    load_in.wait()
    load_out.wait()
    settle(token_recv.at[0], mailbox.at[pl.ds(0, devices - 1)])
    experts(0)
    experts(1)
    stage_three(1)
    experts(2)
    experts(3)
    returned[myself] = mailbox[my_slot]
    stage_four(0)
    stage_four(1)
    stage_five(0)
    stage_five(1)
    settle(token_recv.at[1], returned.at[pl.ds(0, devices - 1)])
    collect(place_one, place_two)
    settle(token_send.at[0], outbox.at[pl.ds(0, devices - 1)])
    settle(token_send.at[1], mailbox.at[pl.ds(0, devices - 1)])

    for half in range(HALVES):
        for turn in range(3):
            settle(send.at[0, half, turn], first[half][turn].at[pl.ds(0, LINE - 1)])
            settle(send.at[3, half, turn], sent.at[half, turn, :, pl.ds(0, line_most)])
            settle(send.at[4, half, turn], first[half][turn].at[pl.ds(0, LINE - 1)])
            settle(recv.at[4, half, turn], targets[half].at[pl.ds(0, (LINE - 1) * piece)])
            own_last(half, turn).wait()


def layer(which, tokens_one, tokens_two, gates_one, gates_two, routes_one, routes_two, old_place, moves, w_in, w_out):
    line_most, plane_most, own_most = LIMITS[which]
    hidden_units, width = w_in.shape
    tokens_here = tokens_one.shape[0]
    devices = lax.axis_size("gx") * lax.axis_size("gy")
    tall = 2 * BATCHES * (2 * tokens_here // devices)
    piece = hidden_units // (3 * LINE)
    block = piece // SIDE
    dtype = w_in.dtype
    vmem = pl.BlockSpec(memory_space=pltpu.VMEM)
    hbm = pl.BlockSpec(memory_space=pl.ANY)
    most = max(line_most, plane_most)

    def each(*shape):
        return [[pltpu.VMEM(shape, dtype)] * 3] * HALVES

    return pl.pallas_call(
        functools.partial(layer_kernel, LIMITS[which]),
        out_shape=[jax.ShapeDtypeStruct((tokens_here, width), dtype)] * 2
        + [jax.ShapeDtypeStruct((1, 128), jnp.int32)]
        + [jax.ShapeDtypeStruct((hidden_units, width), dtype)] * 2,
        in_specs=[vmem] * 8 + [hbm] * 2,
        out_specs=[vmem] * 3 + [hbm] * 2,
        scratch_shapes=[
            each(LINE, piece, width),
            pltpu.VMEM((HALVES, 3, SIDE - 1, most, block, width), dtype),
            each(SIDE, line_most, block, width),
            each(SIDE, own_most, block, width),
            each(SIDE, line_most, block, width),
            pltpu.VMEM((devices, tall, width // 2), dtype),
            pltpu.VMEM((devices, tall, width // 2), dtype),
            pltpu.VMEM((devices, tall, width // 2), dtype),
            pltpu.VMEM((hidden_units, width), dtype),
            pltpu.VMEM((hidden_units, width), dtype),
            pltpu.VMEM((32 * tall // 2, width), dtype),
            pltpu.VMEM((32 * tall // 2, width), jnp.float32),
            pltpu.VMEM((BATCHES, tokens_here, width), jnp.float32),
            pltpu.VMEM((16, 128), jnp.int32),
            pltpu.SMEM((16, 128), jnp.int32),
            pltpu.SemaphoreType.DMA((2, HALVES, 3)),
            pltpu.SemaphoreType.DMA((5, HALVES, 3)),
            pltpu.SemaphoreType.DMA((5, HALVES, 3)),
            pltpu.SemaphoreType.DMA((2,)),
            pltpu.SemaphoreType.DMA((2,)),
            pltpu.SemaphoreType.DMA((3,)),
            pltpu.SemaphoreType.REGULAR((2,)),
        ],
        compiler_params=pltpu.CompilerParams(
            collective_id=1 + which, has_side_effects=True, vmem_limit_bytes=60 * 1024 * 1024
        ),
        cost_estimate=pl.CostEstimate(
            flops=8 * tokens_here * hidden_units * width, bytes_accessed=400_000_000, transcendentals=0
        ),
    )(
        tokens_one,
        tokens_two,
        gates_one.reshape(1, tokens_here),
        gates_two.reshape(1, tokens_here),
        routes_one.reshape(1, tokens_here),
        routes_two.reshape(1, tokens_here),
        old_place.reshape(1, -1),
        moves.T,
        w_in,
        w_out,
    )


def keep_kernel(flags, came_in, came_out, mixed_one, mixed_two, own_in, own_out, *rest):
    *outs, through, mixed, load_sems, store_sems = rest
    parts = load_sems.shape[1]
    count = through.shape[2]
    stores = []

    def load(source, half, part):
        cut = pl.ds(part * count, count)
        return pltpu.make_async_copy(source.at[cut], through.at[half, part], load_sems.at[half, part])

    def load_all(sources):
        for part in range(parts):
            for half, source in enumerate(sources):
                load(source, half, part).start()

    @pl.when(flags[0, 0] != 0)
    def _():
        load_all((came_in, came_out))

    @pl.when(flags[0, 0] == 0)
    def _():
        load_all((own_in.at[0], own_out.at[0]))

    mixes = [
        pltpu.make_async_copy(source, mixed.at[batch], load_sems.at[HALVES, batch])
        for batch, source in enumerate((mixed_one, mixed_two))
    ]
    for copy in mixes:
        copy.start()
    for part in range(parts):
        for half in range(HALVES):
            load(came_in, half, part).wait()
            cut = pl.ds(part * count, count)
            stores.append(
                pltpu.make_async_copy(through.at[half, part], outs[2 + half].at[0, cut], store_sems.at[half, part])
            )
            stores[-1].start()
    for batch, copy in enumerate(mixes):
        copy.wait()
        stores.append(pltpu.make_async_copy(mixed.at[batch], outs[batch], store_sems.at[HALVES, batch]))
        stores[-1].start()
    for copy in stores:
        copy.wait()


def keep(flags, came_in, came_out, mixed_one, mixed_two, own_in, own_out):
    hbm = pl.BlockSpec(memory_space=pl.ANY)
    parts = 6
    hidden_units, width = came_in.shape
    like = [jax.ShapeDtypeStruct(x.shape, x.dtype) for x in (mixed_one, mixed_two, own_in, own_out)]
    return pl.pallas_call(
        keep_kernel,
        out_shape=like,
        in_specs=[pl.BlockSpec(memory_space=pltpu.SMEM)] + [hbm] * 6,
        out_specs=[hbm] * 4,
        scratch_shapes=[
            pltpu.VMEM((HALVES, parts, hidden_units // parts, width), came_in.dtype),
            pltpu.VMEM((BATCHES, *mixed_one.shape), mixed_one.dtype),
            pltpu.SemaphoreType.DMA((HALVES + 1, parts)),
            pltpu.SemaphoreType.DMA((HALVES + 1, parts)),
        ],
        compiler_params=pltpu.CompilerParams(vmem_limit_bytes=56 * 1024 * 1024),
    )(flags, came_in, came_out, mixed_one, mixed_two, own_in, own_out)


def limits_needed(move_slots):
    (sx, sy, sz), _ = coordinates(move_slots[:, 0])
    (tx, ty, tz), _ = coordinates(move_slots[:, 1])

    def same(value):
        return value[:, None] == value[None, :]

    def counts(*masks):
        fields = sum(jnp.where(mask, 1 << (5 * i), 0) for i, mask in enumerate(masks))
        total = jnp.sum(fields, axis=1, dtype=jnp.int32)
        return [(total >> (5 * i)) & 31 for i in range(len(masks))]

    ex, ey, ez, fx, fy, fz = (same(value) for value in (sx, sy, sz, tx, ty, tz))
    lines = counts(ey & ez, ez & ex, ex & ey, fy & fz, fz & fx, fx & fy)
    planes = counts(ez & fz, ex & fx, ey & fy)
    level = 0
    for line_most, plane_most, own_most in LIMITS:
        over = functools.reduce(jnp.logical_or, [count > line_most for count in lines])
        for count, start, end in zip(planes, (sz, sx, sy), (tz, tx, ty)):
            over |= count > jnp.where(start == end, own_most, plane_most)
        level += over.astype(jnp.int32)
    return jnp.max(level)


def relocate_everywhere(expert_in, expert_out, move_slots, myself):
    hidden_units, width = expert_in.shape
    device_count = lax.axis_size("gx") * lax.axis_size("gy")
    sources, targets = move_slots[:, 0], move_slots[:, 1]
    devices = jnp.arange(device_count, dtype=jnp.int32)
    anchor = jnp.sum(jnp.where(targets[None, :] == devices[:, None], sources[None, :], 0), axis=1)
    shape = (device_count, hidden_units // device_count, width)
    results = []
    for weights in (expert_in, expert_out):
        held = lax.all_to_all(weights.reshape(shape), ("gx", "gy"), split_axis=0, concat_axis=0, tiled=True)
        forward = jnp.take(held, anchor, axis=0)
        back = lax.all_to_all(forward, ("gx", "gy"), split_axis=0, concat_axis=0, tiled=True)
        results.append(back.reshape(hidden_units, width))
    return results


def shards(
    tokens_one,
    gates_one,
    routes_one,
    old_place,
    move_slots,
    tokens_two,
    gates_two,
    routes_two,
    expert_in,
    expert_out,
):
    myself = lax.axis_index(("gx", "gy")).astype(jnp.int32)
    weights_in, weights_out = expert_in[0], expert_out[0]
    operands = (
        tokens_one,
        tokens_two,
        gates_one,
        gates_two,
        routes_one,
        routes_two,
        old_place,
        move_slots,
        weights_in,
        weights_out,
    )

    def beyond():
        mixed_one, mixed_two, flags, *_ = layer(0, *operands)
        return (mixed_one, mixed_two, flags, *relocate_everywhere(weights_in, weights_out, move_slots, myself))

    mixed_one, mixed_two, flags, came_in, came_out = lax.switch(
        limits_needed(move_slots),
        [lambda which=which: tuple(layer(which, *operands)) for which in range(len(LIMITS))] + [beyond],
    )
    return tuple(keep(flags, came_in, came_out, mixed_one, mixed_two, expert_in, expert_out))


def solution(mesh):
    return jax.shard_map(
        shards,
        mesh=mesh,
        in_specs=(
            P(("gx", "gy"), None),
            P(("gx", "gy")),
            P(("gx", "gy"), None),
            P(),
            P(),
            P(("gx", "gy"), None),
            P(("gx", "gy")),
            P(("gx", "gy"), None),
            P(("gx", "gy"), None, None),
            P(("gx", "gy"), None, None),
        ),
        out_specs=(
            P(("gx", "gy"), None),
            P(("gx", "gy"), None),
            P(("gx", "gy"), None, None),
            P(("gx", "gy"), None, None),
        ),
        check_vma=False,
    )
```

```python
import functools

import jax
import jax.numpy as jnp
from jax import lax
from jax.experimental import pallas as pl
from jax.experimental.pallas import tpu as pltpu
from jax.sharding import PartitionSpec as P

MESH = pl.DeviceIdType.MESH
SIDE = 4
CORES = 2
LINE = SIDE * CORES
TURNS = ((0, 1, 2), (1, 2, 0), (2, 0, 1))
LIMITS = ((4, 4, 8), (5, 5, 8), (6, 6, 8))
HALVES = 2
BATCHES = 2


def coordinates(device):
    return ((device // CORES) % SIDE, (device // LINE) % SIDE, device // (LINE * SIDE)), device % CORES


def mesh_id(place, core):
    x, y, z = place
    return (z * SIDE + y, x * CORES + core)


def iota(shape, axis):
    return lax.broadcasted_iota(jnp.int32, shape, axis)


def as_row(column):
    count = column.shape[0]
    return jnp.sum(jnp.where(iota((count, count), 0) == iota((count, count), 1), column, 0), axis=0, keepdims=True)


def as_column(row):
    count = row.shape[1]
    return jnp.sum(jnp.where(iota((count, count), 0) == iota((count, count), 1), row, 0), axis=1, keepdims=True)


def rank_in(group):
    count = group.shape[0]
    same = (group == as_row(group)) & (iota((count, count), 1) < iota((count, count), 0))
    return jnp.sum(jnp.where(same, 1, 0), axis=1, keepdims=True)


def split_rows(blocks):
    count, tall, half = blocks.shape
    wide = blocks.astype(jnp.float32)
    left = wide[:, : tall // 2].reshape(count * tall // 2, half)
    right = wide[:, tall // 2 :].reshape(count * tall // 2, half)
    return jnp.concatenate([left, right], axis=1)


def join_rows(rows, tall):
    count, width = rows.shape[0] // (tall // 2), rows.shape[1]
    left = rows[:, : width // 2].reshape(count, tall // 2, width // 2)
    right = rows[:, width // 2 :].reshape(count, tall // 2, width // 2)
    return jnp.concatenate([left, right], axis=1)


def layer_kernel(
    limits,
    tokens_one, tokens_two, gates_one, gates_two, routes_one, routes_two, old_place, moves, w_in, w_out,
    mixed_one, mixed_two, flags, new_in, new_out,
    first, sent, spread, crossed, landed, outbox, mailbox, returned, held_in, held_out, feed, total, mixing,
    plan, table, local, send, recv, token_send, token_recv, loads, hello, held_tokens,
):
    gx, gy = lax.axis_index("gx"), lax.axis_index("gy")
    at, core = (gy // CORES, gx % SIDE, gx // SIDE), gy % CORES
    line_most, plane_most, own_most = limits
    devices = outbox.shape[0]
    tall = outbox.shape[1]
    capacity = tall // 2
    myself = gx * LINE + gy
    piece = first[0][0].shape[1]
    block = spread[0][0].shape[2]
    third = piece * LINE
    sources, targets = (w_in, w_out), (new_in, new_out)
    others = [(step, flip) for step in range(SIDE) for flip in range(CORES) if (step, flip) != (0, 0)]

    def beside(axis, step, flip=0):
        place = list(at)
        place[axis] = (place[axis] + step) % SIDE
        return place, (core + flip) % CORES

    def flat_id(device):
        return (device // LINE, device % LINE)

    barrier = pltpu.get_barrier_semaphore()
    peers = [beside(0, 0, 1)] + [
        beside(axis, step, flip) for axis in range(3) for step in range(1, SIDE) for flip in range(CORES)
    ]
    for place, which in peers:
        pl.semaphore_signal(barrier, inc=1, device_id=mesh_id(place, which), device_id_type=MESH)
    pl.semaphore_wait(barrier, len(peers))

    def meet_all():
        for axis in (1, 2):
            for step in range(1, SIDE):
                place, which = beside(axis, step)
                pl.semaphore_signal(hello.at[axis - 1], inc=1, device_id=mesh_id(place, which), device_id_type=MESH)
            pl.semaphore_wait(hello.at[axis - 1], SIDE - 1)

    def ship(src, dst, stage, half, turn, place, which):
        pltpu.make_async_remote_copy(
            src_ref=src,
            dst_ref=dst,
            send_sem=send.at[stage, half, turn],
            recv_sem=recv.at[stage, half, turn],
            device_id=mesh_id(place, which),
            device_id_type=MESH,
        ).start()

    def settle(semaphore, ref):
        pltpu.make_async_copy(ref, ref, semaphore).wait()

    def rows(turn, index):
        return pl.ds(pl.multiple_of(turn * third + index * piece, piece), piece)

    def spot(turn):
        return at[TURNS[turn][0]] * CORES + core

    def own_first(half, turn):
        me = spot(turn)
        return pltpu.make_async_copy(
            sources[half].at[rows(turn, me)], first[half][turn].at[me], local.at[0, half, turn]
        )

    def own_last(half, turn):
        me = spot(turn)
        return pltpu.make_async_copy(
            first[half][turn].at[me], targets[half].at[rows(turn, me)], local.at[1, half, turn]
        )

    def stage_one(half):
        for turn in range(3):
            me = spot(turn)
            for step, flip in others:
                place, which = beside(TURNS[turn][0], step, flip)
                index = place[TURNS[turn][0]] * CORES + which
                ship(
                    sources[half].at[rows(turn, index)], first[half][turn].at[me], 0, half, turn, place, which
                )
            own_first(half, turn).start()

    def stage_two(half):
        for turn in range(3):
            b = TURNS[turn][1]
            own_first(half, turn).wait()
            settle(recv.at[0, half, turn], first[half][turn].at[pl.ds(0, LINE - 1)])
            for step in (1, 2, 3, 0):
                place, which = beside(b, step)
                cut = pl.ds(pl.multiple_of(place[b] * block, block), block)

                def take(k, carry):
                    data = first[half][turn][table[4 * turn, k], cut, :]
                    if step == 0:
                        spread[half][turn][at[b], k] = data
                    else:
                        sent[half, turn, step - 1, k] = data
                    return carry

                lax.fori_loop(0, line_most, take, 0)
                if step:
                    ship(sent.at[half, turn, step - 1, pl.ds(0, line_most)], spread[half][turn].at[at[b]], 1, half, turn, place, which)

    def stage_three(half):
        for turn in range(3):
            c = TURNS[turn][2]
            settle(recv.at[1, half, turn], spread[half][turn].at[pl.ds(0, SIDE - 1)])
            settle(send.at[1, half, turn], sent.at[half, turn, :, pl.ds(0, line_most)])
            for step in (1, 2, 3, 0):
                place, which = beside(c, step)

                def take(k, carry):
                    index = table[4 * turn + 1, place[c] * own_most + k]
                    data = spread[half][turn][index // line_most, index % line_most]
                    if step == 0:
                        crossed[half][turn][at[c], k] = data
                    else:
                        sent[half, turn, step - 1, k] = data
                    return carry

                lax.fori_loop(0, plane_most if step else own_most, take, 0)
                if step:
                    ship(sent.at[half, turn, step - 1, pl.ds(0, plane_most)], crossed[half][turn].at[at[c], pl.ds(0, plane_most)], 2, half, turn, place, which)

    def stage_four(half):
        for turn in range(3):
            b = TURNS[turn][1]
            settle(recv.at[2, half, turn], crossed[half][turn].at[pl.ds(0, SIDE - 1), pl.ds(0, plane_most)])
            settle(send.at[2, half, turn], sent.at[half, turn, :, pl.ds(0, plane_most)])
            for step in (1, 2, 3, 0):
                place, which = beside(b, step)

                def take(k, carry):
                    index = table[4 * turn + 2, place[b] * line_most + k]
                    data = crossed[half][turn][index // own_most, index % own_most]
                    if step == 0:
                        landed[half][turn][at[b], k] = data
                    else:
                        sent[half, turn, step - 1, k] = data
                    return carry

                lax.fori_loop(0, line_most, take, 0)
                if step:
                    ship(sent.at[half, turn, step - 1, pl.ds(0, line_most)], landed[half][turn].at[at[b]], 3, half, turn, place, which)

    def stage_five(half):
        for turn in range(3):
            me = spot(turn)
            settle(recv.at[3, half, turn], landed[half][turn].at[pl.ds(0, SIDE - 1)])
            for step, flip in others + [(0, 0)]:
                place, which = beside(TURNS[turn][0], step, flip)
                index = place[TURNS[turn][0]] * CORES + which
                chosen = table[4 * turn + 3, index]

                def take(quarter, carry):
                    first[half][turn][index, pl.ds(pl.multiple_of(quarter * block, block), block), :] = landed[half][turn][
                        quarter, chosen
                    ]
                    return carry

                lax.fori_loop(0, SIDE, take, 0)
                if (step, flip) != (0, 0):
                    ship(
                        first[half][turn].at[index], targets[half].at[rows(turn, me)], 4, half, turn, place, which
                    )
            own_last(half, turn).start()

    def make_plan():
        source, target = as_column(moves[0:1, :]), as_column(moves[1:2, :])
        count = source.shape[0]
        s_at, s_core = coordinates(source)
        t_at, t_core = coordinates(target)
        wide = (count, plan.shape[1])
        entry = iota(wide, 1)
        plan[...] = jnp.zeros(plan.shape, jnp.int32)
        for turn, (a, b, c) in enumerate(TURNS):
            s_line, t_line = s_at[b] * SIDE + s_at[c], t_at[b] * SIDE + t_at[c]
            rank_s, rank_t, rank_p = rank_in(s_line), rank_in(t_line), rank_in(s_at[c] * SIDE + t_at[c])
            rank_s, rank_t = jnp.minimum(rank_s, line_most - 1), jnp.minimum(rank_t, line_most - 1)
            rank_p = jnp.minimum(rank_p, own_most - 1)
            here = at[b] * SIDE + at[c]
            for row, (mine, slot, value, largest) in enumerate(
                (
                    (s_line == here, rank_s, s_at[a] * CORES + s_core, LINE - 1),
                    (
                        s_at[c] == at[c],
                        t_at[c] * own_most + rank_p,
                        s_at[b] * line_most + rank_s,
                        SIDE * line_most - 1,
                    ),
                    (
                        t_at[c] == at[c],
                        t_at[b] * line_most + rank_t,
                        s_at[c] * own_most + rank_p,
                        SIDE * own_most - 1,
                    ),
                    (t_line == here, t_at[a] * CORES + t_core, rank_t, line_most - 1),
                )
            ):
                key = jnp.where(mine, slot, -1)
                found = jnp.sum(jnp.where(key == entry, value, 0), axis=0, keepdims=True)
                index = 4 * turn + row
                plan[index : index + 1, :] = jnp.minimum(found, largest)
        arriving = jnp.max(jnp.where(target == myself, 1, 0), axis=0, keepdims=True)
        flags[...] = jnp.broadcast_to(arriving, flags.shape)
        copy = pltpu.make_async_copy(plan, table, loads.at[2])
        copy.start()
        copy.wait()

    def positions():
        routes = as_column(routes_one[...])
        slot_one = jnp.sum(
            jnp.where(routes == iota((routes.shape[0], old_place.shape[1]), 1), old_place[...], 0),
            axis=1,
            keepdims=True,
        )
        goal = as_column(routes_two[...])
        source, target = moves[0:1, :], moves[1:2, :]
        slot_two = goal + jnp.sum(jnp.where(goal == target, source - goal, 0), axis=1, keepdims=True)
        place_one = slot_one * capacity + rank_in(slot_one)
        place_two = slot_two * capacity + capacity // BATCHES + rank_in(slot_two)
        return place_one, place_two

    def one_hot(mask):
        return jnp.where(mask, 1.0, 0.0).astype(jnp.bfloat16)

    def fill_outbox(place_one, place_two):
        row_one, row_two = as_row(place_one), as_row(place_two)
        group = 16
        count = group * capacity

        def fill(index, carry):
            rows_here = iota((count, row_one.shape[1]), 0) + index * count
            picked = jnp.dot(one_hot(rows_here == row_one), held_tokens[0], preferred_element_type=jnp.float32)
            picked += jnp.dot(one_hot(rows_here == row_two), held_tokens[1], preferred_element_type=jnp.float32)
            outbox[pl.ds(index * group, group)] = join_rows(picked, tall).astype(jnp.bfloat16)
            return carry

        lax.fori_loop(0, devices // group, fill, 0)

    def post(src, dst, way, peer):
        pltpu.make_async_remote_copy(
            src_ref=src,
            dst_ref=dst,
            send_sem=token_send.at[way],
            recv_sem=token_recv.at[way],
            device_id=flat_id(peer),
            device_id_type=MESH,
        ).start()

    def send_tokens():
        def go(step, carry):
            peer = (myself + step * 79) % devices
            post(outbox.at[peer], mailbox.at[my_slot], 0, peer)
            return carry

        lax.fori_loop(1, devices, go, 0)
        mailbox[my_slot] = outbox[myself]

    group = SIDE * LINE
    tile = 512
    my_sum = (at[0] + at[1] + at[2]) % SIDE
    my_slot = my_sum * group + myself % group

    def experts(index):
        quarter = (index + my_sum) % SIDE
        begin = quarter * group
        feed[...] = split_rows(mailbox[pl.ds(begin, group)]).astype(jnp.bfloat16)
        total[...] = jnp.zeros(total.shape, jnp.float32)

        def part(step, carry):
            cut = pl.ds(pl.multiple_of(step * tile, tile), tile)
            hidden = lax.dot_general(
                feed[...], held_in[cut, :], (((1,), (1,)), ((), ())), preferred_element_type=jnp.float32
            )
            hidden = jnp.maximum(hidden, 0.0).astype(jnp.bfloat16)
            total[...] += jnp.dot(hidden, held_out[cut, :], preferred_element_type=jnp.float32)
            return carry

        lax.fori_loop(0, held_in.shape[0] // tile, part, 0)
        mailbox[pl.ds(begin, group)] = join_rows(total[...], tall).astype(jnp.bfloat16)

        def back(step, carry):
            low = (myself + step * 13) % group
            z = (quarter + 2 * SIDE - (low // LINE) % SIDE - (low // CORES) % SIDE) % SIDE
            peer = z * group + low

            @pl.when(peer != myself)
            def _():
                post(mailbox.at[begin + low], returned.at[myself], 1, peer)

            return carry

        lax.fori_loop(0, group, back, 0)

    def collect(place_one, place_two):
        count = group * capacity
        mixing[...] = jnp.zeros(mixing.shape, jnp.float32)
        tokens_here = place_one.shape[0]

        def add(index, carry):
            results = split_rows(returned[pl.ds(index * group, group)]).astype(jnp.bfloat16)
            columns = iota((tokens_here, count), 1) + index * count
            for batch, place in enumerate((place_one, place_two)):
                mixing[batch] += jnp.dot(one_hot(columns == place), results, preferred_element_type=jnp.float32)
            return carry

        lax.fori_loop(0, devices // group, add, 0)
        mixed_one[...] = (as_column(gates_one[...]) * mixing[0]).astype(jnp.bfloat16)
        mixed_two[...] = (as_column(gates_two[...]) * mixing[1]).astype(jnp.bfloat16)

    load_tokens = [
        pltpu.make_async_copy(source, held_tokens.at[batch], loads.at[3 + batch])
        for batch, source in enumerate((tokens_one, tokens_two))
    ]
    load_in = pltpu.make_async_copy(w_in, held_in, loads.at[0])
    load_out = pltpu.make_async_copy(w_out, held_out, loads.at[1])

    stage_one(0)
    for load in load_tokens:
        load.start()
    meet_all()
    place_one, place_two = positions()
    for load in load_tokens:
        load.wait()
    fill_outbox(place_one, place_two)
    send_tokens()
    stage_one(1)
    load_in.start()
    load_out.start()
    make_plan()
    stage_two(0)
    stage_two(1)
    stage_three(0)
    load_in.wait()
    load_out.wait()
    settle(token_recv.at[0], mailbox.at[pl.ds(0, devices - 1)])
    experts(0)
    stage_three(1)
    experts(1)
    stage_four(0)
    experts(2)
    stage_four(1)
    experts(3)
    returned[myself] = mailbox[my_slot]
    stage_five(0)
    stage_five(1)
    settle(token_recv.at[1], returned.at[pl.ds(0, devices - 1)])
    collect(place_one, place_two)
    settle(token_send.at[0], outbox.at[pl.ds(0, devices - 1)])
    settle(token_send.at[1], mailbox.at[pl.ds(0, devices - 1)])

    for half in range(HALVES):
        for turn in range(3):
            settle(send.at[0, half, turn], first[half][turn].at[pl.ds(0, LINE - 1)])
            settle(send.at[3, half, turn], sent.at[half, turn, :, pl.ds(0, line_most)])
            settle(send.at[4, half, turn], first[half][turn].at[pl.ds(0, LINE - 1)])
            settle(recv.at[4, half, turn], targets[half].at[pl.ds(0, (LINE - 1) * piece)])
            own_last(half, turn).wait()


def layer(which, tokens_one, tokens_two, gates_one, gates_two, routes_one, routes_two, old_place, moves, w_in, w_out):
    line_most, plane_most, own_most = LIMITS[which]
    hidden_units, width = w_in.shape
    tokens_here = tokens_one.shape[0]
    devices = lax.axis_size("gx") * lax.axis_size("gy")
    tall = 2 * BATCHES * (2 * tokens_here // devices)
    piece = hidden_units // (3 * LINE)
    block = piece // SIDE
    dtype = w_in.dtype
    vmem = pl.BlockSpec(memory_space=pltpu.VMEM)
    hbm = pl.BlockSpec(memory_space=pl.ANY)
    most = max(line_most, plane_most)

    def each(*shape):
        return [[pltpu.VMEM(shape, dtype)] * 3] * HALVES

    return pl.pallas_call(
        functools.partial(layer_kernel, LIMITS[which]),
        out_shape=[jax.ShapeDtypeStruct((tokens_here, width), dtype)] * 2
        + [jax.ShapeDtypeStruct((1, 128), jnp.int32)]
        + [jax.ShapeDtypeStruct((hidden_units, width), dtype)] * 2,
        in_specs=[hbm] * 2 + [vmem] * 6 + [hbm] * 2,
        out_specs=[vmem] * 3 + [hbm] * 2,
        scratch_shapes=[
            each(LINE, piece, width),
            pltpu.VMEM((HALVES, 3, SIDE - 1, most, block, width), dtype),
            each(SIDE, line_most, block, width),
            each(SIDE, own_most, block, width),
            each(SIDE, line_most, block, width),
            pltpu.VMEM((devices, tall, width // 2), dtype),
            pltpu.VMEM((devices, tall, width // 2), dtype),
            pltpu.VMEM((devices, tall, width // 2), dtype),
            pltpu.VMEM((hidden_units, width), dtype),
            pltpu.VMEM((hidden_units, width), dtype),
            pltpu.VMEM((32 * tall // 2, width), dtype),
            pltpu.VMEM((32 * tall // 2, width), jnp.float32),
            pltpu.VMEM((BATCHES, tokens_here, width), jnp.float32),
            pltpu.VMEM((16, 128), jnp.int32),
            pltpu.SMEM((16, 128), jnp.int32),
            pltpu.SemaphoreType.DMA((2, HALVES, 3)),
            pltpu.SemaphoreType.DMA((5, HALVES, 3)),
            pltpu.SemaphoreType.DMA((5, HALVES, 3)),
            pltpu.SemaphoreType.DMA((2,)),
            pltpu.SemaphoreType.DMA((2,)),
            pltpu.SemaphoreType.DMA((5,)),
            pltpu.SemaphoreType.REGULAR((2,)),
            pltpu.VMEM((BATCHES, tokens_here, width), dtype),
        ],
        compiler_params=pltpu.CompilerParams(
            collective_id=1 + which, has_side_effects=True, vmem_limit_bytes=60 * 1024 * 1024
        ),
        cost_estimate=pl.CostEstimate(
            flops=8 * tokens_here * hidden_units * width, bytes_accessed=400_000_000, transcendentals=0
        ),
    )(
        tokens_one,
        tokens_two,
        gates_one.reshape(1, tokens_here),
        gates_two.reshape(1, tokens_here),
        routes_one.reshape(1, tokens_here),
        routes_two.reshape(1, tokens_here),
        old_place.reshape(1, -1),
        moves.T,
        w_in,
        w_out,
    )


def keep_kernel(flags, came_in, came_out, mixed_one, mixed_two, own_in, own_out, *rest):
    *outs, through, mixed, load_sems, store_sems = rest
    parts = load_sems.shape[1]
    count = through.shape[2]
    stores = []

    def load(source, half, part):
        cut = pl.ds(part * count, count)
        return pltpu.make_async_copy(source.at[cut], through.at[half, part], load_sems.at[half, part])

    def load_all(sources):
        for part in range(parts):
            for half, source in enumerate(sources):
                load(source, half, part).start()

    @pl.when(flags[0, 0] != 0)
    def _():
        load_all((came_in, came_out))

    @pl.when(flags[0, 0] == 0)
    def _():
        load_all((own_in.at[0], own_out.at[0]))

    mixes = [
        pltpu.make_async_copy(source, mixed.at[batch], load_sems.at[HALVES, batch])
        for batch, source in enumerate((mixed_one, mixed_two))
    ]
    for copy in mixes:
        copy.start()
    for part in range(parts):
        for half in range(HALVES):
            load(came_in, half, part).wait()
            cut = pl.ds(part * count, count)
            stores.append(
                pltpu.make_async_copy(through.at[half, part], outs[2 + half].at[0, cut], store_sems.at[half, part])
            )
            stores[-1].start()
    for batch, copy in enumerate(mixes):
        copy.wait()
        stores.append(pltpu.make_async_copy(mixed.at[batch], outs[batch], store_sems.at[HALVES, batch]))
        stores[-1].start()
    for copy in stores:
        copy.wait()


def keep(flags, came_in, came_out, mixed_one, mixed_two, own_in, own_out):
    hbm = pl.BlockSpec(memory_space=pl.ANY)
    parts = 6
    hidden_units, width = came_in.shape
    like = [jax.ShapeDtypeStruct(x.shape, x.dtype) for x in (mixed_one, mixed_two, own_in, own_out)]
    return pl.pallas_call(
        keep_kernel,
        out_shape=like,
        in_specs=[pl.BlockSpec(memory_space=pltpu.SMEM)] + [hbm] * 6,
        out_specs=[hbm] * 4,
        scratch_shapes=[
            pltpu.VMEM((HALVES, parts, hidden_units // parts, width), came_in.dtype),
            pltpu.VMEM((BATCHES, *mixed_one.shape), mixed_one.dtype),
            pltpu.SemaphoreType.DMA((HALVES + 1, parts)),
            pltpu.SemaphoreType.DMA((HALVES + 1, parts)),
        ],
        compiler_params=pltpu.CompilerParams(vmem_limit_bytes=56 * 1024 * 1024),
    )(flags, came_in, came_out, mixed_one, mixed_two, own_in, own_out)


def limits_needed(move_slots):
    (sx, sy, sz), _ = coordinates(move_slots[:, 0])
    (tx, ty, tz), _ = coordinates(move_slots[:, 1])

    def same(value):
        return value[:, None] == value[None, :]

    def counts(*masks):
        fields = sum(jnp.where(mask, 1 << (5 * i), 0) for i, mask in enumerate(masks))
        total = jnp.sum(fields, axis=1, dtype=jnp.int32)
        return [(total >> (5 * i)) & 31 for i in range(len(masks))]

    ex, ey, ez, fx, fy, fz = (same(value) for value in (sx, sy, sz, tx, ty, tz))
    lines = counts(ey & ez, ez & ex, ex & ey, fy & fz, fz & fx, fx & fy)
    planes = counts(ez & fz, ex & fx, ey & fy)
    level = 0
    for line_most, plane_most, own_most in LIMITS:
        over = functools.reduce(jnp.logical_or, [count > line_most for count in lines])
        for count, start, end in zip(planes, (sz, sx, sy), (tz, tx, ty)):
            over |= count > jnp.where(start == end, own_most, plane_most)
        level += over.astype(jnp.int32)
    return jnp.max(level)


def relocate_everywhere(expert_in, expert_out, move_slots, myself):
    hidden_units, width = expert_in.shape
    device_count = lax.axis_size("gx") * lax.axis_size("gy")
    sources, targets = move_slots[:, 0], move_slots[:, 1]
    devices = jnp.arange(device_count, dtype=jnp.int32)
    anchor = jnp.sum(jnp.where(targets[None, :] == devices[:, None], sources[None, :], 0), axis=1)
    shape = (device_count, hidden_units // device_count, width)
    results = []
    for weights in (expert_in, expert_out):
        held = lax.all_to_all(weights.reshape(shape), ("gx", "gy"), split_axis=0, concat_axis=0, tiled=True)
        forward = jnp.take(held, anchor, axis=0)
        back = lax.all_to_all(forward, ("gx", "gy"), split_axis=0, concat_axis=0, tiled=True)
        results.append(back.reshape(hidden_units, width))
    return results


def shards(
    tokens_one,
    gates_one,
    routes_one,
    old_place,
    move_slots,
    tokens_two,
    gates_two,
    routes_two,
    expert_in,
    expert_out,
):
    myself = lax.axis_index(("gx", "gy")).astype(jnp.int32)
    weights_in, weights_out = expert_in[0], expert_out[0]
    operands = (
        tokens_one,
        tokens_two,
        gates_one,
        gates_two,
        routes_one,
        routes_two,
        old_place,
        move_slots,
        weights_in,
        weights_out,
    )

    def beyond():
        mixed_one, mixed_two, flags, *_ = layer(0, *operands)
        return (mixed_one, mixed_two, flags, *relocate_everywhere(weights_in, weights_out, move_slots, myself))

    mixed_one, mixed_two, flags, came_in, came_out = lax.switch(
        limits_needed(move_slots),
        [lambda which=which: tuple(layer(which, *operands)) for which in range(len(LIMITS))] + [beyond],
    )
    return tuple(keep(flags, came_in, came_out, mixed_one, mixed_two, expert_in, expert_out))


def solution(mesh):
    return jax.shard_map(
        shards,
        mesh=mesh,
        in_specs=(
            P(("gx", "gy"), None),
            P(("gx", "gy")),
            P(("gx", "gy"), None),
            P(),
            P(),
            P(("gx", "gy"), None),
            P(("gx", "gy")),
            P(("gx", "gy"), None),
            P(("gx", "gy"), None, None),
            P(("gx", "gy"), None, None),
        ),
        out_specs=(
            P(("gx", "gy"), None),
            P(("gx", "gy"), None),
            P(("gx", "gy"), None, None),
            P(("gx", "gy"), None, None),
        ),
        check_vma=False,
    )
```

```python
import functools

import jax
import jax.numpy as jnp
from jax import lax
from jax.experimental import pallas as pl
from jax.experimental.pallas import tpu as pltpu
from jax.sharding import PartitionSpec as P

MESH = pl.DeviceIdType.MESH
SIDE = 4
CORES = 2
LINE = SIDE * CORES
TURNS = ((0, 1, 2), (1, 2, 0), (2, 0, 1))
LIMITS = ((4, 4, 8), (4, 5, 8), (5, 5, 8), (6, 6, 8))
HALVES = 2
BATCHES = 2


def coordinates(device):
    return ((device // CORES) % SIDE, (device // LINE) % SIDE, device // (LINE * SIDE)), device % CORES


def mesh_id(place, core):
    x, y, z = place
    return (z * SIDE + y, x * CORES + core)


def iota(shape, axis):
    return lax.broadcasted_iota(jnp.int32, shape, axis)


def as_row(column):
    count = column.shape[0]
    return jnp.sum(jnp.where(iota((count, count), 0) == iota((count, count), 1), column, 0), axis=0, keepdims=True)


def as_column(row):
    count = row.shape[1]
    return jnp.sum(jnp.where(iota((count, count), 0) == iota((count, count), 1), row, 0), axis=1, keepdims=True)


def rank_in(group):
    count = group.shape[0]
    same = (group == as_row(group)) & (iota((count, count), 1) < iota((count, count), 0))
    return jnp.sum(jnp.where(same, 1, 0), axis=1, keepdims=True)


def split_rows(blocks):
    count, tall, half = blocks.shape
    wide = blocks.astype(jnp.float32)
    left = wide[:, : tall // 2].reshape(count * tall // 2, half)
    right = wide[:, tall // 2 :].reshape(count * tall // 2, half)
    return jnp.concatenate([left, right], axis=1)


def join_rows(rows, tall):
    count, width = rows.shape[0] // (tall // 2), rows.shape[1]
    left = rows[:, : width // 2].reshape(count, tall // 2, width // 2)
    right = rows[:, width // 2 :].reshape(count, tall // 2, width // 2)
    return jnp.concatenate([left, right], axis=1)


def layer_kernel(
    limits,
    tokens_one, tokens_two, gates_one, gates_two, routes_one, routes_two, old_place, moves, w_in, w_out,
    mixed_one, mixed_two, flags, new_in, new_out,
    first, sent, spread, crossed, landed, outbox, mailbox, returned, held_in, held_out, feed, total, mixing,
    plan, table, local, send, recv, token_send, token_recv, loads, hello, held_tokens,
):
    gx, gy = lax.axis_index("gx"), lax.axis_index("gy")
    at, core = (gy // CORES, gx % SIDE, gx // SIDE), gy % CORES
    line_most, plane_most, own_most = limits
    devices = outbox.shape[0]
    tall = outbox.shape[1]
    capacity = tall // 2
    myself = gx * LINE + gy
    piece = first[0][0].shape[1]
    block = spread[0][0].shape[2]
    third = piece * LINE
    sources, targets = (w_in, w_out), (new_in, new_out)
    others = [(step, flip) for step in range(SIDE) for flip in range(CORES) if (step, flip) != (0, 0)]

    def beside(axis, step, flip=0):
        place = list(at)
        place[axis] = (place[axis] + step) % SIDE
        return place, (core + flip) % CORES

    def flat_id(device):
        return (device // LINE, device % LINE)

    barrier = pltpu.get_barrier_semaphore()
    peers = [beside(0, 0, 1)] + [
        beside(axis, step, flip) for axis in range(3) for step in range(1, SIDE) for flip in range(CORES)
    ]
    for place, which in peers:
        pl.semaphore_signal(barrier, inc=1, device_id=mesh_id(place, which), device_id_type=MESH)
    pl.semaphore_wait(barrier, len(peers))

    def meet_all():
        for axis in (1, 2):
            for step in range(1, SIDE):
                place, which = beside(axis, step)
                pl.semaphore_signal(hello.at[axis - 1], inc=1, device_id=mesh_id(place, which), device_id_type=MESH)
            pl.semaphore_wait(hello.at[axis - 1], SIDE - 1)

    def ship(src, dst, stage, half, turn, place, which):
        pltpu.make_async_remote_copy(
            src_ref=src,
            dst_ref=dst,
            send_sem=send.at[stage, half, turn],
            recv_sem=recv.at[stage, half, turn],
            device_id=mesh_id(place, which),
            device_id_type=MESH,
        ).start()

    def settle(semaphore, ref):
        pltpu.make_async_copy(ref, ref, semaphore).wait()

    def rows(turn, index):
        return pl.ds(pl.multiple_of(turn * third + index * piece, piece), piece)

    def spot(turn):
        return at[TURNS[turn][0]] * CORES + core

    def own_first(half, turn):
        me = spot(turn)
        return pltpu.make_async_copy(
            sources[half].at[rows(turn, me)], first[half][turn].at[me], local.at[0, half, turn]
        )

    def own_last(half, turn):
        me = spot(turn)
        return pltpu.make_async_copy(
            first[half][turn].at[me], targets[half].at[rows(turn, me)], local.at[1, half, turn]
        )

    def stage_one(half):
        for turn in range(3):
            me = spot(turn)
            for step, flip in others:
                place, which = beside(TURNS[turn][0], step, flip)
                index = place[TURNS[turn][0]] * CORES + which
                ship(
                    sources[half].at[rows(turn, index)], first[half][turn].at[me], 0, half, turn, place, which
                )
            own_first(half, turn).start()

    def stage_two(half):
        for turn in range(3):
            b = TURNS[turn][1]
            own_first(half, turn).wait()
            settle(recv.at[0, half, turn], first[half][turn].at[pl.ds(0, LINE - 1)])
            for step in (1, 2, 3, 0):
                place, which = beside(b, step)
                cut = pl.ds(pl.multiple_of(place[b] * block, block), block)

                def take(k, carry):
                    data = first[half][turn][table[4 * turn, k], cut, :]
                    if step == 0:
                        spread[half][turn][at[b], k] = data
                    else:
                        sent[half, turn, step - 1, k] = data
                    return carry

                lax.fori_loop(0, line_most, take, 0)
                if step:
                    ship(sent.at[half, turn, step - 1, pl.ds(0, line_most)], spread[half][turn].at[at[b]], 1, half, turn, place, which)

    def stage_three(half):
        for turn in range(3):
            c = TURNS[turn][2]
            settle(recv.at[1, half, turn], spread[half][turn].at[pl.ds(0, SIDE - 1)])
            settle(send.at[1, half, turn], sent.at[half, turn, :, pl.ds(0, line_most)])
            for step in (1, 2, 3, 0):
                place, which = beside(c, step)

                def take(k, carry):
                    index = table[4 * turn + 1, place[c] * own_most + k]
                    data = spread[half][turn][index // line_most, index % line_most]
                    if step == 0:
                        crossed[half][turn][at[c], k] = data
                    else:
                        sent[half, turn, step - 1, k] = data
                    return carry

                lax.fori_loop(0, plane_most if step else own_most, take, 0)
                if step:
                    ship(sent.at[half, turn, step - 1, pl.ds(0, plane_most)], crossed[half][turn].at[at[c], pl.ds(0, plane_most)], 2, half, turn, place, which)

    def stage_four(half):
        for turn in range(3):
            b = TURNS[turn][1]
            settle(recv.at[2, half, turn], crossed[half][turn].at[pl.ds(0, SIDE - 1), pl.ds(0, plane_most)])
            settle(send.at[2, half, turn], sent.at[half, turn, :, pl.ds(0, plane_most)])
            for step in (1, 2, 3, 0):
                place, which = beside(b, step)

                def take(k, carry):
                    index = table[4 * turn + 2, place[b] * line_most + k]
                    data = crossed[half][turn][index // own_most, index % own_most]
                    if step == 0:
                        landed[half][turn][at[b], k] = data
                    else:
                        sent[half, turn, step - 1, k] = data
                    return carry

                lax.fori_loop(0, line_most, take, 0)
                if step:
                    ship(sent.at[half, turn, step - 1, pl.ds(0, line_most)], landed[half][turn].at[at[b]], 3, half, turn, place, which)

    def stage_five(half):
        for turn in range(3):
            me = spot(turn)
            settle(recv.at[3, half, turn], landed[half][turn].at[pl.ds(0, SIDE - 1)])
            for step, flip in others + [(0, 0)]:
                place, which = beside(TURNS[turn][0], step, flip)
                index = place[TURNS[turn][0]] * CORES + which
                chosen = table[4 * turn + 3, index]

                def take(quarter, carry):
                    first[half][turn][index, pl.ds(pl.multiple_of(quarter * block, block), block), :] = landed[half][turn][
                        quarter, chosen
                    ]
                    return carry

                lax.fori_loop(0, SIDE, take, 0)
                if (step, flip) != (0, 0):
                    ship(
                        first[half][turn].at[index], targets[half].at[rows(turn, me)], 4, half, turn, place, which
                    )
            own_last(half, turn).start()

    def make_plan():
        source, target = as_column(moves[0:1, :]), as_column(moves[1:2, :])
        count = source.shape[0]
        s_at, s_core = coordinates(source)
        t_at, t_core = coordinates(target)
        wide = (count, plan.shape[1])
        entry = iota(wide, 1)
        plan[...] = jnp.zeros(plan.shape, jnp.int32)
        for turn, (a, b, c) in enumerate(TURNS):
            s_line, t_line = s_at[b] * SIDE + s_at[c], t_at[b] * SIDE + t_at[c]
            rank_s, rank_t, rank_p = rank_in(s_line), rank_in(t_line), rank_in(s_at[c] * SIDE + t_at[c])
            rank_s, rank_t = jnp.minimum(rank_s, line_most - 1), jnp.minimum(rank_t, line_most - 1)
            rank_p = jnp.minimum(rank_p, own_most - 1)
            here = at[b] * SIDE + at[c]
            for row, (mine, slot, value, largest) in enumerate(
                (
                    (s_line == here, rank_s, s_at[a] * CORES + s_core, LINE - 1),
                    (
                        s_at[c] == at[c],
                        t_at[c] * own_most + rank_p,
                        s_at[b] * line_most + rank_s,
                        SIDE * line_most - 1,
                    ),
                    (
                        t_at[c] == at[c],
                        t_at[b] * line_most + rank_t,
                        s_at[c] * own_most + rank_p,
                        SIDE * own_most - 1,
                    ),
                    (t_line == here, t_at[a] * CORES + t_core, rank_t, line_most - 1),
                )
            ):
                key = jnp.where(mine, slot, -1)
                found = jnp.sum(jnp.where(key == entry, value, 0), axis=0, keepdims=True)
                index = 4 * turn + row
                plan[index : index + 1, :] = jnp.minimum(found, largest)
        arriving = jnp.max(jnp.where(target == myself, 1, 0), axis=0, keepdims=True)
        flags[...] = jnp.broadcast_to(arriving, flags.shape)
        copy = pltpu.make_async_copy(plan, table, loads.at[2])
        copy.start()
        copy.wait()

    def positions():
        routes = as_column(routes_one[...])
        slot_one = jnp.sum(
            jnp.where(routes == iota((routes.shape[0], old_place.shape[1]), 1), old_place[...], 0),
            axis=1,
            keepdims=True,
        )
        goal = as_column(routes_two[...])
        source, target = moves[0:1, :], moves[1:2, :]
        slot_two = goal + jnp.sum(jnp.where(goal == target, source - goal, 0), axis=1, keepdims=True)
        place_one = slot_one * capacity + rank_in(slot_one)
        place_two = slot_two * capacity + capacity // BATCHES + rank_in(slot_two)
        return place_one, place_two

    def one_hot(mask):
        return jnp.where(mask, 1.0, 0.0).astype(jnp.bfloat16)

    def fill_outbox(place_one, place_two):
        row_one, row_two = as_row(place_one), as_row(place_two)
        group = 16
        count = group * capacity

        def fill(index, carry):
            rows_here = iota((count, row_one.shape[1]), 0) + index * count
            picked = jnp.dot(one_hot(rows_here == row_one), held_tokens[0], preferred_element_type=jnp.float32)
            picked += jnp.dot(one_hot(rows_here == row_two), held_tokens[1], preferred_element_type=jnp.float32)
            outbox[pl.ds(index * group, group)] = join_rows(picked, tall).astype(jnp.bfloat16)
            return carry

        lax.fori_loop(0, devices // group, fill, 0)

    def post(src, dst, way, peer):
        pltpu.make_async_remote_copy(
            src_ref=src,
            dst_ref=dst,
            send_sem=token_send.at[way],
            recv_sem=token_recv.at[way],
            device_id=flat_id(peer),
            device_id_type=MESH,
        ).start()

    def send_tokens():
        def go(step, carry):
            peer = (myself + step * 79) % devices
            post(outbox.at[peer], mailbox.at[my_slot], 0, peer)
            return carry

        lax.fori_loop(1, devices, go, 0)
        mailbox[my_slot] = outbox[myself]

    group = SIDE * LINE
    tile = 512
    my_sum = (at[0] + at[1] + at[2]) % SIDE
    my_slot = my_sum * group + myself % group

    def experts(index):
        quarter = (index + my_sum) % SIDE
        begin = quarter * group
        feed[...] = split_rows(mailbox[pl.ds(begin, group)]).astype(jnp.bfloat16)
        total[...] = jnp.zeros(total.shape, jnp.float32)

        def part(step, carry):
            cut = pl.ds(pl.multiple_of(step * tile, tile), tile)
            hidden = lax.dot_general(
                feed[...], held_in[cut, :], (((1,), (1,)), ((), ())), preferred_element_type=jnp.float32
            )
            hidden = jnp.maximum(hidden, 0.0).astype(jnp.bfloat16)
            total[...] += jnp.dot(hidden, held_out[cut, :], preferred_element_type=jnp.float32)
            return carry

        lax.fori_loop(0, held_in.shape[0] // tile, part, 0)
        mailbox[pl.ds(begin, group)] = join_rows(total[...], tall).astype(jnp.bfloat16)

        def back(step, carry):
            low = (myself + step * 13) % group
            z = (quarter + 2 * SIDE - (low // LINE) % SIDE - (low // CORES) % SIDE) % SIDE
            peer = z * group + low

            @pl.when(peer != myself)
            def _():
                post(mailbox.at[begin + low], returned.at[myself], 1, peer)

            return carry

        lax.fori_loop(0, group, back, 0)

    def collect(place_one, place_two):
        count = group * capacity
        mixing[...] = jnp.zeros(mixing.shape, jnp.float32)
        tokens_here = place_one.shape[0]

        def add(index, carry):
            results = split_rows(returned[pl.ds(index * group, group)]).astype(jnp.bfloat16)
            columns = iota((tokens_here, count), 1) + index * count
            for batch, place in enumerate((place_one, place_two)):
                mixing[batch] += jnp.dot(one_hot(columns == place), results, preferred_element_type=jnp.float32)
            return carry

        lax.fori_loop(0, devices // group, add, 0)
        mixed_one[...] = (as_column(gates_one[...]) * mixing[0]).astype(jnp.bfloat16)
        mixed_two[...] = (as_column(gates_two[...]) * mixing[1]).astype(jnp.bfloat16)

    load_tokens = [
        pltpu.make_async_copy(source, held_tokens.at[batch], loads.at[3 + batch])
        for batch, source in enumerate((tokens_one, tokens_two))
    ]
    load_in = pltpu.make_async_copy(w_in, held_in, loads.at[0])
    load_out = pltpu.make_async_copy(w_out, held_out, loads.at[1])

    stage_one(0)
    for load in load_tokens:
        load.start()
    meet_all()
    place_one, place_two = positions()
    for load in load_tokens:
        load.wait()
    fill_outbox(place_one, place_two)
    send_tokens()
    stage_one(1)
    load_in.start()
    load_out.start()
    make_plan()
    stage_two(0)
    stage_two(1)
    stage_three(0)
    load_in.wait()
    load_out.wait()
    settle(token_recv.at[0], mailbox.at[pl.ds(0, devices - 1)])
    experts(0)
    stage_three(1)
    experts(1)
    stage_four(0)
    experts(2)
    stage_four(1)
    experts(3)
    returned[myself] = mailbox[my_slot]
    stage_five(0)
    stage_five(1)
    settle(token_recv.at[1], returned.at[pl.ds(0, devices - 1)])
    collect(place_one, place_two)
    settle(token_send.at[0], outbox.at[pl.ds(0, devices - 1)])
    settle(token_send.at[1], mailbox.at[pl.ds(0, devices - 1)])

    for half in range(HALVES):
        for turn in range(3):
            settle(send.at[0, half, turn], first[half][turn].at[pl.ds(0, LINE - 1)])
            settle(send.at[3, half, turn], sent.at[half, turn, :, pl.ds(0, line_most)])
            settle(send.at[4, half, turn], first[half][turn].at[pl.ds(0, LINE - 1)])
            settle(recv.at[4, half, turn], targets[half].at[pl.ds(0, (LINE - 1) * piece)])
            own_last(half, turn).wait()


def layer(which, tokens_one, tokens_two, gates_one, gates_two, routes_one, routes_two, old_place, moves, w_in, w_out):
    line_most, plane_most, own_most = LIMITS[which]
    hidden_units, width = w_in.shape
    tokens_here = tokens_one.shape[0]
    devices = lax.axis_size("gx") * lax.axis_size("gy")
    tall = 2 * BATCHES * (2 * tokens_here // devices)
    piece = hidden_units // (3 * LINE)
    block = piece // SIDE
    dtype = w_in.dtype
    vmem = pl.BlockSpec(memory_space=pltpu.VMEM)
    hbm = pl.BlockSpec(memory_space=pl.ANY)
    most = max(line_most, plane_most)

    def each(*shape):
        return [[pltpu.VMEM(shape, dtype)] * 3] * HALVES

    return pl.pallas_call(
        functools.partial(layer_kernel, LIMITS[which]),
        out_shape=[jax.ShapeDtypeStruct((tokens_here, width), dtype)] * 2
        + [jax.ShapeDtypeStruct((1, 128), jnp.int32)]
        + [jax.ShapeDtypeStruct((hidden_units, width), dtype)] * 2,
        in_specs=[hbm] * 2 + [vmem] * 6 + [hbm] * 2,
        out_specs=[vmem] * 3 + [hbm] * 2,
        scratch_shapes=[
            each(LINE, piece, width),
            pltpu.VMEM((HALVES, 3, SIDE - 1, most, block, width), dtype),
            each(SIDE, line_most, block, width),
            each(SIDE, own_most, block, width),
            each(SIDE, line_most, block, width),
            pltpu.VMEM((devices, tall, width // 2), dtype),
            pltpu.VMEM((devices, tall, width // 2), dtype),
            pltpu.VMEM((devices, tall, width // 2), dtype),
            pltpu.VMEM((hidden_units, width), dtype),
            pltpu.VMEM((hidden_units, width), dtype),
            pltpu.VMEM((32 * tall // 2, width), dtype),
            pltpu.VMEM((32 * tall // 2, width), jnp.float32),
            pltpu.VMEM((BATCHES, tokens_here, width), jnp.float32),
            pltpu.VMEM((16, 128), jnp.int32),
            pltpu.SMEM((16, 128), jnp.int32),
            pltpu.SemaphoreType.DMA((2, HALVES, 3)),
            pltpu.SemaphoreType.DMA((5, HALVES, 3)),
            pltpu.SemaphoreType.DMA((5, HALVES, 3)),
            pltpu.SemaphoreType.DMA((2,)),
            pltpu.SemaphoreType.DMA((2,)),
            pltpu.SemaphoreType.DMA((5,)),
            pltpu.SemaphoreType.REGULAR((2,)),
            pltpu.VMEM((BATCHES, tokens_here, width), dtype),
        ],
        compiler_params=pltpu.CompilerParams(
            collective_id=1 + which, has_side_effects=True, vmem_limit_bytes=60 * 1024 * 1024
        ),
        cost_estimate=pl.CostEstimate(
            flops=8 * tokens_here * hidden_units * width, bytes_accessed=400_000_000, transcendentals=0
        ),
    )(
        tokens_one,
        tokens_two,
        gates_one.reshape(1, tokens_here),
        gates_two.reshape(1, tokens_here),
        routes_one.reshape(1, tokens_here),
        routes_two.reshape(1, tokens_here),
        old_place.reshape(1, -1),
        moves.T,
        w_in,
        w_out,
    )


def keep_kernel(flags, came_in, came_out, mixed_one, mixed_two, own_in, own_out, *rest):
    *outs, through, mixed, load_sems, store_sems = rest
    parts = load_sems.shape[1]
    count = through.shape[2]
    stores = []

    def load(source, half, part):
        cut = pl.ds(part * count, count)
        return pltpu.make_async_copy(source.at[cut], through.at[half, part], load_sems.at[half, part])

    def load_all(sources):
        for part in range(parts):
            for half, source in enumerate(sources):
                load(source, half, part).start()

    @pl.when(flags[0, 0] != 0)
    def _():
        load_all((came_in, came_out))

    @pl.when(flags[0, 0] == 0)
    def _():
        load_all((own_in.at[0], own_out.at[0]))

    mixes = [
        pltpu.make_async_copy(source, mixed.at[batch], load_sems.at[HALVES, batch])
        for batch, source in enumerate((mixed_one, mixed_two))
    ]
    for copy in mixes:
        copy.start()
    for part in range(parts):
        for half in range(HALVES):
            load(came_in, half, part).wait()
            cut = pl.ds(part * count, count)
            stores.append(
                pltpu.make_async_copy(through.at[half, part], outs[2 + half].at[0, cut], store_sems.at[half, part])
            )
            stores[-1].start()
    for batch, copy in enumerate(mixes):
        copy.wait()
        stores.append(pltpu.make_async_copy(mixed.at[batch], outs[batch], store_sems.at[HALVES, batch]))
        stores[-1].start()
    for copy in stores:
        copy.wait()


def keep(flags, came_in, came_out, mixed_one, mixed_two, own_in, own_out):
    hbm = pl.BlockSpec(memory_space=pl.ANY)
    parts = 3
    hidden_units, width = came_in.shape
    like = [jax.ShapeDtypeStruct(x.shape, x.dtype) for x in (mixed_one, mixed_two, own_in, own_out)]
    return pl.pallas_call(
        keep_kernel,
        out_shape=like,
        in_specs=[pl.BlockSpec(memory_space=pltpu.SMEM)] + [hbm] * 6,
        out_specs=[hbm] * 4,
        scratch_shapes=[
            pltpu.VMEM((HALVES, parts, hidden_units // parts, width), came_in.dtype),
            pltpu.VMEM((BATCHES, *mixed_one.shape), mixed_one.dtype),
            pltpu.SemaphoreType.DMA((HALVES + 1, parts)),
            pltpu.SemaphoreType.DMA((HALVES + 1, parts)),
        ],
        compiler_params=pltpu.CompilerParams(vmem_limit_bytes=56 * 1024 * 1024),
    )(flags, came_in, came_out, mixed_one, mixed_two, own_in, own_out)


def limits_needed(move_slots):
    source, target = move_slots[:, 0], move_slots[:, 1]
    x, y, z = (SIDE - 1) * CORES, (SIDE - 1) * LINE, (SIDE - 1) * LINE * SIDE
    between_s = source[:, None] ^ source[None, :]
    between_t = target[:, None] ^ target[None, :]

    def counts(*masks):
        fields = sum(jnp.where(mask, 1 << (5 * i), 0) for i, mask in enumerate(masks))
        total = jnp.sum(fields, axis=1, dtype=jnp.int32)
        return [(total >> (5 * i)) & 31 for i in range(len(masks))]

    ex, ey, ez = ((between_s & bits) == 0 for bits in (x, y, z))
    fx, fy, fz = ((between_t & bits) == 0 for bits in (x, y, z))
    lines = counts(ey & ez, ez & ex, ex & ey, fy & fz, fz & fx, fx & fy)
    planes = counts(ez & fz, ex & fx, ey & fy)
    level = 0
    for line_most, plane_most, own_most in LIMITS:
        over = functools.reduce(jnp.logical_or, [count > line_most for count in lines])
        for count, bits in zip(planes, (z, x, y)):
            over |= count > jnp.where(((source ^ target) & bits) == 0, own_most, plane_most)
        level += over.astype(jnp.int32)
    return jnp.max(level)


def relocate_everywhere(expert_in, expert_out, move_slots, myself):
    hidden_units, width = expert_in.shape
    device_count = lax.axis_size("gx") * lax.axis_size("gy")
    sources, targets = move_slots[:, 0], move_slots[:, 1]
    devices = jnp.arange(device_count, dtype=jnp.int32)
    anchor = jnp.sum(jnp.where(targets[None, :] == devices[:, None], sources[None, :], 0), axis=1)
    shape = (device_count, hidden_units // device_count, width)
    results = []
    for weights in (expert_in, expert_out):
        held = lax.all_to_all(weights.reshape(shape), ("gx", "gy"), split_axis=0, concat_axis=0, tiled=True)
        forward = jnp.take(held, anchor, axis=0)
        back = lax.all_to_all(forward, ("gx", "gy"), split_axis=0, concat_axis=0, tiled=True)
        results.append(back.reshape(hidden_units, width))
    return results


def shards(
    tokens_one,
    gates_one,
    routes_one,
    old_place,
    move_slots,
    tokens_two,
    gates_two,
    routes_two,
    expert_in,
    expert_out,
):
    myself = lax.axis_index(("gx", "gy")).astype(jnp.int32)
    weights_in, weights_out = expert_in[0], expert_out[0]
    operands = (
        tokens_one,
        tokens_two,
        gates_one,
        gates_two,
        routes_one,
        routes_two,
        old_place,
        move_slots,
        weights_in,
        weights_out,
    )

    def beyond():
        mixed_one, mixed_two, flags, *_ = layer(0, *operands)
        return (mixed_one, mixed_two, flags, *relocate_everywhere(weights_in, weights_out, move_slots, myself))

    mixed_one, mixed_two, flags, came_in, came_out = lax.switch(
        limits_needed(move_slots),
        [lambda which=which: tuple(layer(which, *operands)) for which in range(len(LIMITS))] + [beyond],
    )
    return tuple(keep(flags, came_in, came_out, mixed_one, mixed_two, expert_in, expert_out))


def solution(mesh):
    return jax.shard_map(
        shards,
        mesh=mesh,
        in_specs=(
            P(("gx", "gy"), None),
            P(("gx", "gy")),
            P(("gx", "gy"), None),
            P(),
            P(),
            P(("gx", "gy"), None),
            P(("gx", "gy")),
            P(("gx", "gy"), None),
            P(("gx", "gy"), None, None),
            P(("gx", "gy"), None, None),
        ),
        out_specs=(
            P(("gx", "gy"), None),
            P(("gx", "gy"), None),
            P(("gx", "gy"), None, None),
            P(("gx", "gy"), None, None),
        ),
        check_vma=False,
    )
```

```python
import functools

import jax
import jax.numpy as jnp
from jax import lax
from jax.experimental import pallas as pl
from jax.experimental.pallas import tpu as pltpu
from jax.sharding import PartitionSpec as P

MESH = pl.DeviceIdType.MESH
SIDE = 4
CORES = 2
LINE = SIDE * CORES
TURNS = ((0, 1, 2), (1, 2, 0), (2, 0, 1))
LIMITS = ((4, 4, 8), (5, 5, 8), (6, 6, 8))
HALVES = 2
BATCHES = 2


def coordinates(device):
    return ((device // CORES) % SIDE, (device // LINE) % SIDE, device // (LINE * SIDE)), device % CORES


def mesh_id(place, core):
    x, y, z = place
    return (z * SIDE + y, x * CORES + core)


def iota(shape, axis):
    return lax.broadcasted_iota(jnp.int32, shape, axis)


def as_row(column):
    count = column.shape[0]
    return jnp.sum(jnp.where(iota((count, count), 0) == iota((count, count), 1), column, 0), axis=0, keepdims=True)


def as_column(row):
    count = row.shape[1]
    return jnp.sum(jnp.where(iota((count, count), 0) == iota((count, count), 1), row, 0), axis=1, keepdims=True)


def rank_in(group):
    count = group.shape[0]
    same = (group == as_row(group)) & (iota((count, count), 1) < iota((count, count), 0))
    return jnp.sum(jnp.where(same, 1, 0), axis=1, keepdims=True)


def split_rows(blocks):
    count, tall, half = blocks.shape
    wide = blocks.astype(jnp.float32)
    left = wide[:, : tall // 2].reshape(count * tall // 2, half)
    right = wide[:, tall // 2 :].reshape(count * tall // 2, half)
    return jnp.concatenate([left, right], axis=1)


def join_rows(rows, tall):
    count, width = rows.shape[0] // (tall // 2), rows.shape[1]
    left = rows[:, : width // 2].reshape(count, tall // 2, width // 2)
    right = rows[:, width // 2 :].reshape(count, tall // 2, width // 2)
    return jnp.concatenate([left, right], axis=1)


def layer_kernel(
    limits,
    tokens_one, tokens_two, gates_one, gates_two, routes_one, routes_two, old_place, moves, w_in, w_out,
    mixed_one, mixed_two, flags, new_in, new_out,
    first, sent, spread, crossed, landed, outbox, mailbox, returned, held_in, held_out, feed, total, mixing,
    plan, table, local, send, recv, token_send, token_recv, loads, hello, held_tokens,
):
    gx, gy = lax.axis_index("gx"), lax.axis_index("gy")
    at, core = (gy // CORES, gx % SIDE, gx // SIDE), gy % CORES
    line_most, plane_most, own_most = limits
    devices = outbox.shape[0]
    tall = outbox.shape[1]
    capacity = tall // 2
    myself = gx * LINE + gy
    piece = first[0][0].shape[1]
    block = spread[0][0].shape[2]
    third = piece * LINE
    sources, targets = (w_in, w_out), (new_in, new_out)
    others = [(step, flip) for step in (2, 1, 3, 0) for flip in range(CORES) if (step, flip) != (0, 0)]

    def beside(axis, step, flip=0):
        place = list(at)
        place[axis] = (place[axis] + step) % SIDE
        return place, (core + flip) % CORES

    def flat_id(device):
        return (device // LINE, device % LINE)

    barrier = pltpu.get_barrier_semaphore()
    peers = [beside(0, 0, 1)] + [
        beside(axis, step, flip) for axis in range(3) for step in range(1, SIDE) for flip in range(CORES)
    ]
    for place, which in peers:
        pl.semaphore_signal(barrier, inc=1, device_id=mesh_id(place, which), device_id_type=MESH)
    pl.semaphore_wait(barrier, len(peers))

    def meet_all():
        for axis in (1, 2):
            for step in range(1, SIDE):
                place, which = beside(axis, step)
                pl.semaphore_signal(hello.at[axis - 1], inc=1, device_id=mesh_id(place, which), device_id_type=MESH)
            pl.semaphore_wait(hello.at[axis - 1], SIDE - 1)

    def ship(src, dst, stage, half, turn, place, which):
        pltpu.make_async_remote_copy(
            src_ref=src,
            dst_ref=dst,
            send_sem=send.at[stage, half, turn],
            recv_sem=recv.at[stage, half, turn],
            device_id=mesh_id(place, which),
            device_id_type=MESH,
        ).start()

    def settle(semaphore, ref):
        pltpu.make_async_copy(ref, ref, semaphore).wait()

    def rows(turn, index):
        return pl.ds(pl.multiple_of(turn * third + index * piece, piece), piece)

    def spot(turn):
        return at[TURNS[turn][0]] * CORES + core

    def own_first(half, turn):
        me = spot(turn)
        return pltpu.make_async_copy(
            sources[half].at[rows(turn, me)], first[half][turn].at[me], local.at[0, half, turn]
        )

    def own_last(half, turn):
        me = spot(turn)
        return pltpu.make_async_copy(
            first[half][turn].at[me], targets[half].at[rows(turn, me)], local.at[1, half, turn]
        )

    def stage_one(half):
        for turn in range(3):
            me = spot(turn)
            for step, flip in others:
                place, which = beside(TURNS[turn][0], step, flip)
                index = place[TURNS[turn][0]] * CORES + which
                ship(
                    sources[half].at[rows(turn, index)], first[half][turn].at[me], 0, half, turn, place, which
                )
            own_first(half, turn).start()

    def stage_two(half):
        for turn in range(3):
            b = TURNS[turn][1]
            own_first(half, turn).wait()
            settle(recv.at[0, half, turn], first[half][turn].at[pl.ds(0, LINE - 1)])
            for step in (2, 1, 3, 0):
                place, which = beside(b, step)
                cut = pl.ds(pl.multiple_of(place[b] * block, block), block)

                def take(k, carry):
                    data = first[half][turn][table[4 * turn, k], cut, :]
                    if step == 0:
                        spread[half][turn][at[b], k] = data
                    else:
                        sent[half, turn, step - 1, k] = data
                    return carry

                lax.fori_loop(0, line_most, take, 0)
                if step:
                    ship(sent.at[half, turn, step - 1, pl.ds(0, line_most)], spread[half][turn].at[at[b]], 1, half, turn, place, which)

    def stage_three(half):
        for turn in range(3):
            c = TURNS[turn][2]
            settle(recv.at[1, half, turn], spread[half][turn].at[pl.ds(0, SIDE - 1)])
            settle(send.at[1, half, turn], sent.at[half, turn, :, pl.ds(0, line_most)])
            for step in (2, 1, 3, 0):
                place, which = beside(c, step)

                def take(k, carry):
                    index = table[4 * turn + 1, place[c] * own_most + k]
                    data = spread[half][turn][index // line_most, index % line_most]
                    if step == 0:
                        crossed[half][turn][at[c], k] = data
                    else:
                        sent[half, turn, step - 1, k] = data
                    return carry

                lax.fori_loop(0, plane_most if step else own_most, take, 0)
                if step:
                    ship(sent.at[half, turn, step - 1, pl.ds(0, plane_most)], crossed[half][turn].at[at[c], pl.ds(0, plane_most)], 2, half, turn, place, which)

    def stage_four(half):
        for turn in range(3):
            b = TURNS[turn][1]
            settle(recv.at[2, half, turn], crossed[half][turn].at[pl.ds(0, SIDE - 1), pl.ds(0, plane_most)])
            settle(send.at[2, half, turn], sent.at[half, turn, :, pl.ds(0, plane_most)])
            for step in (2, 1, 3, 0):
                place, which = beside(b, step)

                def take(k, carry):
                    index = table[4 * turn + 2, place[b] * line_most + k]
                    data = crossed[half][turn][index // own_most, index % own_most]
                    if step == 0:
                        landed[half][turn][at[b], k] = data
                    else:
                        sent[half, turn, step - 1, k] = data
                    return carry

                lax.fori_loop(0, line_most, take, 0)
                if step:
                    ship(sent.at[half, turn, step - 1, pl.ds(0, line_most)], landed[half][turn].at[at[b]], 3, half, turn, place, which)

    def stage_five(half):
        for turn in range(3):
            me = spot(turn)
            settle(recv.at[3, half, turn], landed[half][turn].at[pl.ds(0, SIDE - 1)])
            for step, flip in others + [(0, 0)]:
                place, which = beside(TURNS[turn][0], step, flip)
                index = place[TURNS[turn][0]] * CORES + which
                chosen = table[4 * turn + 3, index]

                def take(quarter, carry):
                    first[half][turn][index, pl.ds(pl.multiple_of(quarter * block, block), block), :] = landed[half][turn][
                        quarter, chosen
                    ]
                    return carry

                lax.fori_loop(0, SIDE, take, 0)
                if (step, flip) != (0, 0):
                    ship(
                        first[half][turn].at[index], targets[half].at[rows(turn, me)], 4, half, turn, place, which
                    )
            own_last(half, turn).start()

    def make_plan():
        source, target = as_column(moves[0:1, :]), as_column(moves[1:2, :])
        count = source.shape[0]
        s_at, s_core = coordinates(source)
        t_at, t_core = coordinates(target)
        wide = (count, plan.shape[1])
        entry = iota(wide, 1)
        plan[...] = jnp.zeros(plan.shape, jnp.int32)
        for turn, (a, b, c) in enumerate(TURNS):
            s_line, t_line = s_at[b] * SIDE + s_at[c], t_at[b] * SIDE + t_at[c]
            rank_s, rank_t, rank_p = rank_in(s_line), rank_in(t_line), rank_in(s_at[c] * SIDE + t_at[c])
            rank_s, rank_t = jnp.minimum(rank_s, line_most - 1), jnp.minimum(rank_t, line_most - 1)
            rank_p = jnp.minimum(rank_p, own_most - 1)
            here = at[b] * SIDE + at[c]
            for row, (mine, slot, value, largest) in enumerate(
                (
                    (s_line == here, rank_s, s_at[a] * CORES + s_core, LINE - 1),
                    (
                        s_at[c] == at[c],
                        t_at[c] * own_most + rank_p,
                        s_at[b] * line_most + rank_s,
                        SIDE * line_most - 1,
                    ),
                    (
                        t_at[c] == at[c],
                        t_at[b] * line_most + rank_t,
                        s_at[c] * own_most + rank_p,
                        SIDE * own_most - 1,
                    ),
                    (t_line == here, t_at[a] * CORES + t_core, rank_t, line_most - 1),
                )
            ):
                key = jnp.where(mine, slot, -1)
                found = jnp.sum(jnp.where(key == entry, value, 0), axis=0, keepdims=True)
                index = 4 * turn + row
                plan[index : index + 1, :] = jnp.minimum(found, largest)
        arriving = jnp.max(jnp.where(target == myself, 1, 0), axis=0, keepdims=True)
        flags[...] = jnp.broadcast_to(arriving, flags.shape)
        copy = pltpu.make_async_copy(plan, table, loads.at[2])
        copy.start()
        copy.wait()

    def positions():
        routes = as_column(routes_one[...])
        slot_one = jnp.sum(
            jnp.where(routes == iota((routes.shape[0], old_place.shape[1]), 1), old_place[...], 0),
            axis=1,
            keepdims=True,
        )
        goal = as_column(routes_two[...])
        source, target = moves[0:1, :], moves[1:2, :]
        slot_two = goal + jnp.sum(jnp.where(goal == target, source - goal, 0), axis=1, keepdims=True)
        place_one = slot_one * capacity + rank_in(slot_one)
        place_two = slot_two * capacity + capacity // BATCHES + rank_in(slot_two)
        return place_one, place_two

    def one_hot(mask):
        return jnp.where(mask, 1.0, 0.0).astype(jnp.bfloat16)

    def fill_outbox(place_one, place_two):
        row_one, row_two = as_row(place_one), as_row(place_two)
        group = 16
        count = group * capacity

        def fill(index, carry):
            rows_here = iota((count, row_one.shape[1]), 0) + index * count
            picked = jnp.dot(one_hot(rows_here == row_one), held_tokens[0], preferred_element_type=jnp.float32)
            picked += jnp.dot(one_hot(rows_here == row_two), held_tokens[1], preferred_element_type=jnp.float32)
            outbox[pl.ds(index * group, group)] = join_rows(picked, tall).astype(jnp.bfloat16)
            return carry

        lax.fori_loop(0, devices // group, fill, 0)

    def post(src, dst, way, peer):
        pltpu.make_async_remote_copy(
            src_ref=src,
            dst_ref=dst,
            send_sem=token_send.at[way],
            recv_sem=token_recv.at[way],
            device_id=flat_id(peer),
            device_id_type=MESH,
        ).start()

    def send_tokens():
        def go(step, carry):
            peer = (myself + step * 79) % devices
            post(outbox.at[peer], mailbox.at[my_slot], 0, peer)
            return carry

        lax.fori_loop(1, devices, go, 0)
        mailbox[my_slot] = outbox[myself]

    group = SIDE * LINE
    tile = 512
    my_sum = (at[0] + at[1] + at[2]) % SIDE
    my_slot = my_sum * group + myself % group

    def experts(index):
        quarter = (index + my_sum) % SIDE
        begin = quarter * group
        feed[...] = split_rows(mailbox[pl.ds(begin, group)]).astype(jnp.bfloat16)
        total[...] = jnp.zeros(total.shape, jnp.float32)

        def part(step, carry):
            cut = pl.ds(pl.multiple_of(step * tile, tile), tile)
            hidden = lax.dot_general(
                feed[...], held_in[cut, :], (((1,), (1,)), ((), ())), preferred_element_type=jnp.float32
            )
            hidden = jnp.maximum(hidden, 0.0).astype(jnp.bfloat16)
            total[...] += jnp.dot(hidden, held_out[cut, :], preferred_element_type=jnp.float32)
            return carry

        lax.fori_loop(0, held_in.shape[0] // tile, part, 0)
        mailbox[pl.ds(begin, group)] = join_rows(total[...], tall).astype(jnp.bfloat16)

        def back(step, carry):
            low = (myself + step * 13) % group
            z = (quarter + 2 * SIDE - (low // LINE) % SIDE - (low // CORES) % SIDE) % SIDE
            peer = z * group + low

            @pl.when(peer != myself)
            def _():
                post(mailbox.at[begin + low], returned.at[myself], 1, peer)

            return carry

        lax.fori_loop(0, group, back, 0)

    def collect(place_one, place_two):
        count = group * capacity
        mixing[...] = jnp.zeros(mixing.shape, jnp.float32)
        tokens_here = place_one.shape[0]

        def add(index, carry):
            results = split_rows(returned[pl.ds(index * group, group)]).astype(jnp.bfloat16)
            columns = iota((tokens_here, count), 1) + index * count
            for batch, place in enumerate((place_one, place_two)):
                mixing[batch] += jnp.dot(one_hot(columns == place), results, preferred_element_type=jnp.float32)
            return carry

        lax.fori_loop(0, devices // group, add, 0)
        mixed_one[...] = (as_column(gates_one[...]) * mixing[0]).astype(jnp.bfloat16)
        mixed_two[...] = (as_column(gates_two[...]) * mixing[1]).astype(jnp.bfloat16)

    load_tokens = [
        pltpu.make_async_copy(source, held_tokens.at[batch], loads.at[3 + batch])
        for batch, source in enumerate((tokens_one, tokens_two))
    ]
    load_in = pltpu.make_async_copy(w_in, held_in, loads.at[0])
    load_out = pltpu.make_async_copy(w_out, held_out, loads.at[1])

    stage_one(0)
    for load in load_tokens:
        load.start()
    meet_all()
    place_one, place_two = positions()
    for load in load_tokens:
        load.wait()
    fill_outbox(place_one, place_two)
    send_tokens()
    stage_one(1)
    load_in.start()
    load_out.start()
    make_plan()
    stage_two(0)
    stage_two(1)
    stage_three(0)
    load_in.wait()
    load_out.wait()
    settle(token_recv.at[0], mailbox.at[pl.ds(0, devices - 1)])
    experts(0)
    stage_three(1)
    experts(1)
    stage_four(0)
    experts(2)
    stage_four(1)
    experts(3)
    returned[myself] = mailbox[my_slot]
    stage_five(0)
    stage_five(1)
    settle(token_recv.at[1], returned.at[pl.ds(0, devices - 1)])
    collect(place_one, place_two)
    settle(token_send.at[0], outbox.at[pl.ds(0, devices - 1)])
    settle(token_send.at[1], mailbox.at[pl.ds(0, devices - 1)])

    for half in range(HALVES):
        for turn in range(3):
            settle(send.at[0, half, turn], first[half][turn].at[pl.ds(0, LINE - 1)])
            settle(send.at[3, half, turn], sent.at[half, turn, :, pl.ds(0, line_most)])
            settle(send.at[4, half, turn], first[half][turn].at[pl.ds(0, LINE - 1)])
            settle(recv.at[4, half, turn], targets[half].at[pl.ds(0, (LINE - 1) * piece)])
            own_last(half, turn).wait()


def layer(which, tokens_one, tokens_two, gates_one, gates_two, routes_one, routes_two, old_place, moves, w_in, w_out):
    line_most, plane_most, own_most = LIMITS[which]
    hidden_units, width = w_in.shape
    tokens_here = tokens_one.shape[0]
    devices = lax.axis_size("gx") * lax.axis_size("gy")
    tall = 2 * BATCHES * (2 * tokens_here // devices)
    piece = hidden_units // (3 * LINE)
    block = piece // SIDE
    dtype = w_in.dtype
    vmem = pl.BlockSpec(memory_space=pltpu.VMEM)
    hbm = pl.BlockSpec(memory_space=pl.ANY)
    most = max(line_most, plane_most)

    def each(*shape):
        return [[pltpu.VMEM(shape, dtype)] * 3] * HALVES

    return pl.pallas_call(
        functools.partial(layer_kernel, LIMITS[which]),
        out_shape=[jax.ShapeDtypeStruct((tokens_here, width), dtype)] * 2
        + [jax.ShapeDtypeStruct((1, 128), jnp.int32)]
        + [jax.ShapeDtypeStruct((hidden_units, width), dtype)] * 2,
        in_specs=[hbm] * 2 + [vmem] * 6 + [hbm] * 2,
        out_specs=[vmem] * 3 + [hbm] * 2,
        scratch_shapes=[
            each(LINE, piece, width),
            pltpu.VMEM((HALVES, 3, SIDE - 1, most, block, width), dtype),
            each(SIDE, line_most, block, width),
            each(SIDE, own_most, block, width),
            each(SIDE, line_most, block, width),
            pltpu.VMEM((devices, tall, width // 2), dtype),
            pltpu.VMEM((devices, tall, width // 2), dtype),
            pltpu.VMEM((devices, tall, width // 2), dtype),
            pltpu.VMEM((hidden_units, width), dtype),
            pltpu.VMEM((hidden_units, width), dtype),
            pltpu.VMEM((32 * tall // 2, width), dtype),
            pltpu.VMEM((32 * tall // 2, width), jnp.float32),
            pltpu.VMEM((BATCHES, tokens_here, width), jnp.float32),
            pltpu.VMEM((16, 128), jnp.int32),
            pltpu.SMEM((16, 128), jnp.int32),
            pltpu.SemaphoreType.DMA((2, HALVES, 3)),
            pltpu.SemaphoreType.DMA((5, HALVES, 3)),
            pltpu.SemaphoreType.DMA((5, HALVES, 3)),
            pltpu.SemaphoreType.DMA((2,)),
            pltpu.SemaphoreType.DMA((2,)),
            pltpu.SemaphoreType.DMA((5,)),
            pltpu.SemaphoreType.REGULAR((2,)),
            pltpu.VMEM((BATCHES, tokens_here, width), dtype),
        ],
        compiler_params=pltpu.CompilerParams(
            collective_id=1 + which, has_side_effects=True, vmem_limit_bytes=60 * 1024 * 1024
        ),
        cost_estimate=pl.CostEstimate(
            flops=8 * tokens_here * hidden_units * width, bytes_accessed=400_000_000, transcendentals=0
        ),
    )(
        tokens_one,
        tokens_two,
        gates_one.reshape(1, tokens_here),
        gates_two.reshape(1, tokens_here),
        routes_one.reshape(1, tokens_here),
        routes_two.reshape(1, tokens_here),
        old_place.reshape(1, -1),
        moves.T,
        w_in,
        w_out,
    )


def keep_kernel(flags, came_in, came_out, mixed_one, mixed_two, own_in, own_out, *rest):
    *outs, through, mixed, load_sems, store_sems = rest
    parts = load_sems.shape[1]
    count = through.shape[2]
    stores = []

    def load(source, half, part):
        cut = pl.ds(part * count, count)
        return pltpu.make_async_copy(source.at[cut], through.at[half, part], load_sems.at[half, part])

    def load_all(sources):
        for part in range(parts):
            for half, source in enumerate(sources):
                load(source, half, part).start()

    @pl.when(flags[0, 0] != 0)
    def _():
        load_all((came_in, came_out))

    @pl.when(flags[0, 0] == 0)
    def _():
        load_all((own_in.at[0], own_out.at[0]))

    mixes = [
        pltpu.make_async_copy(source, mixed.at[batch], load_sems.at[HALVES, batch])
        for batch, source in enumerate((mixed_one, mixed_two))
    ]
    for copy in mixes:
        copy.start()
    for part in range(parts):
        for half in range(HALVES):
            load(came_in, half, part).wait()
            cut = pl.ds(part * count, count)
            stores.append(
                pltpu.make_async_copy(through.at[half, part], outs[2 + half].at[0, cut], store_sems.at[half, part])
            )
            stores[-1].start()
    for batch, copy in enumerate(mixes):
        copy.wait()
        stores.append(pltpu.make_async_copy(mixed.at[batch], outs[batch], store_sems.at[HALVES, batch]))
        stores[-1].start()
    for copy in stores:
        copy.wait()


def keep(flags, came_in, came_out, mixed_one, mixed_two, own_in, own_out):
    hbm = pl.BlockSpec(memory_space=pl.ANY)
    parts = 3
    hidden_units, width = came_in.shape
    like = [jax.ShapeDtypeStruct(x.shape, x.dtype) for x in (mixed_one, mixed_two, own_in, own_out)]
    return pl.pallas_call(
        keep_kernel,
        out_shape=like,
        in_specs=[pl.BlockSpec(memory_space=pltpu.SMEM)] + [hbm] * 6,
        out_specs=[hbm] * 4,
        scratch_shapes=[
            pltpu.VMEM((HALVES, parts, hidden_units // parts, width), came_in.dtype),
            pltpu.VMEM((BATCHES, *mixed_one.shape), mixed_one.dtype),
            pltpu.SemaphoreType.DMA((HALVES + 1, parts)),
            pltpu.SemaphoreType.DMA((HALVES + 1, parts)),
        ],
        compiler_params=pltpu.CompilerParams(vmem_limit_bytes=56 * 1024 * 1024),
    )(flags, came_in, came_out, mixed_one, mixed_two, own_in, own_out)


def limits_needed(move_slots):
    source, target = move_slots[:, 0], move_slots[:, 1]
    x, y, z = (SIDE - 1) * CORES, (SIDE - 1) * LINE, (SIDE - 1) * LINE * SIDE
    between_s = source[:, None] ^ source[None, :]
    between_t = target[:, None] ^ target[None, :]

    def counts(*masks):
        fields = sum(jnp.where(mask, 1 << (5 * i), 0) for i, mask in enumerate(masks))
        total = jnp.sum(fields, axis=1, dtype=jnp.int32)
        return [(total >> (5 * i)) & 31 for i in range(len(masks))]

    ex, ey, ez = ((between_s & bits) == 0 for bits in (x, y, z))
    fx, fy, fz = ((between_t & bits) == 0 for bits in (x, y, z))
    lines = counts(ey & ez, ez & ex, ex & ey, fy & fz, fz & fx, fx & fy)
    planes = counts(ez & fz, ex & fx, ey & fy)
    level = 0
    for line_most, plane_most, own_most in LIMITS:
        over = functools.reduce(jnp.logical_or, [count > line_most for count in lines])
        for count, bits in zip(planes, (z, x, y)):
            over |= count > jnp.where(((source ^ target) & bits) == 0, own_most, plane_most)
        level += over.astype(jnp.int32)
    return jnp.max(level)


def relocate_everywhere(expert_in, expert_out, move_slots, myself):
    hidden_units, width = expert_in.shape
    device_count = lax.axis_size("gx") * lax.axis_size("gy")
    sources, targets = move_slots[:, 0], move_slots[:, 1]
    devices = jnp.arange(device_count, dtype=jnp.int32)
    anchor = jnp.sum(jnp.where(targets[None, :] == devices[:, None], sources[None, :], 0), axis=1)
    shape = (device_count, hidden_units // device_count, width)
    results = []
    for weights in (expert_in, expert_out):
        held = lax.all_to_all(weights.reshape(shape), ("gx", "gy"), split_axis=0, concat_axis=0, tiled=True)
        forward = jnp.take(held, anchor, axis=0)
        back = lax.all_to_all(forward, ("gx", "gy"), split_axis=0, concat_axis=0, tiled=True)
        results.append(back.reshape(hidden_units, width))
    return results


def shards(
    tokens_one,
    gates_one,
    routes_one,
    old_place,
    move_slots,
    tokens_two,
    gates_two,
    routes_two,
    expert_in,
    expert_out,
):
    myself = lax.axis_index(("gx", "gy")).astype(jnp.int32)
    weights_in, weights_out = expert_in[0], expert_out[0]
    operands = (
        tokens_one,
        tokens_two,
        gates_one,
        gates_two,
        routes_one,
        routes_two,
        old_place,
        move_slots,
        weights_in,
        weights_out,
    )

    def beyond():
        mixed_one, mixed_two, flags, *_ = layer(0, *operands)
        return (mixed_one, mixed_two, flags, *relocate_everywhere(weights_in, weights_out, move_slots, myself))

    mixed_one, mixed_two, flags, came_in, came_out = lax.switch(
        limits_needed(move_slots),
        [lambda which=which: tuple(layer(which, *operands)) for which in range(len(LIMITS))] + [beyond],
    )
    return tuple(keep(flags, came_in, came_out, mixed_one, mixed_two, expert_in, expert_out))


def solution(mesh):
    return jax.shard_map(
        shards,
        mesh=mesh,
        in_specs=(
            P(("gx", "gy"), None),
            P(("gx", "gy")),
            P(("gx", "gy"), None),
            P(),
            P(),
            P(("gx", "gy"), None),
            P(("gx", "gy")),
            P(("gx", "gy"), None),
            P(("gx", "gy"), None, None),
            P(("gx", "gy"), None, None),
        ),
        out_specs=(
            P(("gx", "gy"), None),
            P(("gx", "gy"), None),
            P(("gx", "gy"), None, None),
            P(("gx", "gy"), None, None),
        ),
        check_vma=False,
    )
```
